32 devices in a mesh: ctx: 8 (over z, y), wt: 4 (over x, core).
Axes of the slice: x: 2, y: 2, z: 4, core: 2. Of those that a mesh axis runs over, the one named last changes fastest.
Arguments:
- block_in: bfloat16 [4096, 1024], P('ctx'), may hold values from -6 to 6
- doc_ids: int32 [4096], replicated, may hold values from 0 to 3, as said below
- block_of: int32 [16], replicated, may hold values from 0 to 15, as said below
- w_query: bfloat16 [1024, 1024], P(None, 'wt'), may hold values from -0.1875 to 0.1875
- w_key: bfloat16 [1024, 512], P(None, 'wt'), may hold values from -0.1875 to 0.1875
- w_value: bfloat16 [1024, 512], P(None, 'wt'), may hold values from -0.1875 to 0.1875
- w_out: bfloat16 [1024, 1024], P('wt'), may hold values from -1.5 to 1.5
- w_gate: bfloat16 [1024, 4608], P(None, 'wt'), may hold values from -0.1875 to 0.1875
- w_up: bfloat16 [1024, 4608], P(None, 'wt'), may hold values from -0.1875 to 0.1875
- w_down: bfloat16 [4608, 1024], P('wt'), may hold values from -0.09375 to 0.09375
- attn_gain: float32 [1024], replicated, may hold values from 0.5 to 1.5
- ffn_gain: float32 [1024], replicated, may hold values from 0.5 to 1.5
- query_gain: float32 [64], replicated, may hold values from 1 to 2
- key_gain: float32 [64], replicated, may hold values from 0.1 to 1.9
- cotangent: bfloat16 [4096, 1024], P('ctx'), may hold values from -8 to 8
Outputs:
- block_out: bfloat16 [4096, 1024], P('ctx')
- input_grad: float32 [4096, 1024], P('ctx')
- grad_query: float32 [1024, 1024], P('ctx', 'wt')
- grad_key: float32 [1024, 512], P('ctx', 'wt')
- grad_value: float32 [1024, 512], P('ctx', 'wt')
- grad_out_proj: float32 [1024, 1024], P('wt', 'ctx')
- grad_gate: float32 [1024, 4608], P('ctx', 'wt')
- grad_up: float32 [1024, 4608], P('ctx', 'wt')
- grad_down: float32 [4608, 1024], P('wt', 'ctx')
- grad_attn_gain: float32 [1024], P('ctx')
- grad_ffn_gain: float32 [1024], P('ctx')
- grad_query_gain: float32 [64], P('ctx')
- grad_key_gain: float32 [64], P('ctx')
The draws below stay inside these ranges and needn't reach their ends.
Inputs may be any that keep to these rules, and one draw needn't show every extreme that they name: doc_ids never falls along the text order, is 0 at the first token and 3 at the last, and document 0 holds at least the first 2048 tokens. block_of is a permutation of 0 to 15 whose entries 2c and 2c + 1 sum to 15 for every c.
All inputs are finite; a program needn't handle non-finite values.
Results may differ from the reference program's by a relative error of at most 0.029.
Values may be sent and summed in bfloat16 or wider, within the bound.
No kernel may reach another device: no remote copies, remote signals or barrier semaphores. Data moves between devices by JAX's collectives and lax.ppermute only.
A program may use at most 128 MiB of HBM per device.

```python
import math
import jax
import jax.numpy as jnp
from jax import lax

D = 1024
H = 16
HD = 64
KVH = 8
FF = 4608
BLK = 256
NBLK = 16
TOKENS = 4096


def draw_doc_ids(key, part):
    key = jax.random.fold_in(key, 11)
    key_one, key_two, key_three = jax.random.split(key, 3)
    first_cut = TOKENS // 2 + jax.random.randint(key_one, (), 0, TOKENS // 4 + 1)
    cut_two = jax.random.randint(key_two, (), first_cut + 1, TOKENS)
    cut_three = jax.random.randint(key_three, (), first_cut + 1, TOKENS)
    places = jnp.arange(TOKENS, dtype=jnp.int32)
    return (places >= first_cut).astype(jnp.int32) + (places >= jnp.minimum(cut_two, cut_three)).astype(jnp.int32) + (places >= jnp.maximum(cut_two, cut_three)).astype(jnp.int32)


def draw_block_of(key, part):
    key = jax.random.fold_in(key, 23)
    key_order, key_flip = jax.random.split(key, 2)
    pair_count = NBLK // 2
    order = jax.random.permutation(key_order, pair_count).astype(jnp.int32)
    flips = jax.random.randint(key_flip, (pair_count,), 0, 2)
    leading = jnp.where(flips == 0, order, NBLK - 1 - order)
    trailing = NBLK - 1 - leading
    return jnp.stack([leading, trailing], axis=1).reshape(NBLK).astype(jnp.int32)


def spiked(array, stream_key, source, target, blocks, factor):
    def block_of(dim):
        return (jnp.arange(array.shape[dim]) // (array.shape[dim] // blocks)).reshape((-1,) + (1,) * (array.ndim - 1 - dim))

    one_side = jax.random.permutation(stream_key, blocks)[block_of(target)]
    far = (block_of(target) + blocks // 2) % blocks
    return jnp.where((block_of(source) == one_side) | (block_of(source) == far), factor * array, array)


def steps_of(own_key, shape, shards, smallest, top_value):
    level = 1.0
    for axis_at, parts in shards:
        draws = jax.random.uniform(jax.random.fold_in(jax.random.fold_in(own_key, 6), axis_at), (parts,), jnp.float32, smallest / len(shards), top_value / len(shards))
        level = level * jnp.repeat(jnp.exp(draws), shape[axis_at] // parts).reshape((-1,) + (1,) * (len(shape) - 1 - axis_at))
    return level


def centred(own_key, extent, width, bound, shards=(), kind=jnp.bfloat16):
    loudness = steps_of(own_key, extent, shards, -0.22, 0.18) if shards else 1.0
    entries = jax.random.normal(own_key, extent, jnp.float32) * width * loudness
    return jnp.minimum(jnp.maximum(entries, -bound), bound).astype(kind)


def bell_draw_with(key, dims, deviation, most, cuts, heavy, kind=jnp.bfloat16):
    values = deviation * jax.random.normal(key, dims, jnp.float32)
    if cuts:
        values = values * steps_of(key, dims, cuts, -0.22, 0.18)
    return jnp.clip(spiked(values, jax.random.fold_in(key, 3), *heavy), -most, most).astype(kind)


def setup_inputs(seed: int = 0) -> dict:
    key_of = jax.random.split(jax.random.key(seed), 16)
    block_in = bell_draw_with(key_of[0], (TOKENS, D), 1.0, 6.0, ((0, 8),), (0, 1, 8, 2.0))
    doc_ids = draw_doc_ids(jax.random.fold_in(key_of[15], 71), 0)
    block_of = draw_block_of(jax.random.fold_in(key_of[15], 71), 0)
    w_query = centred(key_of[3], (D, H * HD), D ** -0.5, 0.1875, ((1, 4),))
    w_key = centred(key_of[4], (D, KVH * HD), D ** -0.5, 0.1875, ((1, 4),))
    w_value = centred(key_of[5], (D, KVH * HD), D ** -0.5, 0.1875, ((1, 4),))
    w_out = centred(key_of[6], (H * HD, D), (HD // 4) ** -0.5, 1.5, ((0, 4),))
    w_gate = centred(key_of[7], (D, FF), D ** -0.5, 0.1875, ((1, 4),))
    w_up = centred(key_of[8], (D, FF), D ** -0.5, 0.1875, ((1, 4),))
    w_down = centred(key_of[9], (FF, D), FF ** -0.5, 0.09375, ((0, 4),))
    attn_gain = jnp.clip(1.0 + 0.1 * jax.random.normal(key_of[10], (D,), jnp.float32), 0.5, 1.5)
    ffn_gain = jnp.clip(1.0 + 0.1 * jax.random.normal(key_of[11], (D,), jnp.float32), 0.5, 1.5)
    query_gain = jnp.clip(jnp.exp(jax.random.uniform(key_of[12], (HD,), jnp.float32, math.log(1.0), math.log(2.0))), 1.0, 2.0)
    key_gain = jnp.clip(1.0 + 0.18 * jax.random.normal(key_of[13], (HD,), jnp.float32), 0.1, 1.9)
    cotangent = bell_draw_with(key_of[14], (TOKENS, D), 1.0, 8.0, ((0, 8),), (0, 1, 8, 2.0))
    return dict(block_in=block_in, doc_ids=doc_ids, block_of=block_of, w_query=w_query, w_key=w_key, w_value=w_value, w_out=w_out, w_gate=w_gate, w_up=w_up, w_down=w_down, attn_gain=attn_gain, ffn_gain=ffn_gain, query_gain=query_gain, key_gain=key_gain, cotangent=cotangent)


@jax.custom_vjp
def low(v):
    return lax.optimization_barrier(v.astype(jnp.bfloat16)).astype(jnp.float32)

@jax.custom_vjp
def low_back(v):
    return v

def low_keep(v):
    return (low(v), None)

def low_pass(kept, grad):
    return (grad,)

def back_keep(v):
    return (v, None)

def back_low(kept, grad):
    return (low(grad),)
low.defvjp(low_keep, low_pass)
low_back.defvjp(back_keep, back_low)
EPS = 1e-05
THETA = 1000000.0
NEG = -1e+30
SCALE = 0.125
EXACT = lax.Precision.HIGHEST

def rms_norm(vector, gain):
    return vector * lax.rsqrt(lax.optimization_barrier(jnp.mean(vector * vector, axis=-1, keepdims=True)) + EPS) * gain

def rotate(vector, cos_table, sin_table):
    half_width = vector.shape[-1] // 2
    lead_part = vector[..., :half_width]
    tail_part = vector[..., half_width:]
    return jnp.concatenate([lead_part * cos_table - tail_part * sin_table, tail_part * cos_table + lead_part * sin_table], axis=-1)

def product(left, right):
    return jnp.dot(left, right, precision=EXACT, preferred_element_type=jnp.float32)

def reference(block_in, doc_ids, block_of, w_query, w_key, w_value, w_out, w_gate, w_up, w_down, attn_gain, ffn_gain, query_gain, key_gain, cotangent):
    where_rows = (block_of[:, None] * BLK + jnp.arange(BLK, dtype=jnp.int32)[None, :]).reshape(TOKENS).astype(jnp.int32)
    inputs = jnp.zeros((TOKENS, D), jnp.float32).at[where_rows].set(block_in.astype(jnp.float32))
    upstream = jnp.zeros((TOKENS, D), jnp.float32).at[where_rows].set(cotangent.astype(jnp.float32))
    positions = jnp.arange(TOKENS, dtype=jnp.int32)
    freqs = THETA ** (-2.0 * jnp.arange(HD // 2, dtype=jnp.float32) / HD)
    angle = positions.astype(jnp.float32)[:, None] * freqs[None, :]
    cos_table = jnp.cos(angle)[:, None, :]
    sin_table = jnp.sin(angle)[:, None, :]
    query_block = math.gcd(TOKENS, 512)
    count_blocks = TOKENS // query_block
    groups = H // KVH

    def attention(queries, keys, values):
        grouped = queries.reshape(count_blocks, query_block, KVH, groups, HD)

        def one_block(pieces):
            query_part, pos_part, doc_part = pieces
            scores = jnp.einsum('bkgd,tkd->kgbt', query_part, keys, precision=EXACT) * SCALE
            scores = low_back(scores)
            allowed = (doc_part[:, None] == doc_ids[None, :]) & (positions[None, :] <= pos_part[:, None])
            scores = jnp.where(allowed[None, None], scores, NEG)
            row_top = lax.optimization_barrier(jnp.max(scores, axis=-1, keepdims=True))
            weights = jnp.exp(scores - row_top)
            probabilities = low(weights / lax.optimization_barrier(jnp.sum(weights, axis=-1, keepdims=True)))
            mixed = jnp.einsum('kgbt,tkd->bkgd', probabilities, values, precision=EXACT)
            return mixed.reshape(query_block, H * HD)
        block_outs = lax.map(jax.checkpoint(one_block), (grouped, positions.reshape(count_blocks, query_block), doc_ids.reshape(count_blocks, query_block)))
        return block_outs.reshape(TOKENS, H * HD)

    def forward(x_rows, wq_full, wk_full, wv_full, wo_full, wg_full, wu_full, wd_full, gain_one, gain_two, gain_query, gain_key):
        normed_one = low(rms_norm(x_rows, gain_one))
        query_raw = low_back(product(normed_one, wq_full)).reshape(TOKENS, H, HD)
        key_raw = low_back(product(normed_one, wk_full)).reshape(TOKENS, KVH, HD)
        value_low = low(low_back(product(normed_one, wv_full))).reshape(TOKENS, KVH, HD)
        query_low = low(rotate(rms_norm(query_raw, gain_query), cos_table, sin_table))
        key_low = low(rotate(rms_norm(key_raw, gain_key), cos_table, sin_table))
        attended = attention(query_low, key_low, value_low)
        attn_sum = low_back(product(low(low_back(attended)), wo_full))
        middle = x_rows + attn_sum
        normed_two = low(rms_norm(middle, gain_two))
        gate_proj = low_back(product(normed_two, wg_full))
        up_proj = low_back(product(normed_two, wu_full))
        hidden = low(jax.nn.silu(gate_proj) * up_proj)
        ffn_sum = low_back(product(hidden, wd_full))
        return middle + ffn_sum
    floats = [w.astype(jnp.float32) for w in (w_query, w_key, w_value, w_out, w_gate, w_up, w_down)]
    result, pullback = jax.vjp(forward, inputs, *floats, attn_gain, ffn_gain, query_gain, key_gain)
    grads = pullback(upstream)
    return (result[where_rows].astype(jnp.bfloat16), grads[0][where_rows], grads[1], grads[2], grads[3], grads[4], grads[5], grads[6], grads[7], grads[8], grads[9], grads[10], grads[11])
```

```python
import functools

import jax
import jax.numpy as jnp
import numpy as np
from jax import lax
from jax.experimental import pallas as pl
from jax.experimental.pallas import tpu as pltpu
from jax.sharding import PartitionSpec as P

EPS = 1e-05
THETA = 1000000.0
NEG = -1e30
SCALE = 0.125
LANES = 128
DOCS = 4
VMEM_LIMIT = 60 * 1024 * 1024
F32 = jnp.float32
BF16 = jnp.bfloat16


def matmul(left, right):
    return jnp.dot(left, right, preferred_element_type=F32)


def contract(left, right, left_dim, right_dim):
    return lax.dot_general(
        left, right, (((left_dim,), (right_dim,)), ((), ())), preferred_element_type=F32
    )


def rms_norm(vector, gain):
    return vector * lax.rsqrt(jnp.mean(vector * vector, axis=-1, keepdims=True) + EPS) * gain


def norm_back(vector, gain, gradient):
    inverse = lax.rsqrt(jnp.mean(vector * vector, axis=-1, keepdims=True) + EPS)
    scaled = gradient * gain
    back = inverse * scaled - vector * inverse**3 * jnp.mean(
        scaled * vector, axis=-1, keepdims=True
    )
    return (back, gradient * vector * inverse)


def lane_index(shape):
    return lax.broadcasted_iota(jnp.int32, shape, len(shape) - 1)


def head_mean(values, head_dim):
    row_id = lax.broadcasted_iota(jnp.int32, (LANES, LANES), 0) // head_dim
    col_id = lax.broadcasted_iota(jnp.int32, (LANES, LANES), 1) // head_dim
    ones = (row_id == col_id).astype(BF16)
    high = values.astype(BF16)
    low = (values - high.astype(F32)).astype(BF16)
    return (matmul(high, ones) + matmul(low, ones)) * (1.0 / head_dim)


def swap_halves(values, head_dim):
    half = head_dim // 2
    lane = lane_index(values.shape)
    return jnp.where(
        lane % head_dim < half,
        pltpu.roll(values, LANES - half, 1),
        pltpu.roll(values, half, 1),
    )


def mix_heads(first, second, head_dim):
    lane = lane_index(first.shape)
    return (
        jnp.where(lane < head_dim, first, pltpu.roll(second, head_dim, 1)),
        jnp.where(lane < head_dim, pltpu.roll(first, head_dim, 1), second),
    )


def mix_low(first, second, head_dim):
    one, two = mix_heads(first.astype(F32), second.astype(F32), head_dim)
    return one.astype(BF16), two.astype(BF16)


def block_tables(base_cos, base_sin, step_cos, step_sin, head_dim):
    cos = base_cos * step_cos - base_sin * step_sin
    sin = base_sin * step_cos + base_cos * step_sin
    lane = lane_index(cos.shape)
    return cos, jnp.where(lane % head_dim < head_dim // 2, -sin, sin)


def head_norm_back(raw, gain, gradient, head_dim):
    inverse = lax.rsqrt(head_mean(raw * raw, head_dim) + EPS)
    scaled = gradient * gain
    back = inverse * scaled - raw * inverse**3 * head_mean(scaled * raw, head_dim)
    return back, jnp.sum(gradient * raw * inverse, axis=0, keepdims=True)


class Info:
    def __init__(self, ref, devices, half_rows):
        self.ref, self.devices, self.half_rows = ref, devices, half_rows
        self.ctx, self.core = ref[0], ref[1]

    def block(self, source, half):
        return self.ref[1 + DOCS + 2 * source + jnp.bitwise_xor(half, self.core)]

    def slot_source(self, slot):
        pairs = self.devices // 2
        same = slot < pairs
        column = jnp.where(same, self.ctx, jnp.bitwise_xor(self.ctx, 1))
        step = jnp.where(same, slot, slot - pairs)
        return lax.rem(column - 2 * step + self.devices, self.devices)

    def doc_start(self, position):
        start = jnp.zeros_like(position)
        for doc in range(1, DOCS):
            first = self.ref[1 + doc]
            start = jnp.where(position >= first, first, start)
        return start

    def relation(self, query_block, key_block):
        rows = self.half_rows
        low = self.doc_start(query_block * rows)
        high = self.doc_start(query_block * rows + rows - 1)
        visible = (key_block <= query_block) & (key_block * rows + rows - 1 >= low)
        whole = (key_block < query_block) & (key_block * rows >= high)
        return visible, whole

    def mask(self, query_block, key_block, query_dim):
        rows = self.half_rows
        query_pos = query_block * rows + lax.broadcasted_iota(jnp.int32, (rows, rows), query_dim)
        key_pos = key_block * rows + lax.broadcasted_iota(jnp.int32, (rows, rows), 1 - query_dim)
        return (key_pos <= query_pos) & (key_pos >= self.doc_start(query_pos))


def rope_rows(info, tables, half, head_dim):
    base_cos, base_sin, step_cos, step_sin = tables
    block = info.block(info.ctx, half)
    return block_tables(
        base_cos[pl.ds(block, 1), :],
        base_sin[pl.ds(block, 1), :],
        step_cos[...],
        step_sin[...],
        head_dim,
    )


def project_kernel(devices, head_dim, info_ref, x_ref, gain_ref, wq_ref, wk_ref, wv_ref, qg_ref,
                   kg_ref, bc_ref, bs_ref, sc_ref, ss_ref, kv_ref, q_ref, raw_ref, n1_ref, x_out):
    rows = x_ref.shape[0] // 2
    info = Info(info_ref, devices, rows)
    tables = (bc_ref, bs_ref, sc_ref, ss_ref)
    chunks = wq_ref.shape[1] // LANES
    for half in range(2):
        here = slice(half * rows, half * rows + rows)
        from_row = pl.multiple_of(jnp.bitwise_xor(half, info.core) * rows, rows)
        x_low = x_ref[pl.ds(from_row, rows), :]
        x_out[here, :] = x_low
        normed = rms_norm(x_low.astype(F32), gain_ref[...]).astype(BF16)
        n1_ref[here, :] = normed
        cos, sin = rope_rows(info, tables, half, head_dim)

        def turned(raw, gain):
            unit = raw * lax.rsqrt(head_mean(raw * raw, head_dim) + EPS) * gain
            return unit * cos + swap_halves(unit, head_dim) * sin

        key_raw = matmul(normed, wk_ref[...])
        kv_ref[here, 0:LANES] = turned(key_raw, kg_ref[...]).astype(BF16)
        kv_ref[here, LANES : 2 * LANES] = matmul(normed, wv_ref[...]).astype(BF16)
        raw_ref[here, chunks * LANES : (chunks + 1) * LANES] = key_raw
        query_raw = matmul(normed, wq_ref[...])
        raw_ref[here, 0 : chunks * LANES] = query_raw
        for chunk in range(chunks):
            cols = slice(chunk * LANES, (chunk + 1) * LANES)
            q_ref[here, cols] = (turned(query_raw[:, cols], qg_ref[...]) * SCALE).astype(BF16)


def spread_heads(low, rows, half, head_dim, out_ref):
    here = slice(half * rows, half * rows + rows)
    groups = mix_low(low[here, 0:LANES], low[here, LANES : 2 * LANES], head_dim)
    lane = lane_index((rows, LANES))
    for kv in range(2):
        for group in range(2):
            at = (2 * kv + group) * rows
            out_ref[half, at : at + rows, :] = jnp.where(
                lane // head_dim == kv, groups[group].astype(F32), 0.0
            ).astype(BF16)


def join_heads(stacked, rows, head_dim):
    lane = lane_index((rows, LANES))
    groups = [
        jnp.where(
            lane < head_dim,
            stacked[group * rows : (group + 1) * rows],
            stacked[(2 + group) * rows : (3 + group) * rows],
        )
        for group in range(2)
    ]
    return mix_heads(groups[0], groups[1], head_dim)


def fetch_slots(slot_refs, held, sems):
    copies = [
        pltpu.make_async_copy(ref, held.at[at], sems.at[at]) for at, ref in enumerate(slot_refs)
    ]
    for copy in copies:
        copy.start()
    return copies


def attend_kernel(devices, head_dim, info_ref, q_ref, *refs):
    slots = refs[:devices]
    o_ref, o32_ref, lse_ref, held, spread, total, sems = refs[devices:]
    rows = q_ref.shape[0] // 2
    info = Info(info_ref, devices, rows)
    copies = fetch_slots(slots, held, sems)
    q_low = q_ref[...]
    for half in range(2):
        spread_heads(q_low, rows, half, head_dim, spread)
    total[...] = jnp.zeros_like(total)
    for copy in copies:
        copy.wait()

    def one_key_block(step, carry):
        slot, key_half = step // 2, lax.rem(step, 2)
        key_block = info.block(info.slot_source(slot), key_half)
        key_rows = pl.ds(pl.multiple_of(key_half * rows, rows), rows)
        for half in range(2):
            query_block = info.block(info.ctx, half)
            visible, whole = info.relation(query_block, key_block)

            def take(masked, half=half, query_block=query_block):
                keys = held[slot, key_rows, 0:LANES]
                values = jnp.concatenate(
                    [held[slot, key_rows, LANES : 2 * LANES], jnp.ones((rows, LANES), BF16)], axis=1
                )
                if masked:
                    allowed = info.mask(query_block, key_block, 0)
                for part in range(4):
                    at = slice(part * rows, part * rows + rows)
                    scores = contract(spread[half, at, :], keys, 1, 1)
                    if masked:
                        scores = jnp.where(allowed, scores, NEG)
                    weights = jnp.exp(scores).astype(BF16)
                    total[half, at, :] += matmul(weights, values)

            pl.when(visible & whole)(functools.partial(take, False))
            pl.when(visible & jnp.logical_not(whole))(functools.partial(take, True))
        return carry

    lax.fori_loop(0, 2 * devices, one_key_block, 0)
    for half in range(2):
        here = slice(half * rows, half * rows + rows)
        sums = total[half, :, LANES : 2 * LANES]
        chunks = join_heads(total[half, :, 0:LANES] / sums, rows, head_dim)
        for chunk in range(2):
            cols = slice(chunk * LANES, (chunk + 1) * LANES)
            o32_ref[here, cols] = chunks[chunk]
            o_ref[here, cols] = chunks[chunk].astype(BF16)
        lse_ref[half] = jnp.transpose(jnp.log(sums))[0:8, :]


def attend_back_kernel(devices, head_dim, info_ref, q_ref, do_ref, o32_ref, lse_ref, raw_ref, qg_ref,
                       bc_ref, bs_ref, sc_ref, ss_ref, *refs):
    slots = refs[:devices]
    same_ref, other_ref, dq_ref, gain_ref, held, spread, spread_do, delta, dq_t, dkv, sems = refs[
        devices:
    ]
    rows = q_ref.shape[0] // 2
    pairs = devices // 2
    info = Info(info_ref, devices, rows)
    copies = fetch_slots(slots, held, sems)
    q_low, do_low = q_ref[...], do_ref[...]
    for half in range(2):
        here = slice(half * rows, half * rows + rows)
        spread_heads(q_low, rows, half, head_dim, spread)
        spread_heads(do_low, rows, half, head_dim, spread_do)
        product = do_low[here, :].astype(F32) * o32_ref[here, :]
        for chunk in range(2):
            turned = jnp.transpose(product[:, chunk * LANES : (chunk + 1) * LANES])
            for group in range(2):
                at = (2 * chunk + group) * rows
                delta[half, :, at : at + rows] = jnp.broadcast_to(
                    jnp.sum(
                        turned[group * head_dim : (group + 1) * head_dim], axis=0, keepdims=True
                    ),
                    (8, rows),
                )
    dq_t[...] = jnp.zeros_like(dq_t)
    for copy in copies:
        copy.wait()

    def one_key_block(step, carry):
        slot, key_half = step // 2, lax.rem(step, 2)
        key_block = info.block(info.slot_source(slot), key_half)
        key_rows = pl.ds(pl.multiple_of(key_half * rows, rows), rows)
        dkv[...] = jnp.zeros_like(dkv)
        for half in range(2):
            query_block = info.block(info.ctx, half)
            visible, whole = info.relation(query_block, key_block)

            def take(masked, half=half, query_block=query_block):
                keys = held[slot, key_rows, 0:LANES]
                values = held[slot, key_rows, LANES : 2 * LANES]
                if masked:
                    allowed = info.mask(query_block, key_block, 1)
                for part in range(4):
                    at = slice(part * rows, part * rows + rows)
                    queries, grads = spread[half, at, :], spread_do[half, at, :]
                    scores = contract(keys, queries, 1, 1) - lse_ref[half, 0:1, at]
                    if masked:
                        scores = jnp.where(allowed, scores, NEG)
                    probs = jnp.exp(scores)
                    grad_probs = contract(values, grads, 1, 1)
                    grad_scores = (probs * (grad_probs - delta[half, 0:1, at])).astype(BF16)
                    dkv[:, LANES : 2 * LANES] += matmul(probs.astype(BF16), grads)
                    dkv[:, 0:LANES] += matmul(grad_scores, queries)
                    dq_t[half, :, at] += contract(keys, grad_scores, 0, 0)

            pl.when(visible & whole)(functools.partial(take, False))
            pl.when(visible & jnp.logical_not(whole))(functools.partial(take, True))
        result = dkv[...].astype(BF16)

        @pl.when(slot < pairs)
        def _():
            same_ref[slot, key_rows, :] = result

        @pl.when(slot >= pairs)
        def _():
            other_ref[slot - pairs, key_rows, :] = result

        return carry

    lax.fori_loop(0, 2 * devices, one_key_block, 0)
    gain_sum = jnp.zeros((1, LANES), F32)
    for half in range(2):
        here = slice(half * rows, half * rows + rows)
        cos, sin = rope_rows(info, (bc_ref, bs_ref, sc_ref, ss_ref), half, head_dim)
        chunks = join_heads(jnp.transpose(dq_t[half]), rows, head_dim)
        for chunk in range(2):
            cols = slice(chunk * LANES, (chunk + 1) * LANES)
            grad = chunks[chunk] * SCALE
            grad = grad * cos - swap_halves(grad, head_dim) * sin
            back, term = head_norm_back(raw_ref[here, cols], qg_ref[...], grad, head_dim)
            dq_ref[here, cols] = back.astype(BF16)
            gain_sum += term
    gain_ref[...] = gain_sum


def key_back_kernel(devices, head_dim, count, info_ref, raw_ref, kg_ref, bc_ref, bs_ref, sc_ref,
                    ss_ref, *refs):
    parts = refs[:count]
    dk_ref, dv_ref, gain_ref = refs[count:]
    rows = raw_ref.shape[0] // 2
    info = Info(info_ref, devices, rows)
    gain_sum = jnp.zeros((1, LANES), F32)
    for half in range(2):
        here = slice(half * rows, half * rows + rows)
        grad = sum(part[here, :].astype(F32) for part in parts)
        dv_ref[here, :] = grad[:, LANES : 2 * LANES].astype(BF16)
        cos, sin = rope_rows(info, (bc_ref, bs_ref, sc_ref, ss_ref), half, head_dim)
        grad_k = grad[:, 0:LANES]
        grad_k = grad_k * cos - swap_halves(grad_k, head_dim) * sin
        back, term = head_norm_back(
            raw_ref[here, 2 * LANES : 3 * LANES], kg_ref[...], grad_k, head_dim
        )
        dk_ref[here, :] = back.astype(BF16)
        gain_sum += term
    gain_ref[...] = gain_sum


def call_kernel(body, outs, operands, memory, scratch=(), flops=10**9):
    kinds = {
        "s": pl.BlockSpec(memory_space=pltpu.SMEM),
        "v": pl.BlockSpec(memory_space=pltpu.VMEM),
        "a": pl.BlockSpec(memory_space=pl.ANY),
    }
    return pl.pallas_call(
        body,
        out_shape=[jax.ShapeDtypeStruct(shape, kind) for shape, kind in outs],
        in_specs=[kinds[m] for m in memory],
        out_specs=[kinds["v"]] * len(outs),
        scratch_shapes=list(scratch),
        compiler_params=pltpu.CompilerParams(vmem_limit_bytes=VMEM_LIMIT),
        cost_estimate=pl.CostEstimate(flops=flops, bytes_accessed=4 * 10**6, transcendentals=0),
    )(*operands)


def flip(values, axis, bit):
    size = lax.axis_size(axis)
    return lax.ppermute(values, axis, [(i, i ^ bit) for i in range(size)])


def shift(values, step):
    size = lax.axis_size("ctx")
    return lax.ppermute(values, "ctx", [(i, (i + step) % size) for i in range(size)])


def gather_slots(values):
    pairs = lax.axis_size("ctx") // 2
    same = [values] + [shift(values, 2 * k) for k in range(1, pairs)]
    return same + [flip(part, "ctx", 1) for part in same]


def wt_sum(mine, other):
    chip = (mine.astype(F32) + flip(other, "wt", 1).astype(F32)).astype(BF16)
    whole = (chip.astype(F32) + flip(chip, "wt", 2).astype(F32)).astype(BF16)
    return whole, flip(whole, "wt", 1)


def ctx_scatter(values):
    devices = lax.axis_size("ctx")
    pairs = devices // 2
    index = lax.axis_index("ctx")
    column, row = index % 2, index // 2
    split = values.reshape((pairs, 2) + values.shape[1:])
    sent = lax.dynamic_index_in_dim(split, 1 - column, 1, keepdims=False)
    kept = lax.dynamic_index_in_dim(split, column, 1, keepdims=False)
    both = (kept.astype(F32) + flip(sent, "ctx", 1).astype(F32)).astype(values.dtype)
    total = lax.dynamic_index_in_dim(both, row, 0, keepdims=False).astype(F32)
    for k in range(1, pairs):
        piece = lax.dynamic_index_in_dim(both, (row - k + pairs) % pairs, 0, keepdims=False)
        total = total + shift(piece, -2 * k).astype(F32)
    return total


def on_device(
    block_in,
    doc_ids,
    block_of,
    w_query,
    w_key,
    w_value,
    w_out,
    w_gate,
    w_up,
    w_down,
    attn_gain,
    ffn_gain,
    query_gain,
    key_gain,
    cotangent,
):
    tok_rows, width = block_in.shape
    half_rows = tok_rows // 2
    head_dim = query_gain.shape[0]
    q_width, kv_width = w_query.shape[1], w_key.shape[1]
    devices = lax.axis_size("ctx")
    pairs = devices // 2
    blocks = block_of.shape[0]
    wt_count = lax.axis_size("wt")
    core = lax.axis_index("wt") % 2

    starts = [jnp.sum((doc_ids < doc).astype(jnp.int32)) for doc in range(1, DOCS)]
    info = jnp.concatenate(
        [jnp.stack([lax.axis_index("ctx"), core] + starts).astype(jnp.int32), block_of]
    )
    half_dim = head_dim // 2
    freqs = THETA ** (-2.0 * (np.arange(LANES) % half_dim).astype(np.float64) / head_dim)
    base_angle = (np.arange(blocks) * half_rows)[:, None] * freqs[None, :]
    step_angle = np.arange(half_rows)[:, None] * freqs[None, :]
    tables = [
        jnp.asarray(table.astype(np.float32))
        for table in (np.cos(base_angle), np.sin(base_angle), np.cos(step_angle), np.sin(step_angle))
    ]
    query_gain_row = jnp.tile(query_gain, LANES // head_dim)[None, :]
    key_gain_row = jnp.tile(key_gain, LANES // head_dim)[None, :]

    def to_local(values):
        return jnp.where(core == 0, values, jnp.roll(values, half_rows, 0))

    def from_local(mine, other):
        return jnp.concatenate(
            [jnp.where(core == 0, mine, other), jnp.where(core == 0, other, mine)], axis=0
        )

    key_value, query, raw, normed_one, x_local = call_kernel(
        functools.partial(project_kernel, devices, head_dim),
        [
            ((tok_rows, 2 * kv_width), BF16),
            ((tok_rows, q_width), BF16),
            ((tok_rows, q_width + kv_width), F32),
            ((tok_rows, width), BF16),
            ((tok_rows, width), BF16),
        ],
        [info, block_in, attn_gain[None, :], w_query, w_key, w_value, query_gain_row, key_gain_row]
        + tables,
        "s" + "v" * 11,
    )
    slots = gather_slots(key_value)
    out_grad = to_local(cotangent)
    grad_hidden = contract(out_grad, w_down, 1, 1)
    scratch_kv = pltpu.VMEM((devices, tok_rows, 2 * kv_width), BF16)
    stacked = 4 * half_rows
    out_low, out_wide, log_total = call_kernel(
        functools.partial(attend_kernel, devices, head_dim),
        [
            ((tok_rows, q_width), BF16),
            ((tok_rows, q_width), F32),
            ((2, 8, stacked), F32),
        ],
        [info, query] + slots,
        "sv" + "a" * devices,
        [
            scratch_kv,
            pltpu.VMEM((2, stacked, LANES), BF16),
            pltpu.VMEM((2, stacked, 2 * LANES), F32),
            pltpu.SemaphoreType.DMA((devices,)),
        ],
        flops=8 * 10**9,
    )
    attn_other = matmul(out_low[half_rows:], w_out).astype(BF16)
    attn_mine = matmul(out_low[:half_rows], w_out).astype(BF16)
    attn_sum = jnp.concatenate(wt_sum(attn_mine, attn_other), axis=0)
    inputs = x_local.astype(F32)
    middle = inputs + attn_sum.astype(F32)
    normed_two = rms_norm(middle, ffn_gain).astype(BF16)
    gate_proj = matmul(normed_two, w_gate)
    up_proj = matmul(normed_two, w_up)
    sigmoid_gate = jax.nn.sigmoid(gate_proj)
    silu_gate = gate_proj * sigmoid_gate
    hidden = (silu_gate * up_proj).astype(BF16)
    grad_gate = (
        grad_hidden * up_proj * sigmoid_gate * (1.0 + gate_proj * (1.0 - sigmoid_gate))
    ).astype(BF16)
    grad_upper = (grad_hidden * silu_gate).astype(BF16)

    def normed_two_part(here):
        return (
            contract(grad_gate[here], w_gate, 1, 1) + contract(grad_upper[here], w_up, 1, 1)
        ).astype(BF16)

    mine, other = slice(0, half_rows), slice(half_rows, tok_rows)
    n2_other = normed_two_part(other)
    n2_mine = normed_two_part(mine)
    normed_two_grad = jnp.concatenate(wt_sum(n2_mine, n2_other), axis=0).astype(F32)

    def by_device(grad):
        return grad.astype(BF16).reshape((devices, grad.shape[0] // devices) + grad.shape[1:])

    grad_w_down = ctx_scatter(by_device(contract(out_grad, hidden, 0, 0)))
    grad_w_gate = ctx_scatter(by_device(contract(normed_two, grad_gate, 0, 0)))
    grad_w_up = ctx_scatter(by_device(contract(normed_two, grad_upper, 0, 0)))

    middle_back, ffn_gain_terms = norm_back(middle, ffn_gain, normed_two_grad)
    grad_middle = out_grad.astype(F32) + middle_back
    grad_middle_low = grad_middle.astype(BF16)
    grad_attended = contract(grad_middle_low, w_out, 1, 1).astype(BF16)
    grad_same, grad_other, query_raw_low, query_gain_sum = call_kernel(
        functools.partial(attend_back_kernel, devices, head_dim),
        [
            ((pairs, tok_rows, 2 * kv_width), BF16),
            ((pairs, tok_rows, 2 * kv_width), BF16),
            ((tok_rows, q_width), BF16),
            ((1, LANES), F32),
        ],
        [info, query, grad_attended, out_wide, log_total, raw, query_gain_row] + tables + slots,
        "s" + "v" * 10 + "a" * devices,
        [
            scratch_kv,
            pltpu.VMEM((2, stacked, LANES), BF16),
            pltpu.VMEM((2, stacked, LANES), BF16),
            pltpu.VMEM((2, 8, stacked), F32),
            pltpu.VMEM((2, LANES, stacked), F32),
            pltpu.VMEM((half_rows, 2 * LANES), F32),
            pltpu.SemaphoreType.DMA((devices,)),
        ],
        flops=16 * 10**9,
    )
    hidden_late, normed_two_late = lax.optimization_barrier((hidden, normed_two_grad))
    ffn_other = matmul(hidden_late[other], w_down).astype(BF16)
    ffn_mine = matmul(hidden_late[mine], w_down).astype(BF16)
    ffn_mine, ffn_other = wt_sum(ffn_mine, ffn_other)
    block_out = from_local(
        (middle[mine] + ffn_mine.astype(F32)).astype(BF16),
        (middle[other] + ffn_other.astype(F32)).astype(BF16),
    )

    both = (grad_same.astype(F32) + flip(grad_other, "ctx", 1).astype(F32)).astype(BF16)
    key_value_parts = [both[0]] + [shift(both[k], -2 * k) for k in range(1, pairs)]
    key_raw_low, value_raw_low, key_gain_sum = call_kernel(
        functools.partial(key_back_kernel, devices, head_dim, pairs),
        [
            ((tok_rows, kv_width), BF16),
            ((tok_rows, kv_width), BF16),
            ((1, LANES), F32),
        ],
        [info, raw, key_gain_row] + tables + key_value_parts,
        "s" + "v" * (6 + pairs),
    )
    normed_one_part = (
        contract(query_raw_low, w_query, 1, 1)
        + contract(key_raw_low, w_key, 1, 1)
        + contract(value_raw_low, w_value, 1, 1)
    )
    part_low = normed_one_part.astype(BF16)
    n1_mine, n1_other = wt_sum(part_low[mine], part_low[other])
    normed_one_grad = jnp.concatenate([n1_mine, n1_other], axis=0).astype(F32)

    inverse_one = lax.rsqrt(jnp.mean(inputs * inputs, axis=-1, keepdims=True) + EPS)
    attn_gain_part = jnp.sum(normed_one_part * inputs * inverse_one, axis=0)
    ffn_gain_part = jnp.sum(ffn_gain_terms, axis=0) * (1.0 / wt_count)

    def fold(row):
        return jnp.sum(row.reshape(LANES // head_dim, head_dim), axis=0)

    gains = jnp.concatenate(
        [
            part.reshape(devices, part.shape[0] // devices)
            for part in (attn_gain_part, ffn_gain_part, fold(query_gain_sum), fold(key_gain_sum))
        ],
        axis=1,
    )
    gains = gains + flip(gains, "wt", 1)
    gains = gains + flip(gains, "wt", 2)
    gains = ctx_scatter(gains)
    gain_width, head_width = width // devices, head_dim // devices

    grad_w_out = ctx_scatter(by_device(contract(grad_middle_low, out_low, 0, 0)))
    grad_w_qkv = ctx_scatter(
        by_device(
            contract(
                normed_one,
                jnp.concatenate([query_raw_low, key_raw_low, value_raw_low], axis=1),
                0,
                0,
            )
        )
    )
    input_back, _ = norm_back(inputs, attn_gain, normed_one_grad)
    grad_input = grad_middle + input_back
    return (
        block_out,
        from_local(grad_input[mine], grad_input[other]),
        grad_w_qkv[:, :q_width],
        grad_w_qkv[:, q_width : q_width + kv_width],
        grad_w_qkv[:, q_width + kv_width :],
        grad_w_out.T,
        grad_w_gate,
        grad_w_up,
        grad_w_down.T,
        gains[:gain_width],
        gains[gain_width : 2 * gain_width],
        gains[2 * gain_width : 2 * gain_width + head_width],
        gains[2 * gain_width + head_width :],
    )


def solution(mesh):
    in_specs = (
        P("ctx", None),
        P(),
        P(),
        P(None, "wt"),
        P(None, "wt"),
        P(None, "wt"),
        P("wt", None),
        P(None, "wt"),
        P(None, "wt"),
        P("wt", None),
        P(),
        P(),
        P(),
        P(),
        P("ctx", None),
    )
    out_specs = (
        P("ctx", None),
        P("ctx", None),
        P("ctx", "wt"),
        P("ctx", "wt"),
        P("ctx", "wt"),
        P("wt", "ctx"),
        P("ctx", "wt"),
        P("ctx", "wt"),
        P("wt", "ctx"),
        P("ctx"),
        P("ctx"),
        P("ctx"),
        P("ctx"),
    )
    return jax.shard_map(
        on_device, mesh=mesh, in_specs=in_specs, out_specs=out_specs, check_vma=False
    )
```

```python
import functools

import jax
import jax.numpy as jnp
import numpy as np
from jax import lax
from jax.experimental import pallas as pl
from jax.experimental.pallas import tpu as pltpu
from jax.sharding import PartitionSpec as P

EPS = 1e-05
THETA = 1000000.0
NEG = -1e30
SCALE = 0.125
LANES = 128
DOCS = 4
FORWARD_ROWS = 512
BACK_ROWS = 512
GAIN_ROWS = 16
VMEM_LIMIT = 60 * 1024 * 1024
F32 = jnp.float32
BF16 = jnp.bfloat16


def matmul(left, right):
    return jnp.dot(left, right, preferred_element_type=F32)


def contract(left, right, left_dim, right_dim):
    return lax.dot_general(
        left, right, (((left_dim,), (right_dim,)), ((), ())), preferred_element_type=F32
    )


def rms_norm(vector, gain):
    return vector * lax.rsqrt(jnp.mean(vector * vector, axis=-1, keepdims=True) + EPS) * gain


def norm_back(vector, gain, gradient):
    inverse = lax.rsqrt(jnp.mean(vector * vector, axis=-1, keepdims=True) + EPS)
    scaled = gradient * gain
    back = inverse * scaled - vector * inverse**3 * jnp.mean(
        scaled * vector, axis=-1, keepdims=True
    )
    return (back, gradient * vector * inverse)


def lane_index(shape):
    return lax.broadcasted_iota(jnp.int32, shape, len(shape) - 1)


def head_mean(values, head_dim):
    row_id = lax.broadcasted_iota(jnp.int32, (LANES, LANES), 0) // head_dim
    col_id = lax.broadcasted_iota(jnp.int32, (LANES, LANES), 1) // head_dim
    ones = (row_id == col_id).astype(BF16)
    high = values.astype(BF16)
    low = (values - high.astype(F32)).astype(BF16)
    return (matmul(high, ones) + matmul(low, ones)) * (1.0 / head_dim)


def swap_halves(values, head_dim):
    half = head_dim // 2
    lane = lane_index(values.shape)
    return jnp.where(
        lane % head_dim < half,
        pltpu.roll(values, LANES - half, 1),
        pltpu.roll(values, half, 1),
    )


def mix_heads(first, second, head_dim):
    lane = lane_index(first.shape)
    return (
        jnp.where(lane < head_dim, first, pltpu.roll(second, head_dim, 1)),
        jnp.where(lane < head_dim, pltpu.roll(first, head_dim, 1), second),
    )


def mix_low(first, second, head_dim):
    one, two = mix_heads(first.astype(F32), second.astype(F32), head_dim)
    return one.astype(BF16), two.astype(BF16)


def block_tables(base_cos, base_sin, step_cos, step_sin, head_dim):
    cos = base_cos * step_cos - base_sin * step_sin
    sin = base_sin * step_cos + base_cos * step_sin
    lane = lane_index(cos.shape)
    return cos, jnp.where(lane % head_dim < head_dim // 2, -sin, sin)


def head_norm_back(raw, gain, gradient, head_dim):
    inverse = lax.rsqrt(head_mean(raw * raw, head_dim) + EPS)
    scaled = gradient * gain
    back = inverse * scaled - raw * inverse**3 * head_mean(scaled * raw, head_dim)
    return back, jnp.sum(gradient * raw * inverse, axis=0, keepdims=True)


class Info:
    def __init__(self, block_ref, start_ref, devices, half_rows):
        self.block_ref, self.start_ref = block_ref, start_ref
        self.devices, self.half_rows = devices, half_rows
        self.ctx, self.core = lax.axis_index("ctx"), lax.rem(lax.axis_index("wt"), 2)

    def block(self, source, half):
        return self.block_ref[2 * source + jnp.bitwise_xor(half, self.core)]

    def slot_source(self, slot, other):
        column = jnp.bitwise_xor(self.ctx, 1) if other else self.ctx
        return lax.rem(column - 2 * slot + self.devices, self.devices)

    def doc_start(self, position):
        start = jnp.zeros_like(position)
        for doc in range(1, DOCS):
            first = self.start_ref[doc]
            start = jnp.where(position >= first, first, start)
        return start

    def relation(self, query_block, key_block):
        rows = self.half_rows
        low = self.doc_start(query_block * rows)
        high = self.doc_start(query_block * rows + rows - 1)
        visible = (key_block <= query_block) & (key_block * rows + rows - 1 >= low)
        whole = (key_block < query_block) & (key_block * rows >= high)
        return visible, whole

    def mask(self, query_block, key_block, query_dim):
        rows = self.half_rows
        query_pos = query_block * rows + lax.broadcasted_iota(jnp.int32, (rows, rows), query_dim)
        key_pos = key_block * rows + lax.broadcasted_iota(jnp.int32, (rows, rows), 1 - query_dim)
        return (key_pos <= query_pos) & (key_pos >= self.doc_start(query_pos))


def rope_rows(info, tables, half, head_dim):
    base_cos, base_sin, step_cos, step_sin = tables
    block = info.block(info.ctx, half)
    return block_tables(
        base_cos[pl.ds(block, 1), :],
        base_sin[pl.ds(block, 1), :],
        step_cos[...],
        step_sin[...],
        head_dim,
    )


def half_slice(half, rows):
    return slice(half * rows, half * rows + rows)


def twice(ref):
    row = ref[...]
    return jnp.concatenate([row] * (LANES // row.shape[1]), axis=1)


def project_kernel(devices, head_dim, block_ref, x_ref, doc_ref, gain_ref, wq_ref, wk_ref, wv_ref,
                   qg_ref, kg_ref, bc_ref, bs_ref, sc_ref, ss_ref,
                   kv_ref, q_ref, raw_ref, n1_ref, x_out, start_ref):
    rows = x_ref.shape[0] // 2
    start_ref[0] = 0
    for doc in range(1, DOCS):
        start_ref[doc] = jnp.sum((doc_ref[...] < doc).astype(jnp.int32))
    info = Info(block_ref, start_ref, devices, rows)
    tables = (bc_ref, bs_ref, sc_ref, ss_ref)
    query_gain, key_gain = twice(qg_ref), twice(kg_ref)
    chunks = wq_ref.shape[1] // LANES
    for half in range(2):
        here = half_slice(half, rows)
        from_row = pl.multiple_of(jnp.bitwise_xor(half, info.core) * rows, rows)
        x_low = x_ref[pl.ds(from_row, rows), :]
        x_out[here, :] = x_low
        normed = rms_norm(x_low.astype(F32), gain_ref[...]).astype(BF16)
        n1_ref[here, :] = normed
        cos, sin = rope_rows(info, tables, half, head_dim)

        def turned(raw, gain):
            unit = raw * lax.rsqrt(head_mean(raw * raw, head_dim) + EPS) * gain
            return unit * cos + swap_halves(unit, head_dim) * sin

        key_raw = matmul(normed, wk_ref[...])
        kv_ref[here, 0:LANES] = turned(key_raw, key_gain).astype(BF16)
        kv_ref[here, LANES : 2 * LANES] = matmul(normed, wv_ref[...]).astype(BF16)
        raw_ref[here, chunks * LANES : (chunks + 1) * LANES] = key_raw
        query_raw = matmul(normed, wq_ref[...])
        raw_ref[here, 0 : chunks * LANES] = query_raw
        for chunk in range(chunks):
            cols = slice(chunk * LANES, (chunk + 1) * LANES)
            q_ref[here, cols] = (turned(query_raw[:, cols], query_gain) * SCALE).astype(BF16)


def spread_heads(low, rows, half, head_dim, out_ref):
    here = half_slice(half, rows)
    groups = mix_low(low[here, 0:LANES], low[here, LANES : 2 * LANES], head_dim)
    lane = lane_index((rows, LANES))
    for kv in range(2):
        for group in range(2):
            at = (2 * kv + group) * rows
            out_ref[half, at : at + rows, :] = jnp.where(
                lane // head_dim == kv, groups[group].astype(F32), 0.0
            ).astype(BF16)


def join_heads(stacked, rows, head_dim):
    lane = lane_index((rows, LANES))
    groups = [
        jnp.where(
            lane < head_dim,
            stacked[group * rows : (group + 1) * rows],
            stacked[(2 + group) * rows : (3 + group) * rows],
        )
        for group in range(2)
    ]
    return mix_heads(groups[0], groups[1], head_dim)


def fetch(pairs_of_refs, sems):
    copies = [
        pltpu.make_async_copy(source, target, sems.at[at])
        for at, (source, target) in enumerate(pairs_of_refs)
    ]
    for copy in copies:
        copy.start()
    return copies


def attend_slots(info, other, held, spread, total):
    rows = info.half_rows

    def one_key_block(step, carry):
        slot, key_half = step // 2, lax.rem(step, 2)
        key_block = info.block(info.slot_source(slot, other), key_half)
        key_rows = pl.ds(pl.multiple_of(key_half * rows, rows), rows)
        for half in range(2):
            query_block = info.block(info.ctx, half)
            visible, whole = info.relation(query_block, key_block)

            def take(masked, half=half, query_block=query_block):
                keys = held[slot, key_rows, 0:LANES]
                values = jnp.concatenate(
                    [held[slot, key_rows, LANES : 2 * LANES], jnp.ones((rows, LANES), BF16)], axis=1
                )
                if masked:
                    allowed = info.mask(query_block, key_block, 0)
                    allowed = jnp.concatenate([allowed] * (FORWARD_ROWS // rows), axis=0)
                for part in range(4 * rows // FORWARD_ROWS):
                    at = slice(part * FORWARD_ROWS, (part + 1) * FORWARD_ROWS)
                    scores = contract(spread[half, at, :], keys, 1, 1)
                    if masked:
                        scores = jnp.where(allowed, scores, NEG)
                    weights = jnp.exp(scores).astype(BF16)
                    total[half, at, :] += matmul(weights, values)

            pl.when(visible & whole)(functools.partial(take, False))
            pl.when(visible & jnp.logical_not(whole))(functools.partial(take, True))
        return carry

    lax.fori_loop(0, 2 * held.shape[0], one_key_block, 0)


def attend_first_kernel(devices, head_dim, block_ref, start_ref, q_ref, *refs):
    pairs = devices // 2
    slots = refs[:pairs]
    total, spread, held, sems = refs[pairs:]
    rows = q_ref.shape[0] // 2
    info = Info(block_ref, start_ref, devices, rows)
    copies = fetch([(slots[at], held.at[at]) for at in range(pairs)], sems)
    q_low = q_ref[...]
    for half in range(2):
        spread_heads(q_low, rows, half, head_dim, spread)
    total[...] = jnp.zeros_like(total)
    for copy in copies:
        copy.wait()
    attend_slots(info, False, held, spread, total)


def attend_second_kernel(devices, head_dim, block_ref, start_ref, spread, total_ref, wo_ref, *refs):
    pairs = devices // 2
    slots = refs[:pairs]
    o_ref, o32_ref, lse_ref, mine_ref, other_ref, held, total, sems = refs[pairs:]
    rows = o_ref.shape[0] // 2
    info = Info(block_ref, start_ref, devices, rows)
    copies = fetch(
        [(slots[at], held.at[at]) for at in range(pairs)] + [(total_ref, total)], sems
    )
    for copy in copies:
        copy.wait()
    attend_slots(info, True, held, spread, total)
    for half in (1, 0):
        here = half_slice(half, rows)
        sums = total[half, :, LANES : 2 * LANES]
        chunks = join_heads(total[half, :, 0:LANES] / sums, rows, head_dim)
        for chunk in range(2):
            cols = slice(chunk * LANES, (chunk + 1) * LANES)
            o32_ref[here, cols] = chunks[chunk]
            o_ref[here, cols] = chunks[chunk].astype(BF16)
        lse_ref[half] = jnp.transpose(jnp.log(sums))[0:8, :]
        part = matmul(o_ref[here, :], wo_ref[...]).astype(BF16)
        (mine_ref, other_ref)[half][...] = part


def feed_kernel(x_ref, mine_ref, other_ref, gain_ref, wg_ref, wu_ref, dh_ref,
                mid_ref, n2_ref, hid_ref, dgate_ref, dup_ref, part_mine, part_other):
    rows = x_ref.shape[0] // 2
    hidden = wg_ref.shape[1]
    for half in range(2):
        here = half_slice(half, rows)
        middle = x_ref[here, :].astype(F32) + (mine_ref, other_ref)[half][...].astype(F32)
        mid_ref[here, :] = middle
        n2_ref[here, :] = rms_norm(middle, gain_ref[...]).astype(BF16)
    step = 2 * LANES
    for at in range(0, hidden, step):
        cols = slice(at, min(at + step, hidden))
        normed = n2_ref[...]
        gate = matmul(normed, wg_ref[:, cols])
        up = matmul(normed, wu_ref[:, cols])
        grad_hidden = dh_ref[:, cols]
        sigmoid = jax.nn.sigmoid(gate)
        silu = gate * sigmoid
        hid_ref[:, cols] = (silu * up).astype(BF16)
        dgate_ref[:, cols] = (
            grad_hidden * up * sigmoid * (1.0 + gate * (1.0 - sigmoid))
        ).astype(BF16)
        dup_ref[:, cols] = (grad_hidden * silu).astype(BF16)
    for half, part in ((1, part_other), (0, part_mine)):
        here = half_slice(half, rows)
        for at in range(0, wg_ref.shape[0], step):
            wide = slice(at, at + step)
            part[:, wide] = (
                contract(dgate_ref[here, :], wg_ref[wide, :], 1, 1)
                + contract(dup_ref[here, :], wu_ref[wide, :], 1, 1)
            ).astype(BF16)


def prepare_back(info, head_dim, q_ref, do_ref, o32_ref, spread, spread_do, delta):
    rows = info.half_rows
    q_low, do_low = q_ref[...], do_ref[...]
    for half in range(2):
        here = half_slice(half, rows)
        spread_heads(q_low, rows, half, head_dim, spread)
        spread_heads(do_low, rows, half, head_dim, spread_do)
        product = do_low[here, :].astype(F32) * o32_ref[here, :]
        for chunk in range(2):
            turned = jnp.transpose(product[:, chunk * LANES : (chunk + 1) * LANES])
            for group in range(2):
                at = (2 * chunk + group) * rows
                delta[half, :, at : at + rows] = jnp.broadcast_to(
                    jnp.sum(
                        turned[group * head_dim : (group + 1) * head_dim], axis=0, keepdims=True
                    ),
                    (8, rows),
                )


def back_slots(info, other, held, spread, spread_do, lse_ref, delta, dq_t, dkv, out_ref):
    rows = info.half_rows

    def one_key_block(step, carry):
        slot, key_half = step // 2, lax.rem(step, 2)
        source = info.slot_source(slot, other)
        key_block = info.block(source, key_half)
        key_rows = pl.ds(pl.multiple_of(key_half * rows, rows), rows)
        dkv[...] = jnp.zeros_like(dkv)
        for half in range(2):
            query_block = info.block(info.ctx, half)
            visible, whole = info.relation(query_block, key_block)

            def take(masked, half=half, query_block=query_block):
                keys = held[slot, key_rows, 0:LANES]
                values = held[slot, key_rows, LANES : 2 * LANES]
                if masked:
                    allowed = info.mask(query_block, key_block, 1)
                    allowed = jnp.concatenate([allowed] * (BACK_ROWS // rows), axis=1)
                for part in range(4 * rows // BACK_ROWS):
                    at = slice(part * BACK_ROWS, (part + 1) * BACK_ROWS)
                    queries, grads = spread[half, at, :], spread_do[half, at, :]
                    scores = contract(keys, queries, 1, 1) - lse_ref[half, 0:1, at]
                    if masked:
                        scores = jnp.where(allowed, scores, NEG)
                    probs = jnp.exp(scores)
                    grad_probs = contract(values, grads, 1, 1)
                    grad_scores = (probs * (grad_probs - delta[half, 0:1, at])).astype(BF16)
                    dkv[:, LANES : 2 * LANES] += matmul(probs.astype(BF16), grads)
                    dkv[:, 0:LANES] += matmul(grad_scores, queries)
                    dq_t[half, :, at] += contract(keys, grad_scores, 0, 0)

            pl.when(visible & whole)(functools.partial(take, False))
            pl.when(visible & jnp.logical_not(whole))(functools.partial(take, True))
        out_ref[source // 2, key_rows, :] = dkv[...].astype(BF16)
        return carry

    lax.fori_loop(0, 2 * held.shape[0], one_key_block, 0)


def back_first_kernel(devices, head_dim, wt_count, block_ref, start_ref, q_ref, o32_ref, lse_ref,
                      mid_ref, mine_ref, other_ref, c_ref, gain_ref, wo_ref, *refs):
    pairs = devices // 2
    slots = refs[:pairs]
    dkv_out, dq_t, dy_ref, dyb_ref, do_ref, ffn_gain = refs[pairs : pairs + 6]
    held, spread, spread_do, delta, dkv, sems = refs[pairs + 6 :]
    rows = q_ref.shape[0] // 2
    info = Info(block_ref, start_ref, devices, rows)
    copies = fetch([(slots[at], held.at[at]) for at in range(pairs)], sems)
    gain_sum = jnp.zeros((1, gain_ref.shape[1]), F32)
    for half in range(2):
        here = half_slice(half, rows)
        back, terms = norm_back(
            mid_ref[here, :], gain_ref[...], (mine_ref, other_ref)[half][...].astype(F32)
        )
        gain_sum += jnp.sum(terms, axis=0, keepdims=True)
        grad_middle = c_ref[here, :].astype(F32) + back
        dy_ref[here, :] = grad_middle
        dyb_ref[here, :] = grad_middle.astype(BF16)
        do_ref[here, :] = contract(dyb_ref[here, :], wo_ref[...], 1, 1).astype(BF16)
    ffn_gain[...] = gain_sum * (1.0 / wt_count)
    prepare_back(info, head_dim, q_ref, do_ref, o32_ref, spread, spread_do, delta)
    dq_t[...] = jnp.zeros_like(dq_t)
    for copy in copies:
        copy.wait()
    back_slots(info, True, held, spread, spread_do, lse_ref, delta, dq_t, dkv, dkv_out)


def back_second_kernel(devices, head_dim, block_ref, start_ref, q_ref, do_ref, o32_ref, lse_ref,
                       raw_ref, qg_ref, bc_ref, bs_ref, sc_ref, ss_ref, dq_in, *refs):
    pairs = devices // 2
    slots = refs[:pairs]
    dkv_out, dq_ref, gain_ref, held, spread, spread_do, delta, dq_t, dkv, sems = refs[pairs:]
    rows = q_ref.shape[0] // 2
    info = Info(block_ref, start_ref, devices, rows)
    copies = fetch([(slots[at], held.at[at]) for at in range(pairs)] + [(dq_in, dq_t)], sems)
    prepare_back(info, head_dim, q_ref, do_ref, o32_ref, spread, spread_do, delta)
    for copy in copies:
        copy.wait()
    back_slots(info, False, held, spread, spread_do, lse_ref, delta, dq_t, dkv, dkv_out)
    query_gain = twice(qg_ref)
    gain_sum = jnp.zeros((1, LANES), F32)
    for half in range(2):
        here = half_slice(half, rows)
        cos, sin = rope_rows(info, (bc_ref, bs_ref, sc_ref, ss_ref), half, head_dim)
        chunks = join_heads(jnp.transpose(dq_t[half]), rows, head_dim)
        for chunk in range(2):
            cols = slice(chunk * LANES, (chunk + 1) * LANES)
            grad = chunks[chunk] * SCALE
            grad = grad * cos - swap_halves(grad, head_dim) * sin
            back, term = head_norm_back(raw_ref[here, cols], query_gain, grad, head_dim)
            dq_ref[here, cols] = back.astype(BF16)
            gain_sum += term
    gain_ref[...] = gain_sum


def key_back_kernel(devices, head_dim, count, block_ref, start_ref, raw_ref, kg_ref, bc_ref, bs_ref,
                    sc_ref, ss_ref, dq_ref, x_ref, wq_ref, wk_ref, wv_ref, ffn_gain, query_gain,
                    *refs):
    parts = refs[:count]
    dkv_ref, mine_ref, other_ref, gains_ref = refs[count:]
    rows = raw_ref.shape[0] // 2
    width = x_ref.shape[1]
    info = Info(block_ref, start_ref, devices, rows)
    key_gain = twice(kg_ref)
    key_sum = jnp.zeros((1, LANES), F32)
    attn_sum = jnp.zeros((1, width), F32)
    for half in (1, 0):
        here = half_slice(half, rows)
        grad = sum(part[here, :].astype(F32) for part in parts)
        cos, sin = rope_rows(info, (bc_ref, bs_ref, sc_ref, ss_ref), half, head_dim)
        grad_k = grad[:, 0:LANES]
        grad_k = grad_k * cos - swap_halves(grad_k, head_dim) * sin
        back, term = head_norm_back(raw_ref[here, 2 * LANES : 3 * LANES], key_gain, grad_k, head_dim)
        key_sum += term
        key_low, value_low = back.astype(BF16), grad[:, LANES : 2 * LANES].astype(BF16)
        dkv_ref[here, 0:LANES] = key_low
        dkv_ref[here, LANES : 2 * LANES] = value_low
        part = (
            contract(dq_ref[here, :], wq_ref[...], 1, 1)
            + contract(key_low, wk_ref[...], 1, 1)
            + contract(value_low, wv_ref[...], 1, 1)
        )
        (mine_ref, other_ref)[half][...] = part.astype(BF16)
        inputs = x_ref[here, :].astype(F32)
        inverse = lax.rsqrt(jnp.mean(inputs * inputs, axis=-1, keepdims=True) + EPS)
        attn_sum += jnp.sum(part * inputs * inverse, axis=0, keepdims=True)
    gains_ref[:, 0:width] = attn_sum
    gains_ref[:, width : 2 * width] = ffn_gain[...]
    gains_ref[:, 2 * width : 2 * width + LANES] = query_gain[...]
    gains_ref[:, 2 * width + LANES : 2 * width + 2 * LANES] = key_sum


def finish_kernel(x_ref, mine_ref, other_ref, gain_ref, dy_ref, out_ref):
    rows = x_ref.shape[0] // 2
    core = lax.rem(lax.axis_index("wt"), 2)
    for half in range(2):
        here = half_slice(half, rows)
        back, _ = norm_back(
            x_ref[here, :].astype(F32), gain_ref[...], (mine_ref, other_ref)[half][...].astype(F32)
        )
        to_row = pl.multiple_of(jnp.bitwise_xor(half, core) * rows, rows)
        out_ref[pl.ds(to_row, rows), :] = dy_ref[here, :] + back


def put_shard(kept, sent, bit, device, rows, cols, piece):
    index = device // (2 << bit) * (1 << bit) + device % (1 << bit)
    same = lax.rem(lax.axis_index("ctx") // (1 << bit), 2) == device // (1 << bit) % 2

    @pl.when(same)
    def _():
        kept[index, rows, cols] = piece

    @pl.when(jnp.logical_not(same))
    def _():
        sent[index, rows, cols] = piece


def put_rows(kept, sent, bit, shard, row, cols, block):
    for part in range(block.shape[0] // shard):
        piece = block[part * shard : (part + 1) * shard]
        put_shard(kept, sent, bit, row // shard + part, slice(0, shard), cols, piece)


def feed_grad_kernel(c_ref, n2_ref, hid_ref, dgate_ref, dup_ref, wd_ref, mine_ref, other_ref,
                     y_kept, y_sent, z_kept, z_sent):
    rows = c_ref.shape[0] // 2
    width, hidden = c_ref.shape[1], hid_ref.shape[1]
    shard, first = y_kept.shape[1:]
    gate_end = z_kept.shape[2]
    gate_at = 2 * hidden - first
    for half, part in ((1, other_ref), (0, mine_ref)):
        part[...] = matmul(hid_ref[half_slice(half, rows), :], wd_ref[...]).astype(BF16)
    step = 2 * LANES
    for at in range(0, width, step):
        here = slice(at, at + step)
        turned = jnp.transpose(n2_ref[:, here])
        block = matmul(turned, dup_ref[...]).astype(BF16)
        put_rows(y_kept, y_sent, 0, shard, at, slice(0, first), block[:, :first])
        put_rows(z_kept, z_sent, 1, shard, at, slice(hidden, gate_at), block[:, first:])
        block = matmul(turned, dgate_ref[:, : gate_end - gate_at]).astype(BF16)
        put_rows(z_kept, z_sent, 1, shard, at, slice(gate_at, gate_end), block)
        block = matmul(jnp.transpose(c_ref[:, here]), hid_ref[...]).astype(BF16)
        put_rows(z_kept, z_sent, 1, shard, at, slice(0, hidden), block)


def narrow_grad_kernel(devices, count, *refs):
    kept, sent = refs[-2:]
    width = refs[0].shape[1]
    shard = width // devices
    begin = 0
    if len(refs) > 2 * count + 2:
        gains = refs[2 * count][...]
        for device in range(devices):
            at = device * shard
            blank = [jnp.zeros((1, LANES - shard), F32)] if shard < LANES else []
            first = [gains[:, at : at + shard]] + blank
            second = [gains[:, width + at : width + at + shard]] + blank
            block = jnp.concatenate(
                [
                    jnp.concatenate(first + second, axis=1),
                    gains[:, 2 * width : 2 * width + 2 * LANES],
                    jnp.zeros((GAIN_ROWS - 2, 2 * LANES), F32),
                ],
                axis=0,
            ).astype(BF16)
            put_shard(
                kept, sent, 0, device, slice(shard, shard + GAIN_ROWS), slice(0, 2 * LANES), block
            )
    step = 2 * LANES
    for at in range(count):
        left, right = refs[2 * at], refs[2 * at + 1]
        cols = slice(begin, begin + right.shape[1])
        begin = cols.stop
        for row in range(0, width, step):
            block = matmul(jnp.transpose(left[:, row : row + step]), right[...]).astype(BF16)
            put_rows(kept, sent, 0, shard, row, cols, block)


def call_kernel(body, outs, operands, memory, scratch=(), flops=1000, after=()):
    kinds = {
        "s": pl.BlockSpec(memory_space=pltpu.SMEM),
        "v": pl.BlockSpec(memory_space=pltpu.VMEM),
        "a": pl.BlockSpec(memory_space=pl.ANY),
    }
    count = len(operands)

    def whole(*refs):
        body(*refs[:count], *refs[count + len(after) :])

    return pl.pallas_call(
        whole,
        out_shape=[jax.ShapeDtypeStruct(shape, kind) for shape, kind, *_ in outs],
        in_specs=[kinds[m] for m in memory] + [kinds["a"]] * len(after),
        out_specs=[kinds[out[2] if len(out) > 2 else "v"] for out in outs],
        scratch_shapes=list(scratch),
        compiler_params=pltpu.CompilerParams(vmem_limit_bytes=VMEM_LIMIT),
        cost_estimate=pl.CostEstimate(flops=flops, bytes_accessed=0, transcendentals=0),
    )(*operands, *after)


def hold(values, after):
    return pl.pallas_call(
        lambda *refs: None,
        out_shape=jax.ShapeDtypeStruct(values.shape, values.dtype),
        in_specs=[pl.BlockSpec(memory_space=pl.ANY)] * (1 + len(after)),
        out_specs=pl.BlockSpec(memory_space=pl.ANY),
        input_output_aliases={0: 0},
        cost_estimate=pl.CostEstimate(flops=0, bytes_accessed=0, transcendentals=0),
    )(values, *after)


def flip(values, axis, bit):
    size = lax.axis_size(axis)
    return lax.ppermute(values, axis, [(i, i ^ bit) for i in range(size)])


def shift(values, step):
    size = lax.axis_size("ctx")
    return lax.ppermute(values, "ctx", [(i, (i + step) % size) for i in range(size)])


def gather_slots(values):
    pairs = lax.axis_size("ctx") // 2
    same = [values] + [shift(values, 2 * k) for k in range(1, pairs)]
    return same, [flip(part, "ctx", 1) for part in same]


def chip_sum(mine, other):
    return (mine.astype(F32) + flip(other, "wt", 1).astype(F32)).astype(BF16)


def slice_sum(chip):
    whole = (chip.astype(F32) + flip(chip, "wt", 2).astype(F32)).astype(BF16)
    return whole, flip(whole, "wt", 1)


def halve(kept, received, bits, bit):
    after = len([b for b in bits if b < bit])
    view = (-1, 2, 1 << after) + kept.shape[1:]
    kept, received = kept.reshape(view), received.reshape(view)
    side = (lax.axis_index("ctx") // (1 << bit)) % 2

    def pick(at):
        picked = lax.dynamic_index_in_dim(kept, at, 1, keepdims=False).astype(
            F32
        ) + lax.dynamic_index_in_dim(received, at, 1, keepdims=False).astype(F32)
        return picked.astype(BF16).reshape((-1,) + view[3:])

    return pick(side), pick(1 - side)


def last_sum(kept, received):
    return kept[0].astype(F32) + received[0].astype(F32)


def ctx_bits():
    return range(lax.axis_size("ctx").bit_length() - 1)


def scatter_tail(kept, received, bits):
    bits = list(bits)
    sends = []
    for bit in list(bits):
        kept, sent = halve(kept, received, bits, bit)
        bits.remove(bit)
        sends.append(sent)
        received = flip(sent, "ctx", 1 << bit)
    return last_sum(kept, received), sends


def scatter_rest(kept, received, first, waits=()):
    bits = [bit for bit in ctx_bits() if bit != first]
    sends = []
    for step, bit in enumerate(list(bits)):
        if step < len(waits):
            kept = hold(kept, waits[step])
        kept, sent = halve(kept, received, bits, bit)
        bits.remove(bit)
        sends.append(sent)
        received = flip(sent, "ctx", 1 << bit)
    return last_sum(kept, received), sends


def on_device(
    block_in,
    doc_ids,
    block_of,
    w_query,
    w_key,
    w_value,
    w_out,
    w_gate,
    w_up,
    w_down,
    attn_gain,
    ffn_gain,
    query_gain,
    key_gain,
    cotangent,
):
    tok_rows, width = block_in.shape
    half_rows = tok_rows // 2
    head_dim = query_gain.shape[0]
    q_width, kv_width = w_query.shape[1], w_key.shape[1]
    hidden_width = w_gate.shape[1]
    devices = lax.axis_size("ctx")
    pairs = devices // 2
    blocks = block_of.shape[0]
    wt_count = lax.axis_size("wt")
    ctx = lax.axis_index("ctx")
    core = lax.axis_index("wt") % 2
    mine, other = slice(0, half_rows), slice(half_rows, tok_rows)

    half_dim = head_dim // 2
    freqs = THETA ** (-2.0 * (np.arange(LANES) % half_dim).astype(np.float64) / head_dim)
    base_angle = (np.arange(blocks) * half_rows)[:, None] * freqs[None, :]
    step_angle = np.arange(half_rows)[:, None] * freqs[None, :]
    tables = [
        jnp.asarray(table.astype(np.float32))
        for table in (np.cos(base_angle), np.sin(base_angle), np.cos(step_angle), np.sin(step_angle))
    ]
    attn_gain_row, ffn_gain_row = attn_gain[None, :], ffn_gain[None, :]
    query_gain_row, key_gain_row = query_gain[None, :], key_gain[None, :]
    stacked = 4 * half_rows
    half_low = ((half_rows, width), BF16)
    held = pltpu.VMEM((pairs, tok_rows, 2 * kv_width), BF16)
    spread = pltpu.VMEM((2, stacked, LANES), BF16)

    key_value, query, raw, normed_one, x_local, starts = call_kernel(
        functools.partial(project_kernel, devices, head_dim),
        [
            ((tok_rows, 2 * kv_width), BF16),
            ((tok_rows, q_width), BF16),
            ((tok_rows, q_width + kv_width), F32),
            ((tok_rows, width), BF16),
            ((tok_rows, width), BF16),
            ((DOCS,), jnp.int32, "s"),
        ],
        [
            block_of,
            block_in,
            doc_ids.reshape(-1, LANES),
            attn_gain_row,
            w_query,
            w_key,
            w_value,
            query_gain_row,
            key_gain_row,
        ]
        + tables,
        "s" + "v" * 12,
    )
    place = [block_of, starts]
    same_slots, other_slots = gather_slots(key_value)

    out_grad = jnp.where(core == 0, cotangent, jnp.roll(cotangent, half_rows, 0))
    grad_hidden = contract(out_grad, w_down, 1, 1)

    total, spread_query = call_kernel(
        functools.partial(attend_first_kernel, devices, head_dim),
        [((2, stacked, 2 * LANES), F32), ((2, stacked, LANES), BF16)],
        place + [query] + same_slots,
        "ssv" + "a" * pairs,
        [held, pltpu.SemaphoreType.DMA((pairs,))],
        after=[grad_hidden],
    )
    out_low, out_wide, log_total, attn_mine, attn_other = call_kernel(
        functools.partial(attend_second_kernel, devices, head_dim),
        [
            ((tok_rows, q_width), BF16),
            ((tok_rows, q_width), F32),
            ((2, 8, stacked), F32),
            half_low,
            half_low,
        ],
        place + [spread_query, total, w_out] + other_slots,
        "ssvav" + "a" * pairs,
        [held, pltpu.VMEM((2, stacked, 2 * LANES), F32), pltpu.SemaphoreType.DMA((pairs + 1,))],
    )
    attn_mine, attn_other = slice_sum(chip_sum(attn_mine, attn_other))

    middle, normed_two, hidden, grad_gate, grad_upper, part_mine, part_other = call_kernel(
        feed_kernel,
        [
            ((tok_rows, width), F32),
            ((tok_rows, width), BF16),
            ((tok_rows, hidden_width), BF16),
            ((tok_rows, hidden_width), BF16),
            ((tok_rows, hidden_width), BF16),
            half_low,
            half_low,
        ],
        [x_local, attn_mine, attn_other, ffn_gain_row, w_gate, w_up, grad_hidden],
        "v" * 7,
    )
    chip = chip_sum(part_mine, part_other)
    n2_mine, n2_other = slice_sum(chip)

    shard = width // devices
    y_width = hidden_width * 7 // 9 // LANES * LANES
    gate_cut = hidden_width // 3 // LANES * LANES
    gate_at = 2 * hidden_width - y_width
    z_width = gate_at + gate_cut
    ffn_mine, ffn_other, y_kept, y_sent, z_kept, z_sent = call_kernel(
        feed_grad_kernel,
        [half_low, half_low]
        + [((pairs, shard, y_width), BF16)] * 2
        + [((pairs, shard, z_width), BF16)] * 2,
        [out_grad, normed_two, hidden, grad_gate, grad_upper, w_down],
        "v" * 6,
        flops=14 * 10**9,
        after=[chip],
    )
    ffn_chip = hold(chip_sum(ffn_mine, ffn_other), [n2_mine])
    y_received = flip(y_sent, "ctx", 1)
    z_received = flip(z_sent, "ctx", 2)

    grad_other, grad_query_t, grad_middle, grad_middle_low, grad_attended, ffn_gain_part = (
        call_kernel(
            functools.partial(back_first_kernel, devices, head_dim, wt_count),
            [
                ((pairs, tok_rows, 2 * kv_width), BF16),
                ((2, LANES, stacked), F32),
                ((tok_rows, width), F32),
                ((tok_rows, width), BF16),
                ((tok_rows, q_width), BF16),
                ((1, width), F32),
            ],
            place
            + [query, out_wide, log_total, middle, n2_mine, n2_other, out_grad, ffn_gain_row, w_out]
            + other_slots,
            "ss" + "v" * 9 + "a" * pairs,
            [
                held,
                spread,
                spread,
                pltpu.VMEM((2, 8, stacked), F32),
                pltpu.VMEM((half_rows, 2 * LANES), F32),
                pltpu.SemaphoreType.DMA((pairs,)),
            ],
            after=[ffn_chip],
            )
    )
    ffn_mine, ffn_other = slice_sum(ffn_chip)
    grad_same, query_raw_low, query_gain_sum = call_kernel(
        functools.partial(back_second_kernel, devices, head_dim),
        [
            ((pairs, tok_rows, 2 * kv_width), BF16),
            ((tok_rows, q_width), BF16),
            ((1, LANES), F32),
        ],
        place
        + [query, grad_attended, out_wide, log_total, raw, query_gain_row]
        + tables
        + [grad_query_t]
        + same_slots,
        "ss" + "v" * 10 + "a" * (1 + pairs),
        [
            held,
            spread,
            spread,
            pltpu.VMEM((2, 8, stacked), F32),
            pltpu.VMEM((2, LANES, stacked), F32),
            pltpu.VMEM((half_rows, 2 * LANES), F32),
            pltpu.SemaphoreType.DMA((pairs + 1,)),
        ],
        after=[ffn_mine],
    )
    bits = list(ctx_bits())
    key_value_received = flip(grad_other, "ctx", 1)
    y_kept, y_sent = halve(hold(y_kept, [grad_same]), y_received, bits[1:], 1)
    y_received = flip(y_sent, "ctx", 2)
    z_kept, z_sent = halve(hold(z_kept, [y_sent]), z_received, bits[:1] + bits[2:], 0)
    z_received = flip(z_sent, "ctx", 1)
    first_kept, first_sent = call_kernel(
        functools.partial(narrow_grad_kernel, devices, 3),
        [((pairs, shard, hidden_width - gate_cut + 2 * q_width), BF16)] * 2,
        [normed_two, grad_gate[:, gate_cut:], normed_one, query_raw_low, grad_middle_low, out_low],
        "v" * 6,
        flops=8 * 10**9,
        after=[y_sent, z_sent],
    )
    key_value_kept = hold(grad_same, [first_sent])
    key_value_sends = []
    rest = bits[1:]
    for bit in bits[1:]:
        key_value_kept, sent = halve(key_value_kept, key_value_received, rest, bit)
        rest.remove(bit)
        key_value_received = flip(sent, "ctx", 1 << bit)
        key_value_sends.append(sent)
    first_received = flip(hold(first_sent, key_value_sends[:1]), "ctx", 1)
    y_total, _ = scatter_tail(hold(y_kept, key_value_sends[:1]), y_received, bits[2:])
    z_total, z_sends = scatter_tail(hold(z_kept, key_value_sends[1:2]), z_received, bits[2:])

    grad_key_value_low, part_mine, part_other, gains = call_kernel(
        functools.partial(key_back_kernel, devices, head_dim, 2),
        [
            ((tok_rows, 2 * kv_width), BF16),
            half_low,
            half_low,
            ((1, 2 * width + 2 * LANES), F32),
        ],
        place
        + [raw, key_gain_row]
        + tables
        + [query_raw_low, x_local, w_query, w_key, w_value, ffn_gain_part, query_gain_sum]
        + [key_value_kept[0], key_value_received[0]],
        "ss" + "v" * 15,
        after=[y_total, z_sends[-1]],
    )
    n1_chip = chip_sum(part_mine, part_other)
    gains = gains + flip(gains, "wt", 1)
    gains = gains + flip(gains, "wt", 2)
    n1_received = flip(n1_chip, "wt", 2)
    first_kept, first_sent = halve(hold(first_kept, [n1_chip]), first_received, bits[1:], 1)
    first_received = flip(first_sent, "ctx", 2)
    n1_mine = (hold(n1_chip, [first_sent]).astype(F32) + n1_received.astype(F32)).astype(BF16)
    n1_other = flip(n1_mine, "wt", 1)

    second_kept, second_sent = call_kernel(
        functools.partial(narrow_grad_kernel, devices, 1),
        [((pairs, shard + GAIN_ROWS, 2 * kv_width), BF16)] * 2,
        [normed_one, grad_key_value_low, gains],
        "v" * 3,
        flops=3 * 10**9,
        after=[n1_chip],
    )
    (grad_input,) = call_kernel(
        finish_kernel,
        [((tok_rows, width), F32)],
        [x_local, n1_mine, n1_other, attn_gain_row, grad_middle],
        "v" * 5,
    )
    second, second_sends = scatter_rest(
        second_kept, flip(second_sent, "ctx", 1), 0, [[n1_mine], [grad_input]]
    )
    first, _ = scatter_tail(hold(first_kept, [grad_input]), first_received, bits[2:])
    gain_rows = second[shard : shard + 2]

    def head_gain(at):
        row = jnp.sum(gain_rows[1, at * LANES : (at + 1) * LANES].reshape(-1, head_dim), axis=0)
        return lax.dynamic_slice_in_dim(row, ctx * (head_dim // devices), head_dim // devices)

    gate_rest = hidden_width - gate_cut
    out_mine = (middle[mine] + ffn_mine.astype(F32)).astype(BF16)
    out_other = (middle[other] + ffn_other.astype(F32)).astype(BF16)
    return (
        jnp.concatenate(
            [jnp.where(core == 0, out_mine, out_other), jnp.where(core == 0, out_other, out_mine)],
            axis=0,
        ),
        grad_input,
        first[:, gate_rest : gate_rest + q_width],
        second[:shard, :kv_width],
        second[:shard, kv_width:],
        first[:, gate_rest + q_width :].T,
        jnp.concatenate([z_total[:, gate_at:], first[:, :gate_rest]], axis=1),
        jnp.concatenate([y_total, z_total[:, hidden_width:gate_at]], axis=1),
        z_total[:, :hidden_width].T,
        gain_rows[0, :shard],
        gain_rows[0, LANES : LANES + shard],
        head_gain(0),
        head_gain(1),
    )


def solution(mesh):
    in_specs = (
        P("ctx", None),
        P(),
        P(),
        P(None, "wt"),
        P(None, "wt"),
        P(None, "wt"),
        P("wt", None),
        P(None, "wt"),
        P(None, "wt"),
        P("wt", None),
        P(),
        P(),
        P(),
        P(),
        P("ctx", None),
    )
    out_specs = (
        P("ctx", None),
        P("ctx", None),
        P("ctx", "wt"),
        P("ctx", "wt"),
        P("ctx", "wt"),
        P("wt", "ctx"),
        P("ctx", "wt"),
        P("ctx", "wt"),
        P("wt", "ctx"),
        P("ctx"),
        P("ctx"),
        P("ctx"),
        P("ctx"),
    )
    return jax.shard_map(
        on_device, mesh=mesh, in_specs=in_specs, out_specs=out_specs, check_vma=False
    )
```

```python
import functools

import jax
import jax.numpy as jnp
import numpy as np
from jax import lax
from jax.experimental import pallas as pl
from jax.experimental.pallas import tpu as pltpu
from jax.sharding import PartitionSpec as P

EPS = 1e-05
THETA = 1000000.0
NEG = -1e30
SCALE = 0.125
LANES = 128
DOCS = 4
FORWARD_ROWS = 512
BACK_ROWS = 512
GAIN_ROWS = 16
VMEM_LIMIT = 60 * 1024 * 1024
F32 = jnp.float32
BF16 = jnp.bfloat16


def matmul(left, right):
    return jnp.dot(left, right, preferred_element_type=F32)


def contract(left, right, left_dim, right_dim):
    return lax.dot_general(
        left, right, (((left_dim,), (right_dim,)), ((), ())), preferred_element_type=F32
    )


def rms_norm(vector, gain):
    return vector * lax.rsqrt(jnp.mean(vector * vector, axis=-1, keepdims=True) + EPS) * gain


def norm_back(vector, gain, gradient):
    inverse = lax.rsqrt(jnp.mean(vector * vector, axis=-1, keepdims=True) + EPS)
    scaled = gradient * gain
    back = inverse * scaled - vector * inverse**3 * jnp.mean(
        scaled * vector, axis=-1, keepdims=True
    )
    return (back, gradient * vector * inverse)


def lane_index(shape):
    return lax.broadcasted_iota(jnp.int32, shape, len(shape) - 1)


def head_mean(values, head_dim):
    row_id = lax.broadcasted_iota(jnp.int32, (LANES, LANES), 0) // head_dim
    col_id = lax.broadcasted_iota(jnp.int32, (LANES, LANES), 1) // head_dim
    ones = (row_id == col_id).astype(BF16)
    high = values.astype(BF16)
    low = (values - high.astype(F32)).astype(BF16)
    return (matmul(high, ones) + matmul(low, ones)) * (1.0 / head_dim)


def swap_halves(values, head_dim):
    half = head_dim // 2
    lane = lane_index(values.shape)
    return jnp.where(
        lane % head_dim < half,
        pltpu.roll(values, LANES - half, 1),
        pltpu.roll(values, half, 1),
    )


def mix_heads(first, second, head_dim):
    lane = lane_index(first.shape)
    return (
        jnp.where(lane < head_dim, first, pltpu.roll(second, head_dim, 1)),
        jnp.where(lane < head_dim, pltpu.roll(first, head_dim, 1), second),
    )


def mix_low(first, second, head_dim):
    one, two = mix_heads(first.astype(F32), second.astype(F32), head_dim)
    return one.astype(BF16), two.astype(BF16)


def block_tables(base_cos, base_sin, step_cos, step_sin, head_dim):
    cos = base_cos * step_cos - base_sin * step_sin
    sin = base_sin * step_cos + base_cos * step_sin
    lane = lane_index(cos.shape)
    return cos, jnp.where(lane % head_dim < head_dim // 2, -sin, sin)


def head_norm_back(raw, gain, gradient, head_dim):
    inverse = lax.rsqrt(head_mean(raw * raw, head_dim) + EPS)
    scaled = gradient * gain
    back = inverse * scaled - raw * inverse**3 * head_mean(scaled * raw, head_dim)
    return back, jnp.sum(gradient * raw * inverse, axis=0, keepdims=True)


class Info:
    def __init__(self, block_ref, start_ref, devices, half_rows):
        self.block_ref, self.start_ref = block_ref, start_ref
        self.devices, self.half_rows = devices, half_rows
        self.ctx, self.core = lax.axis_index("ctx"), lax.rem(lax.axis_index("wt"), 2)

    def block(self, source, half):
        return self.block_ref[2 * source + jnp.bitwise_xor(half, self.core)]

    def slot_source(self, slot):
        pairs = self.devices // 2
        same = slot < pairs
        column = jnp.where(same, self.ctx, jnp.bitwise_xor(self.ctx, 1))
        step = jnp.where(same, slot, slot - pairs)
        return lax.rem(column - 2 * step + self.devices, self.devices)

    def doc_start(self, position):
        start = jnp.zeros_like(position)
        for doc in range(1, DOCS):
            first = self.start_ref[doc]
            start = jnp.where(position >= first, first, start)
        return start

    def relation(self, query_block, key_block):
        rows = self.half_rows
        low = self.doc_start(query_block * rows)
        high = self.doc_start(query_block * rows + rows - 1)
        visible = (key_block <= query_block) & (key_block * rows + rows - 1 >= low)
        whole = (key_block < query_block) & (key_block * rows >= high)
        return visible, whole

    def mask(self, query_block, key_block, query_dim):
        rows = self.half_rows
        query_pos = query_block * rows + lax.broadcasted_iota(jnp.int32, (rows, rows), query_dim)
        key_pos = key_block * rows + lax.broadcasted_iota(jnp.int32, (rows, rows), 1 - query_dim)
        return (key_pos <= query_pos) & (key_pos >= self.doc_start(query_pos))


def rope_rows(info, tables, half, head_dim):
    base_cos, base_sin, step_cos, step_sin = tables
    block = info.block(info.ctx, half)
    return block_tables(
        base_cos[pl.ds(block, 1), :],
        base_sin[pl.ds(block, 1), :],
        step_cos[...],
        step_sin[...],
        head_dim,
    )


def half_slice(half, rows):
    return slice(half * rows, half * rows + rows)


def twice(ref):
    row = ref[...]
    return jnp.concatenate([row] * (LANES // row.shape[1]), axis=1)


def project_kernel(devices, head_dim, block_ref, x_ref, doc_ref, gain_ref, wq_ref, wk_ref, wv_ref,
                   qg_ref, kg_ref, bc_ref, bs_ref, sc_ref, ss_ref,
                   kv_ref, q_ref, raw_ref, n1_ref, x_out, start_ref):
    rows = x_ref.shape[0] // 2
    start_ref[0] = 0
    for doc in range(1, DOCS):
        start_ref[doc] = jnp.sum((doc_ref[...] < doc).astype(jnp.int32))
    info = Info(block_ref, start_ref, devices, rows)
    tables = (bc_ref, bs_ref, sc_ref, ss_ref)
    query_gain, key_gain = twice(qg_ref), twice(kg_ref)
    chunks = wq_ref.shape[1] // LANES
    for half in range(2):
        here = half_slice(half, rows)
        from_row = pl.multiple_of(jnp.bitwise_xor(half, info.core) * rows, rows)
        x_low = x_ref[pl.ds(from_row, rows), :]
        x_out[here, :] = x_low
        normed = rms_norm(x_low.astype(F32), gain_ref[...]).astype(BF16)
        n1_ref[here, :] = normed
        cos, sin = rope_rows(info, tables, half, head_dim)

        def turned(raw, gain):
            unit = raw * lax.rsqrt(head_mean(raw * raw, head_dim) + EPS) * gain
            return unit * cos + swap_halves(unit, head_dim) * sin

        key_raw = matmul(normed, wk_ref[...])
        kv_ref[here, 0:LANES] = turned(key_raw, key_gain).astype(BF16)
        kv_ref[here, LANES : 2 * LANES] = matmul(normed, wv_ref[...]).astype(BF16)
        raw_ref[here, chunks * LANES : (chunks + 1) * LANES] = key_raw
        query_raw = matmul(normed, wq_ref[...])
        raw_ref[here, 0 : chunks * LANES] = query_raw
        for chunk in range(chunks):
            cols = slice(chunk * LANES, (chunk + 1) * LANES)
            q_ref[here, cols] = (turned(query_raw[:, cols], query_gain) * SCALE).astype(BF16)


def spread_heads(low, rows, half, head_dim, out_ref):
    here = half_slice(half, rows)
    groups = mix_low(low[here, 0:LANES], low[here, LANES : 2 * LANES], head_dim)
    lane = lane_index((rows, LANES))
    for kv in range(2):
        for group in range(2):
            at = (2 * kv + group) * rows
            out_ref[half, at : at + rows, :] = jnp.where(
                lane // head_dim == kv, groups[group].astype(F32), 0.0
            ).astype(BF16)


def join_heads(stacked, rows, head_dim):
    lane = lane_index((rows, LANES))
    groups = [
        jnp.where(
            lane < head_dim,
            stacked[group * rows : (group + 1) * rows],
            stacked[(2 + group) * rows : (3 + group) * rows],
        )
        for group in range(2)
    ]
    return mix_heads(groups[0], groups[1], head_dim)


def fetch(pairs_of_refs, sems):
    copies = [
        pltpu.make_async_copy(source, target, sems.at[at])
        for at, (source, target) in enumerate(pairs_of_refs)
    ]
    for copy in copies:
        copy.start()
    return copies


def attend_slots(info, first_slot, held, spread, total):
    rows = info.half_rows

    def one_key_block(step, carry):
        slot, key_half = step // 2, lax.rem(step, 2)
        key_block = info.block(info.slot_source(first_slot + slot), key_half)
        key_rows = pl.ds(pl.multiple_of(key_half * rows, rows), rows)
        for half in range(2):
            query_block = info.block(info.ctx, half)
            visible, whole = info.relation(query_block, key_block)

            def take(masked, half=half, query_block=query_block):
                keys = held[slot, key_rows, 0:LANES]
                values = jnp.concatenate(
                    [held[slot, key_rows, LANES : 2 * LANES], jnp.ones((rows, LANES), BF16)], axis=1
                )
                if masked:
                    allowed = info.mask(query_block, key_block, 0)
                    allowed = jnp.concatenate([allowed] * (FORWARD_ROWS // rows), axis=0)
                for part in range(4 * rows // FORWARD_ROWS):
                    at = slice(part * FORWARD_ROWS, (part + 1) * FORWARD_ROWS)
                    scores = contract(spread[half, at, :], keys, 1, 1)
                    if masked:
                        scores = jnp.where(allowed, scores, NEG)
                    weights = jnp.exp(scores).astype(BF16)
                    total[half, at, :] += matmul(weights, values)

            pl.when(visible & whole)(functools.partial(take, False))
            pl.when(visible & jnp.logical_not(whole))(functools.partial(take, True))
        return carry

    lax.fori_loop(0, 2 * held.shape[0], one_key_block, 0)


def attend_first_kernel(devices, head_dim, block_ref, start_ref, q_ref, *refs):
    count = devices // 2 + 1
    slots = refs[:count]
    total, spread, held, sems = refs[count:]
    rows = q_ref.shape[0] // 2
    info = Info(block_ref, start_ref, devices, rows)
    copies = fetch([(slots[at], held.at[at]) for at in range(count)], sems)
    q_low = q_ref[...]
    for half in range(2):
        spread_heads(q_low, rows, half, head_dim, spread)
    total[...] = jnp.zeros_like(total)
    for copy in copies:
        copy.wait()
    attend_slots(info, 0, held, spread, total)


def attend_second_kernel(devices, head_dim, block_ref, start_ref, spread, total_ref, wo_ref, *refs):
    count = devices // 2 - 1
    slots = refs[:count]
    o_ref, o32_ref, lse_ref, mine_ref, other_ref, held, total, sems = refs[count:]
    rows = o_ref.shape[0] // 2
    info = Info(block_ref, start_ref, devices, rows)
    copies = fetch(
        [(slots[at], held.at[at]) for at in range(count)] + [(total_ref, total)], sems
    )
    for copy in copies:
        copy.wait()
    attend_slots(info, devices - count, held, spread, total)
    for half in (1, 0):
        here = half_slice(half, rows)
        sums = total[half, :, LANES : 2 * LANES]
        chunks = join_heads(total[half, :, 0:LANES] / sums, rows, head_dim)
        for chunk in range(2):
            cols = slice(chunk * LANES, (chunk + 1) * LANES)
            o32_ref[here, cols] = chunks[chunk]
            o_ref[here, cols] = chunks[chunk].astype(BF16)
        lse_ref[half] = jnp.transpose(jnp.log(sums))[0:8, :]
        part = matmul(o_ref[here, :], wo_ref[...]).astype(BF16)
        (mine_ref, other_ref)[half][...] = part


def feed_kernel(x_ref, mine_ref, other_ref, gain_ref, wg_ref, wu_ref, dh_ref,
                mid_ref, n2_ref, hid_ref, dgate_ref, dup_ref, part_mine, part_other):
    rows = x_ref.shape[0] // 2
    hidden = wg_ref.shape[1]
    for half in range(2):
        here = half_slice(half, rows)
        middle = x_ref[here, :].astype(F32) + (mine_ref, other_ref)[half][...].astype(F32)
        mid_ref[here, :] = middle
        n2_ref[here, :] = rms_norm(middle, gain_ref[...]).astype(BF16)
    step = 2 * LANES
    for at in range(0, hidden, step):
        cols = slice(at, min(at + step, hidden))
        normed = n2_ref[...]
        gate = matmul(normed, wg_ref[:, cols])
        up = matmul(normed, wu_ref[:, cols])
        grad_hidden = dh_ref[:, cols]
        sigmoid = jax.nn.sigmoid(gate)
        silu = gate * sigmoid
        hid_ref[:, cols] = (silu * up).astype(BF16)
        dgate_ref[:, cols] = (
            grad_hidden * up * sigmoid * (1.0 + gate * (1.0 - sigmoid))
        ).astype(BF16)
        dup_ref[:, cols] = (grad_hidden * silu).astype(BF16)
    for half, part in ((1, part_other), (0, part_mine)):
        here = half_slice(half, rows)
        for at in range(0, wg_ref.shape[0], step):
            wide = slice(at, at + step)
            part[:, wide] = (
                contract(dgate_ref[here, :], wg_ref[wide, :], 1, 1)
                + contract(dup_ref[here, :], wu_ref[wide, :], 1, 1)
            ).astype(BF16)


def prepare_back(info, head_dim, q_ref, do_ref, o32_ref, spread, spread_do, delta):
    rows = info.half_rows
    q_low, do_low = q_ref[...], do_ref[...]
    for half in range(2):
        here = half_slice(half, rows)
        spread_heads(q_low, rows, half, head_dim, spread)
        spread_heads(do_low, rows, half, head_dim, spread_do)
        product = do_low[here, :].astype(F32) * o32_ref[here, :]
        for chunk in range(2):
            turned = jnp.transpose(product[:, chunk * LANES : (chunk + 1) * LANES])
            for group in range(2):
                at = (2 * chunk + group) * rows
                delta[half, :, at : at + rows] = jnp.broadcast_to(
                    jnp.sum(
                        turned[group * head_dim : (group + 1) * head_dim], axis=0, keepdims=True
                    ),
                    (8, rows),
                )


def back_slots(info, first_slot, held, spread, spread_do, lse_ref, delta, dq_t, dkv, out_ref):
    rows = info.half_rows

    def one_key_block(step, carry):
        slot, key_half = step // 2, lax.rem(step, 2)
        source = info.slot_source(first_slot + slot)
        key_block = info.block(source, key_half)
        key_rows = pl.ds(pl.multiple_of(key_half * rows, rows), rows)
        dkv[...] = jnp.zeros_like(dkv)
        for half in range(2):
            query_block = info.block(info.ctx, half)
            visible, whole = info.relation(query_block, key_block)

            def take(masked, half=half, query_block=query_block):
                keys = held[slot, key_rows, 0:LANES]
                values = held[slot, key_rows, LANES : 2 * LANES]
                if masked:
                    allowed = info.mask(query_block, key_block, 1)
                    allowed = jnp.concatenate([allowed] * (BACK_ROWS // rows), axis=1)
                for part in range(4 * rows // BACK_ROWS):
                    at = slice(part * BACK_ROWS, (part + 1) * BACK_ROWS)
                    queries, grads = spread[half, at, :], spread_do[half, at, :]
                    scores = contract(keys, queries, 1, 1) - lse_ref[half, 0:1, at]
                    if masked:
                        scores = jnp.where(allowed, scores, NEG)
                    probs = jnp.exp(scores)
                    grad_probs = contract(values, grads, 1, 1)
                    grad_scores = (probs * (grad_probs - delta[half, 0:1, at])).astype(BF16)
                    dkv[:, LANES : 2 * LANES] += matmul(probs.astype(BF16), grads)
                    dkv[:, 0:LANES] += matmul(grad_scores, queries)
                    dq_t[half, :, at] += contract(keys, grad_scores, 0, 0)

            pl.when(visible & whole)(functools.partial(take, False))
            pl.when(visible & jnp.logical_not(whole))(functools.partial(take, True))
        out_ref[source // 2, key_rows, :] = dkv[...].astype(BF16)
        return carry

    lax.fori_loop(0, 2 * held.shape[0], one_key_block, 0)


def back_first_kernel(devices, head_dim, wt_count, block_ref, start_ref, q_ref, o32_ref, lse_ref,
                      mid_ref, mine_ref, other_ref, c_ref, gain_ref, wo_ref, *refs):
    pairs = devices // 2
    slots = refs[:pairs]
    dkv_out, dq_t, dy_ref, dyb_ref, do_ref, ffn_gain = refs[pairs : pairs + 6]
    held, spread, spread_do, delta, dkv, sems = refs[pairs + 6 :]
    rows = q_ref.shape[0] // 2
    info = Info(block_ref, start_ref, devices, rows)
    copies = fetch([(slots[at], held.at[at]) for at in range(pairs)], sems)
    gain_sum = jnp.zeros((1, gain_ref.shape[1]), F32)
    for half in range(2):
        here = half_slice(half, rows)
        back, terms = norm_back(
            mid_ref[here, :], gain_ref[...], (mine_ref, other_ref)[half][...].astype(F32)
        )
        gain_sum += jnp.sum(terms, axis=0, keepdims=True)
        grad_middle = c_ref[here, :].astype(F32) + back
        dy_ref[here, :] = grad_middle
        dyb_ref[here, :] = grad_middle.astype(BF16)
        do_ref[here, :] = contract(dyb_ref[here, :], wo_ref[...], 1, 1).astype(BF16)
    ffn_gain[...] = gain_sum * (1.0 / wt_count)
    prepare_back(info, head_dim, q_ref, do_ref, o32_ref, spread, spread_do, delta)
    dq_t[...] = jnp.zeros_like(dq_t)
    for copy in copies:
        copy.wait()
    back_slots(info, pairs, held, spread, spread_do, lse_ref, delta, dq_t, dkv, dkv_out)


def back_second_kernel(devices, head_dim, block_ref, start_ref, q_ref, do_ref, o32_ref, lse_ref,
                       raw_ref, qg_ref, bc_ref, bs_ref, sc_ref, ss_ref, dq_in, *refs):
    pairs = devices // 2
    slots = refs[:pairs]
    dkv_out, dq_ref, gain_ref, held, spread, spread_do, delta, dq_t, dkv, sems = refs[pairs:]
    rows = q_ref.shape[0] // 2
    info = Info(block_ref, start_ref, devices, rows)
    copies = fetch([(slots[at], held.at[at]) for at in range(pairs)] + [(dq_in, dq_t)], sems)
    prepare_back(info, head_dim, q_ref, do_ref, o32_ref, spread, spread_do, delta)
    for copy in copies:
        copy.wait()
    back_slots(info, 0, held, spread, spread_do, lse_ref, delta, dq_t, dkv, dkv_out)
    query_gain = twice(qg_ref)
    gain_sum = jnp.zeros((1, LANES), F32)
    for half in range(2):
        here = half_slice(half, rows)
        cos, sin = rope_rows(info, (bc_ref, bs_ref, sc_ref, ss_ref), half, head_dim)
        chunks = join_heads(jnp.transpose(dq_t[half]), rows, head_dim)
        for chunk in range(2):
            cols = slice(chunk * LANES, (chunk + 1) * LANES)
            grad = chunks[chunk] * SCALE
            grad = grad * cos - swap_halves(grad, head_dim) * sin
            back, term = head_norm_back(raw_ref[here, cols], query_gain, grad, head_dim)
            dq_ref[here, cols] = back.astype(BF16)
            gain_sum += term
    gain_ref[...] = gain_sum


def key_back_kernel(devices, head_dim, count, block_ref, start_ref, raw_ref, kg_ref, bc_ref, bs_ref,
                    sc_ref, ss_ref, dq_ref, x_ref, wq_ref, wk_ref, wv_ref, ffn_gain, query_gain,
                    *refs):
    parts = refs[:count]
    dkv_ref, mine_ref, other_ref, gains_ref = refs[count:]
    rows = raw_ref.shape[0] // 2
    width = x_ref.shape[1]
    info = Info(block_ref, start_ref, devices, rows)
    key_gain = twice(kg_ref)
    key_sum = jnp.zeros((1, LANES), F32)
    attn_sum = jnp.zeros((1, width), F32)
    for half in (1, 0):
        here = half_slice(half, rows)
        grad = sum(part[here, :].astype(F32) for part in parts)
        cos, sin = rope_rows(info, (bc_ref, bs_ref, sc_ref, ss_ref), half, head_dim)
        grad_k = grad[:, 0:LANES]
        grad_k = grad_k * cos - swap_halves(grad_k, head_dim) * sin
        back, term = head_norm_back(raw_ref[here, 2 * LANES : 3 * LANES], key_gain, grad_k, head_dim)
        key_sum += term
        key_low, value_low = back.astype(BF16), grad[:, LANES : 2 * LANES].astype(BF16)
        dkv_ref[here, 0:LANES] = key_low
        dkv_ref[here, LANES : 2 * LANES] = value_low
        part = (
            contract(dq_ref[here, :], wq_ref[...], 1, 1)
            + contract(key_low, wk_ref[...], 1, 1)
            + contract(value_low, wv_ref[...], 1, 1)
        )
        (mine_ref, other_ref)[half][...] = part.astype(BF16)
        inputs = x_ref[here, :].astype(F32)
        inverse = lax.rsqrt(jnp.mean(inputs * inputs, axis=-1, keepdims=True) + EPS)
        attn_sum += jnp.sum(part * inputs * inverse, axis=0, keepdims=True)
    gains_ref[:, 0:width] = attn_sum
    gains_ref[:, width : 2 * width] = ffn_gain[...]
    gains_ref[:, 2 * width : 2 * width + LANES] = query_gain[...]
    gains_ref[:, 2 * width + LANES : 2 * width + 2 * LANES] = key_sum


def finish_kernel(x_ref, mine_ref, other_ref, gain_ref, dy_ref, out_ref):
    rows = x_ref.shape[0] // 2
    core = lax.rem(lax.axis_index("wt"), 2)
    for half in range(2):
        here = half_slice(half, rows)
        back, _ = norm_back(
            x_ref[here, :].astype(F32), gain_ref[...], (mine_ref, other_ref)[half][...].astype(F32)
        )
        to_row = pl.multiple_of(jnp.bitwise_xor(half, core) * rows, rows)
        out_ref[pl.ds(to_row, rows), :] = dy_ref[here, :] + back


def put_shard(kept, sent, bit, device, rows, cols, piece):
    index = device // (2 << bit) * (1 << bit) + device % (1 << bit)
    same = lax.rem(lax.axis_index("ctx") // (1 << bit), 2) == device // (1 << bit) % 2

    @pl.when(same)
    def _():
        kept[index, rows, cols] = piece

    @pl.when(jnp.logical_not(same))
    def _():
        sent[index, rows, cols] = piece


def put_rows(kept, sent, bit, shard, row, cols, block):
    for part in range(block.shape[0] // shard):
        piece = block[part * shard : (part + 1) * shard]
        put_shard(kept, sent, bit, row // shard + part, slice(0, shard), cols, piece)


def feed_grad_kernel(c_ref, n2_ref, hid_ref, dgate_ref, dup_ref, wd_ref, mine_ref, other_ref,
                     y_kept, y_sent, z_kept, z_sent):
    rows = c_ref.shape[0] // 2
    width, hidden = c_ref.shape[1], hid_ref.shape[1]
    shard, first = y_kept.shape[1:]
    gate_end = z_kept.shape[2]
    gate_at = 2 * hidden - first
    for half, part in ((1, other_ref), (0, mine_ref)):
        part[...] = matmul(hid_ref[half_slice(half, rows), :], wd_ref[...]).astype(BF16)
    step = 2 * LANES
    for at in range(0, width, step):
        here = slice(at, at + step)
        turned = jnp.transpose(n2_ref[:, here])
        block = matmul(turned, dup_ref[...]).astype(BF16)
        put_rows(y_kept, y_sent, 0, shard, at, slice(0, first), block[:, :first])
        put_rows(z_kept, z_sent, 1, shard, at, slice(hidden, gate_at), block[:, first:])
        block = matmul(turned, dgate_ref[:, : gate_end - gate_at]).astype(BF16)
        put_rows(z_kept, z_sent, 1, shard, at, slice(gate_at, gate_end), block)
        block = matmul(jnp.transpose(c_ref[:, here]), hid_ref[...]).astype(BF16)
        put_rows(z_kept, z_sent, 1, shard, at, slice(0, hidden), block)


def narrow_grad_kernel(devices, skips, *refs):
    kept, sent = refs[-2:]
    count = len(skips)
    width = refs[0].shape[1]
    shard = width // devices
    begin = 0
    if len(refs) > 2 * count + 2:
        gains = refs[2 * count][...]
        for device in range(devices):
            at = device * shard
            blank = [jnp.zeros((1, LANES - shard), F32)] if shard < LANES else []
            first = [gains[:, at : at + shard]] + blank
            second = [gains[:, width + at : width + at + shard]] + blank
            block = jnp.concatenate(
                [
                    jnp.concatenate(first + second, axis=1),
                    gains[:, 2 * width : 2 * width + 2 * LANES],
                    jnp.zeros((GAIN_ROWS - 2, 2 * LANES), F32),
                ],
                axis=0,
            ).astype(BF16)
            put_shard(
                kept, sent, 0, device, slice(shard, shard + GAIN_ROWS), slice(0, 2 * LANES), block
            )
    step = 2 * LANES
    for at in range(count):
        left, right = refs[2 * at], refs[2 * at + 1]
        cols = slice(begin, begin + right.shape[1] - skips[at])
        begin = cols.stop
        for row in range(0, width, step):
            block = matmul(jnp.transpose(left[:, row : row + step]), right[:, skips[at] :])
            block = block.astype(BF16)
            put_rows(kept, sent, 0, shard, row, cols, block)


def call_kernel(body, outs, operands, memory, scratch=(), flops=1000, after=()):
    kinds = {
        "s": pl.BlockSpec(memory_space=pltpu.SMEM),
        "v": pl.BlockSpec(memory_space=pltpu.VMEM),
        "a": pl.BlockSpec(memory_space=pl.ANY),
    }
    count = len(operands)

    def whole(*refs):
        body(*refs[:count], *refs[count + len(after) :])

    return pl.pallas_call(
        whole,
        out_shape=[jax.ShapeDtypeStruct(shape, kind) for shape, kind, *_ in outs],
        in_specs=[kinds[m] for m in memory] + [kinds["a"]] * len(after),
        out_specs=[kinds[out[2] if len(out) > 2 else "v"] for out in outs],
        scratch_shapes=list(scratch),
        compiler_params=pltpu.CompilerParams(vmem_limit_bytes=VMEM_LIMIT),
        cost_estimate=pl.CostEstimate(flops=flops, bytes_accessed=0, transcendentals=0),
    )(*operands, *after)


def hold(values, after):
    return pl.pallas_call(
        lambda *refs: None,
        out_shape=jax.ShapeDtypeStruct(values.shape, values.dtype),
        in_specs=[pl.BlockSpec(memory_space=pl.ANY)] * (1 + len(after)),
        out_specs=pl.BlockSpec(memory_space=pl.ANY),
        input_output_aliases={0: 0},
        cost_estimate=pl.CostEstimate(flops=0, bytes_accessed=0, transcendentals=0),
    )(values, *after)


def flip(values, axis, bit):
    size = lax.axis_size(axis)
    return lax.ppermute(values, axis, [(i, i ^ bit) for i in range(size)])


def shift(values, step):
    size = lax.axis_size("ctx")
    return lax.ppermute(values, "ctx", [(i, (i + step) % size) for i in range(size)])


def gather_slots(values):
    pairs = lax.axis_size("ctx") // 2
    same = [values] + [shift(values, 2 * k) for k in range(1, pairs)]
    return same, [flip(part, "ctx", 1) for part in same]


def chip_sum(mine, other):
    return (mine.astype(F32) + flip(other, "wt", 1).astype(F32)).astype(BF16)


def slice_sum(chip):
    whole = (chip.astype(F32) + flip(chip, "wt", 2).astype(F32)).astype(BF16)
    return whole, flip(whole, "wt", 1)


def halve(kept, received, bits, bit):
    after = len([b for b in bits if b < bit])
    view = (-1, 2, 1 << after) + kept.shape[1:]
    kept, received = kept.reshape(view), received.reshape(view)
    side = (lax.axis_index("ctx") // (1 << bit)) % 2

    def pick(at):
        picked = lax.dynamic_index_in_dim(kept, at, 1, keepdims=False).astype(
            F32
        ) + lax.dynamic_index_in_dim(received, at, 1, keepdims=False).astype(F32)
        return picked.astype(BF16).reshape((-1,) + view[3:])

    return pick(side), pick(1 - side)


def last_sum(kept, received):
    return kept[0].astype(F32) + received[0].astype(F32)


def ctx_bits():
    return range(lax.axis_size("ctx").bit_length() - 1)


def scatter_tail(kept, received, bits):
    bits = list(bits)
    sends = []
    for bit in list(bits):
        kept, sent = halve(kept, received, bits, bit)
        bits.remove(bit)
        sends.append(sent)
        received = flip(sent, "ctx", 1 << bit)
    return last_sum(kept, received), sends


def scatter_tail_from(kept, received, bits):
    if len(bits) == 1:
        return last_sum(kept, received), []
    return scatter_tail(kept, received, bits[1:])


def scatter_rest(kept, received, first, waits=()):
    bits = [bit for bit in ctx_bits() if bit != first]
    sends = []
    for step, bit in enumerate(list(bits)):
        if step < len(waits):
            kept = hold(kept, waits[step])
        kept, sent = halve(kept, received, bits, bit)
        bits.remove(bit)
        sends.append(sent)
        received = flip(sent, "ctx", 1 << bit)
    return last_sum(kept, received), sends


def on_device(
    block_in,
    doc_ids,
    block_of,
    w_query,
    w_key,
    w_value,
    w_out,
    w_gate,
    w_up,
    w_down,
    attn_gain,
    ffn_gain,
    query_gain,
    key_gain,
    cotangent,
):
    tok_rows, width = block_in.shape
    half_rows = tok_rows // 2
    head_dim = query_gain.shape[0]
    q_width, kv_width = w_query.shape[1], w_key.shape[1]
    hidden_width = w_gate.shape[1]
    devices = lax.axis_size("ctx")
    pairs = devices // 2
    blocks = block_of.shape[0]
    wt_count = lax.axis_size("wt")
    ctx = lax.axis_index("ctx")
    core = lax.axis_index("wt") % 2
    mine, other = slice(0, half_rows), slice(half_rows, tok_rows)

    half_dim = head_dim // 2
    freqs = THETA ** (-2.0 * (np.arange(LANES) % half_dim).astype(np.float64) / head_dim)
    base_angle = (np.arange(blocks) * half_rows)[:, None] * freqs[None, :]
    step_angle = np.arange(half_rows)[:, None] * freqs[None, :]
    tables = [
        jnp.asarray(table.astype(np.float32))
        for table in (np.cos(base_angle), np.sin(base_angle), np.cos(step_angle), np.sin(step_angle))
    ]
    attn_gain_row, ffn_gain_row = attn_gain[None, :], ffn_gain[None, :]
    query_gain_row, key_gain_row = query_gain[None, :], key_gain[None, :]
    stacked = 4 * half_rows
    half_low = ((half_rows, width), BF16)
    held = pltpu.VMEM((pairs, tok_rows, 2 * kv_width), BF16)
    spread = pltpu.VMEM((2, stacked, LANES), BF16)

    key_value, query, raw, normed_one, x_local, starts = call_kernel(
        functools.partial(project_kernel, devices, head_dim),
        [
            ((tok_rows, 2 * kv_width), BF16),
            ((tok_rows, q_width), BF16),
            ((tok_rows, q_width + kv_width), F32),
            ((tok_rows, width), BF16),
            ((tok_rows, width), BF16),
            ((DOCS,), jnp.int32, "s"),
        ],
        [
            block_of,
            block_in,
            doc_ids.reshape(-1, LANES),
            attn_gain_row,
            w_query,
            w_key,
            w_value,
            query_gain_row,
            key_gain_row,
        ]
        + tables,
        "s" + "v" * 12,
    )
    place = [block_of, starts]
    same_slots, other_slots = gather_slots(key_value)

    out_grad = jnp.where(core == 0, cotangent, jnp.roll(cotangent, half_rows, 0))
    grad_hidden = contract(out_grad, w_down, 1, 1)

    total, spread_query = call_kernel(
        functools.partial(attend_first_kernel, devices, head_dim),
        [((2, stacked, 2 * LANES), F32), ((2, stacked, LANES), BF16)],
        place + [query] + same_slots + other_slots[:1],
        "ssv" + "a" * (pairs + 1),
        [
            pltpu.VMEM((pairs + 1, tok_rows, 2 * kv_width), BF16),
            pltpu.SemaphoreType.DMA((pairs + 1,)),
        ],
        after=[grad_hidden],
    )
    out_low, out_wide, log_total, attn_mine, attn_other = call_kernel(
        functools.partial(attend_second_kernel, devices, head_dim),
        [
            ((tok_rows, q_width), BF16),
            ((tok_rows, q_width), F32),
            ((2, 8, stacked), F32),
            half_low,
            half_low,
        ],
        place + [spread_query, total, w_out] + other_slots[1:],
        "ssvav" + "a" * (pairs - 1),
        [
            pltpu.VMEM((pairs - 1, tok_rows, 2 * kv_width), BF16),
            pltpu.VMEM((2, stacked, 2 * LANES), F32),
            pltpu.SemaphoreType.DMA((pairs,)),
        ],
    )
    attn_mine, attn_other = slice_sum(chip_sum(attn_mine, attn_other))

    middle, normed_two, hidden, grad_gate, grad_upper, part_mine, part_other = call_kernel(
        feed_kernel,
        [
            ((tok_rows, width), F32),
            ((tok_rows, width), BF16),
            ((tok_rows, hidden_width), BF16),
            ((tok_rows, hidden_width), BF16),
            ((tok_rows, hidden_width), BF16),
            half_low,
            half_low,
        ],
        [x_local, attn_mine, attn_other, ffn_gain_row, w_gate, w_up, grad_hidden],
        "v" * 7,
    )
    chip = chip_sum(part_mine, part_other)
    n2_mine, n2_other = slice_sum(chip)

    shard = width // devices
    y_width = hidden_width * 7 // 9 // LANES * LANES
    gate_cut = hidden_width // 3 // LANES * LANES
    gate_at = 2 * hidden_width - y_width
    z_width = gate_at + gate_cut
    ffn_mine, ffn_other, y_kept, y_sent, z_kept, z_sent = call_kernel(
        feed_grad_kernel,
        [half_low, half_low]
        + [((pairs, shard, y_width), BF16)] * 2
        + [((pairs, shard, z_width), BF16)] * 2,
        [out_grad, normed_two, hidden, grad_gate, grad_upper, w_down],
        "v" * 6,
        flops=14 * 10**9,
        after=[chip],
    )
    ffn_chip = hold(chip_sum(ffn_mine, ffn_other), [n2_mine])
    y_received = flip(y_sent, "ctx", 1)
    z_received = flip(z_sent, "ctx", 2)

    grad_other, grad_query_t, grad_middle, grad_middle_low, grad_attended, ffn_gain_part = (
        call_kernel(
            functools.partial(back_first_kernel, devices, head_dim, wt_count),
            [
                ((pairs, tok_rows, 2 * kv_width), BF16),
                ((2, LANES, stacked), F32),
                ((tok_rows, width), F32),
                ((tok_rows, width), BF16),
                ((tok_rows, q_width), BF16),
                ((1, width), F32),
            ],
            place
            + [query, out_wide, log_total, middle, n2_mine, n2_other, out_grad, ffn_gain_row, w_out]
            + other_slots,
            "ss" + "v" * 9 + "a" * pairs,
            [
                held,
                spread,
                spread,
                pltpu.VMEM((2, 8, stacked), F32),
                pltpu.VMEM((half_rows, 2 * LANES), F32),
                pltpu.SemaphoreType.DMA((pairs,)),
            ],
            after=[ffn_chip],
            )
    )
    ffn_mine, ffn_other = slice_sum(ffn_chip)
    grad_same, query_raw_low, query_gain_sum = call_kernel(
        functools.partial(back_second_kernel, devices, head_dim),
        [
            ((pairs, tok_rows, 2 * kv_width), BF16),
            ((tok_rows, q_width), BF16),
            ((1, LANES), F32),
        ],
        place
        + [query, grad_attended, out_wide, log_total, raw, query_gain_row]
        + tables
        + [grad_query_t]
        + same_slots,
        "ss" + "v" * 10 + "a" * (1 + pairs),
        [
            held,
            spread,
            spread,
            pltpu.VMEM((2, 8, stacked), F32),
            pltpu.VMEM((2, LANES, stacked), F32),
            pltpu.VMEM((half_rows, 2 * LANES), F32),
            pltpu.SemaphoreType.DMA((pairs + 1,)),
        ],
        after=[ffn_mine],
    )
    bits = list(ctx_bits())
    key_value_received = flip(grad_other, "ctx", 1)
    y_kept, y_sent = halve(hold(y_kept, [grad_same]), y_received, bits[1:], 1)
    y_received = flip(y_sent, "ctx", 2)
    first_kept, first_sent = call_kernel(
        functools.partial(narrow_grad_kernel, devices, (gate_cut, 0, 0)),
        [((pairs, shard, hidden_width - gate_cut + 2 * q_width), BF16)] * 2,
        [normed_two, grad_gate, normed_one, query_raw_low, grad_middle_low, out_low],
        "v" * 6,
        after=[y_sent],
    )
    z_kept, z_sent = halve(hold(z_kept, [first_sent]), z_received, bits[:1] + bits[2:], 0)
    z_received = flip(z_sent, "ctx", 1)
    key_value_kept = hold(grad_same, [z_sent])
    key_value_sends = []
    rest = bits[1:]
    for bit in bits[1:]:
        key_value_kept, sent = halve(key_value_kept, key_value_received, rest, bit)
        rest.remove(bit)
        key_value_received = flip(sent, "ctx", 1 << bit)
        key_value_sends.append(sent)
    first_received = flip(hold(first_sent, key_value_sends[:1]), "ctx", 1)
    z_kept, z_sent = halve(hold(z_kept, key_value_sends[1:2]), z_received, bits[2:], bits[2])
    z_received = flip(z_sent, "ctx", 1 << bits[2])
    y_total, _ = scatter_tail(hold(y_kept, key_value_sends[:1]), y_received, bits[2:])

    grad_key_value_low, part_mine, part_other, gains = call_kernel(
        functools.partial(key_back_kernel, devices, head_dim, 2),
        [
            ((tok_rows, 2 * kv_width), BF16),
            half_low,
            half_low,
            ((1, 2 * width + 2 * LANES), F32),
        ],
        place
        + [raw, key_gain_row]
        + tables
        + [query_raw_low, x_local, w_query, w_key, w_value, ffn_gain_part, query_gain_sum]
        + [key_value_kept[0], key_value_received[0]],
        "ss" + "v" * 15,
        after=[y_total, z_sent],
    )
    n1_chip = chip_sum(part_mine, part_other)
    n1_received = flip(n1_chip, "wt", 2)

    second_kept, second_sent = call_kernel(
        functools.partial(narrow_grad_kernel, devices, (0,)),
        [((pairs, shard + GAIN_ROWS, 2 * kv_width), BF16)] * 2,
        [normed_one, grad_key_value_low, gains],
        "v" * 3,
        after=[n1_chip],
    )
    first_kept, first_sent = halve(hold(first_kept, [second_sent]), first_received, bits[1:], 1)
    first_received = flip(first_sent, "ctx", 2)
    n1_mine = (hold(n1_chip, [first_sent]).astype(F32) + n1_received.astype(F32)).astype(BF16)
    n1_other = flip(n1_mine, "wt", 1)
    second_kept, second_sent = halve(
        hold(second_kept, [n1_mine]), flip(second_sent, "ctx", 1), bits[1:], 1
    )
    second_received = flip(second_sent, "ctx", 2)
    (grad_input,) = call_kernel(
        finish_kernel,
        [((tok_rows, width), F32)],
        [x_local, n1_mine, n1_other, attn_gain_row, grad_middle],
        "v" * 5,
        after=[second_sent],
    )
    first, first_sends = scatter_tail(hold(first_kept, [grad_input]), first_received, bits[2:])
    second, second_sends = scatter_tail(
        hold(second_kept, first_sends[-1:]), second_received, bits[2:]
    )
    z_total, _ = scatter_tail_from(hold(z_kept, second_sends[-1:]), z_received, bits[2:])
    gain_rows = second[shard : shard + 2]
    gain_rows = sum([flip(gain_rows, "wt", other_wt) for other_wt in range(1, wt_count)], gain_rows)

    def head_gain(at):
        row = jnp.sum(gain_rows[1, at * LANES : (at + 1) * LANES].reshape(-1, head_dim), axis=0)
        return lax.dynamic_slice_in_dim(row, ctx * (head_dim // devices), head_dim // devices)

    gate_rest = hidden_width - gate_cut
    ffn_mine = hold(ffn_mine, [n1_mine])
    out_mine = (middle[mine] + ffn_mine.astype(F32)).astype(BF16)
    out_other = (middle[other] + ffn_other.astype(F32)).astype(BF16)
    return (
        jnp.concatenate(
            [jnp.where(core == 0, out_mine, out_other), jnp.where(core == 0, out_other, out_mine)],
            axis=0,
        ),
        grad_input,
        first[:, gate_rest : gate_rest + q_width],
        second[:shard, :kv_width],
        second[:shard, kv_width:],
        first[:, gate_rest + q_width :].T,
        jnp.concatenate([z_total[:, gate_at:], first[:, :gate_rest]], axis=1),
        jnp.concatenate([y_total, z_total[:, hidden_width:gate_at]], axis=1),
        z_total[:, :hidden_width].T,
        gain_rows[0, :shard],
        gain_rows[0, LANES : LANES + shard],
        head_gain(0),
        head_gain(1),
    )


def solution(mesh):
    in_specs = (
        P("ctx", None),
        P(),
        P(),
        P(None, "wt"),
        P(None, "wt"),
        P(None, "wt"),
        P("wt", None),
        P(None, "wt"),
        P(None, "wt"),
        P("wt", None),
        P(),
        P(),
        P(),
        P(),
        P("ctx", None),
    )
    out_specs = (
        P("ctx", None),
        P("ctx", None),
        P("ctx", "wt"),
        P("ctx", "wt"),
        P("ctx", "wt"),
        P("wt", "ctx"),
        P("ctx", "wt"),
        P("ctx", "wt"),
        P("wt", "ctx"),
        P("ctx"),
        P("ctx"),
        P("ctx"),
        P("ctx"),
    )
    return jax.shard_map(
        on_device, mesh=mesh, in_specs=in_specs, out_specs=out_specs, check_vma=False
    )
```

```python
import functools

import jax
import jax.numpy as jnp
import numpy as np
from jax import lax
from jax.experimental import pallas as pl
from jax.experimental.pallas import tpu as pltpu
from jax.sharding import PartitionSpec as P

EPS = 1e-05
THETA = 1000000.0
NEG = -1e30
SCALE = 0.125
LANES = 128
DOCS = 4
FORWARD_ROWS = 512
BACK_ROWS = 512
GAIN_ROWS = 16
VMEM_LIMIT = 60 * 1024 * 1024
F32 = jnp.float32
BF16 = jnp.bfloat16


def matmul(left, right):
    return jnp.dot(left, right, preferred_element_type=F32)


def contract(left, right, left_dim, right_dim):
    return lax.dot_general(
        left, right, (((left_dim,), (right_dim,)), ((), ())), preferred_element_type=F32
    )


def rms_norm(vector, gain):
    return vector * lax.rsqrt(jnp.mean(vector * vector, axis=-1, keepdims=True) + EPS) * gain


def norm_back(vector, gain, gradient):
    inverse = lax.rsqrt(jnp.mean(vector * vector, axis=-1, keepdims=True) + EPS)
    scaled = gradient * gain
    back = inverse * scaled - vector * inverse**3 * jnp.mean(
        scaled * vector, axis=-1, keepdims=True
    )
    return (back, gradient * vector * inverse)


def lane_index(shape):
    return lax.broadcasted_iota(jnp.int32, shape, len(shape) - 1)


def head_mean(values, head_dim):
    row_id = lax.broadcasted_iota(jnp.int32, (LANES, LANES), 0) // head_dim
    col_id = lax.broadcasted_iota(jnp.int32, (LANES, LANES), 1) // head_dim
    ones = (row_id == col_id).astype(BF16)
    high = values.astype(BF16)
    low = (values - high.astype(F32)).astype(BF16)
    return (matmul(high, ones) + matmul(low, ones)) * (1.0 / head_dim)


def swap_halves(values, head_dim):
    half = head_dim // 2
    lane = lane_index(values.shape)
    return jnp.where(
        lane % head_dim < half,
        pltpu.roll(values, LANES - half, 1),
        pltpu.roll(values, half, 1),
    )


def mix_heads(first, second, head_dim):
    lane = lane_index(first.shape)
    return (
        jnp.where(lane < head_dim, first, pltpu.roll(second, head_dim, 1)),
        jnp.where(lane < head_dim, pltpu.roll(first, head_dim, 1), second),
    )


def mix_low(first, second, head_dim):
    one, two = mix_heads(first.astype(F32), second.astype(F32), head_dim)
    return one.astype(BF16), two.astype(BF16)


def block_tables(base_cos, base_sin, step_cos, step_sin, head_dim):
    cos = base_cos * step_cos - base_sin * step_sin
    sin = base_sin * step_cos + base_cos * step_sin
    lane = lane_index(cos.shape)
    return cos, jnp.where(lane % head_dim < head_dim // 2, -sin, sin)


def head_norm_back(raw, gain, gradient, head_dim):
    inverse = lax.rsqrt(head_mean(raw * raw, head_dim) + EPS)
    scaled = gradient * gain
    back = inverse * scaled - raw * inverse**3 * head_mean(scaled * raw, head_dim)
    return back, jnp.sum(gradient * raw * inverse, axis=0, keepdims=True)


class Info:
    def __init__(self, block_ref, start_ref, devices, half_rows):
        self.block_ref, self.start_ref = block_ref, start_ref
        self.devices, self.half_rows = devices, half_rows
        self.ctx, self.core = lax.axis_index("ctx"), lax.rem(lax.axis_index("wt"), 2)

    def block(self, source, half):
        return self.block_ref[2 * source + jnp.bitwise_xor(half, self.core)]

    def slot_source(self, slot):
        pairs = self.devices // 2
        same = slot < pairs
        column = jnp.where(same, self.ctx, jnp.bitwise_xor(self.ctx, 1))
        step = jnp.where(same, slot, slot - pairs)
        return lax.rem(column - 2 * step + self.devices, self.devices)

    def doc_start(self, position):
        start = jnp.zeros_like(position)
        for doc in range(1, DOCS):
            first = self.start_ref[doc]
            start = jnp.where(position >= first, first, start)
        return start

    def relation(self, query_block, key_block):
        rows = self.half_rows
        low = self.doc_start(query_block * rows)
        high = self.doc_start(query_block * rows + rows - 1)
        visible = (key_block <= query_block) & (key_block * rows + rows - 1 >= low)
        whole = (key_block < query_block) & (key_block * rows >= high)
        return visible, whole

    def mask(self, query_block, key_block, query_dim):
        rows = self.half_rows
        query_pos = query_block * rows + lax.broadcasted_iota(jnp.int32, (rows, rows), query_dim)
        key_pos = key_block * rows + lax.broadcasted_iota(jnp.int32, (rows, rows), 1 - query_dim)
        return (key_pos <= query_pos) & (key_pos >= self.doc_start(query_pos))


def rope_rows(info, tables, half, head_dim):
    base_cos, base_sin, step_cos, step_sin = tables
    block = info.block(info.ctx, half)
    return block_tables(
        base_cos[pl.ds(block, 1), :],
        base_sin[pl.ds(block, 1), :],
        step_cos[...],
        step_sin[...],
        head_dim,
    )


def half_slice(half, rows):
    return slice(half * rows, half * rows + rows)


def twice(ref):
    row = ref[...]
    return jnp.concatenate([row] * (LANES // row.shape[1]), axis=1)


def project_kernel(devices, head_dim, block_ref, x_ref, doc_ref, gain_ref, wq_ref, wk_ref, wv_ref,
                   qg_ref, kg_ref, bc_ref, bs_ref, sc_ref, ss_ref,
                   kv_ref, q_ref, raw_ref, n1_ref, x_out, start_ref):
    rows = x_ref.shape[0] // 2
    start_ref[0] = 0
    for doc in range(1, DOCS):
        start_ref[doc] = jnp.sum((doc_ref[...] < doc).astype(jnp.int32))
    info = Info(block_ref, start_ref, devices, rows)
    tables = (bc_ref, bs_ref, sc_ref, ss_ref)
    query_gain, key_gain = twice(qg_ref), twice(kg_ref)
    chunks = wq_ref.shape[1] // LANES
    for half in range(2):
        here = half_slice(half, rows)
        from_row = pl.multiple_of(jnp.bitwise_xor(half, info.core) * rows, rows)
        x_low = x_ref[pl.ds(from_row, rows), :]
        x_out[here, :] = x_low
        normed = rms_norm(x_low.astype(F32), gain_ref[...]).astype(BF16)
        n1_ref[here, :] = normed
        cos, sin = rope_rows(info, tables, half, head_dim)

        def turned(raw, gain):
            unit = raw * lax.rsqrt(head_mean(raw * raw, head_dim) + EPS) * gain
            return unit * cos + swap_halves(unit, head_dim) * sin

        key_raw = matmul(normed, wk_ref[...])
        kv_ref[here, 0:LANES] = turned(key_raw, key_gain).astype(BF16)
        kv_ref[here, LANES : 2 * LANES] = matmul(normed, wv_ref[...]).astype(BF16)
        raw_ref[here, chunks * LANES : (chunks + 1) * LANES] = key_raw
        query_raw = matmul(normed, wq_ref[...])
        raw_ref[here, 0 : chunks * LANES] = query_raw
        for chunk in range(chunks):
            cols = slice(chunk * LANES, (chunk + 1) * LANES)
            q_ref[here, cols] = (turned(query_raw[:, cols], query_gain) * SCALE).astype(BF16)


def spread_heads(low, rows, half, head_dim, out_ref):
    here = half_slice(half, rows)
    groups = mix_low(low[here, 0:LANES], low[here, LANES : 2 * LANES], head_dim)
    lane = lane_index((rows, LANES))
    for kv in range(2):
        for group in range(2):
            at = (2 * kv + group) * rows
            out_ref[half, at : at + rows, :] = jnp.where(
                lane // head_dim == kv, groups[group].astype(F32), 0.0
            ).astype(BF16)


def join_heads(stacked, rows, head_dim):
    lane = lane_index((rows, LANES))
    groups = [
        jnp.where(
            lane < head_dim,
            stacked[group * rows : (group + 1) * rows],
            stacked[(2 + group) * rows : (3 + group) * rows],
        )
        for group in range(2)
    ]
    return mix_heads(groups[0], groups[1], head_dim)


def fetch(pairs_of_refs, sems):
    copies = [
        pltpu.make_async_copy(source, target, sems.at[at])
        for at, (source, target) in enumerate(pairs_of_refs)
    ]
    for copy in copies:
        copy.start()
    return copies


def attend_slots(info, first_slot, held, spread, total):
    rows = info.half_rows

    def one_key_block(step, carry):
        slot, key_half = step // 2, lax.rem(step, 2)
        key_block = info.block(info.slot_source(first_slot + slot), key_half)
        key_rows = pl.ds(pl.multiple_of(key_half * rows, rows), rows)
        for half in range(2):
            query_block = info.block(info.ctx, half)
            visible, whole = info.relation(query_block, key_block)

            def take(masked, half=half, query_block=query_block):
                keys = held[slot, key_rows, 0:LANES]
                values = jnp.concatenate(
                    [held[slot, key_rows, LANES : 2 * LANES], jnp.ones((rows, LANES), BF16)], axis=1
                )
                if masked:
                    allowed = info.mask(query_block, key_block, 0)
                    allowed = jnp.concatenate([allowed] * (FORWARD_ROWS // rows), axis=0)
                for part in range(4 * rows // FORWARD_ROWS):
                    at = slice(part * FORWARD_ROWS, (part + 1) * FORWARD_ROWS)
                    scores = contract(spread[half, at, :], keys, 1, 1)
                    if masked:
                        scores = jnp.where(allowed, scores, NEG)
                    weights = jnp.exp(scores).astype(BF16)
                    total[half, at, :] += matmul(weights, values)

            pl.when(visible & whole)(functools.partial(take, False))
            pl.when(visible & jnp.logical_not(whole))(functools.partial(take, True))
        return carry

    lax.fori_loop(0, 2 * held.shape[0], one_key_block, 0)


def attend_first_kernel(devices, head_dim, block_ref, start_ref, q_ref, *refs):
    count = devices // 2 + 1
    slots = refs[:count]
    total, spread, held, sems = refs[count:]
    rows = q_ref.shape[0] // 2
    info = Info(block_ref, start_ref, devices, rows)
    copies = fetch([(slots[at], held.at[at]) for at in range(count)], sems)
    q_low = q_ref[...]
    for half in range(2):
        spread_heads(q_low, rows, half, head_dim, spread)
    total[...] = jnp.zeros_like(total)
    for copy in copies:
        copy.wait()
    attend_slots(info, 0, held, spread, total)


def attend_second_kernel(devices, head_dim, block_ref, start_ref, spread, total_ref, wo_ref, *refs):
    count = devices // 2 - 1
    slots = refs[:count]
    o_ref, o32_ref, lse_ref, mine_ref, other_ref, held, total, sems = refs[count:]
    rows = o_ref.shape[0] // 2
    info = Info(block_ref, start_ref, devices, rows)
    copies = fetch(
        [(slots[at], held.at[at]) for at in range(count)] + [(total_ref, total)], sems
    )
    for copy in copies:
        copy.wait()
    attend_slots(info, devices - count, held, spread, total)
    for half in (1, 0):
        here = half_slice(half, rows)
        sums = total[half, :, LANES : 2 * LANES]
        chunks = join_heads(total[half, :, 0:LANES] / sums, rows, head_dim)
        for chunk in range(2):
            cols = slice(chunk * LANES, (chunk + 1) * LANES)
            o32_ref[here, cols] = chunks[chunk]
            o_ref[here, cols] = chunks[chunk].astype(BF16)
        lse_ref[half] = jnp.transpose(jnp.log(sums))[0:8, :]
        part = matmul(o_ref[here, :], wo_ref[...]).astype(BF16)
        (mine_ref, other_ref)[half][...] = part


def feed_kernel(x_ref, mine_ref, other_ref, gain_ref, wg_ref, wu_ref, dh_ref,
                mid_ref, n2_ref, hid_ref, dgate_ref, dup_ref, part_mine, part_other):
    rows = x_ref.shape[0] // 2
    hidden = wg_ref.shape[1]
    for half in range(2):
        here = half_slice(half, rows)
        middle = x_ref[here, :].astype(F32) + (mine_ref, other_ref)[half][...].astype(F32)
        mid_ref[here, :] = middle
        n2_ref[here, :] = rms_norm(middle, gain_ref[...]).astype(BF16)
    step = 2 * LANES
    for at in range(0, hidden, step):
        cols = slice(at, min(at + step, hidden))
        normed = n2_ref[...]
        gate = matmul(normed, wg_ref[:, cols])
        up = matmul(normed, wu_ref[:, cols])
        grad_hidden = dh_ref[:, cols]
        sigmoid = jax.nn.sigmoid(gate)
        silu = gate * sigmoid
        hid_ref[:, cols] = (silu * up).astype(BF16)
        dgate_ref[:, cols] = (
            grad_hidden * up * sigmoid * (1.0 + gate * (1.0 - sigmoid))
        ).astype(BF16)
        dup_ref[:, cols] = (grad_hidden * silu).astype(BF16)
    for half, part in ((1, part_other), (0, part_mine)):
        here = half_slice(half, rows)
        for at in range(0, wg_ref.shape[0], step):
            wide = slice(at, at + step)
            part[:, wide] = (
                contract(dgate_ref[here, :], wg_ref[wide, :], 1, 1)
                + contract(dup_ref[here, :], wu_ref[wide, :], 1, 1)
            ).astype(BF16)


def prepare_back(info, head_dim, q_ref, do_ref, o32_ref, spread, spread_do, delta):
    rows = info.half_rows
    q_low, do_low = q_ref[...], do_ref[...]
    for half in range(2):
        here = half_slice(half, rows)
        spread_heads(q_low, rows, half, head_dim, spread)
        spread_heads(do_low, rows, half, head_dim, spread_do)
        product = do_low[here, :].astype(F32) * o32_ref[here, :]
        for chunk in range(2):
            turned = jnp.transpose(product[:, chunk * LANES : (chunk + 1) * LANES])
            for group in range(2):
                at = (2 * chunk + group) * rows
                delta[half, :, at : at + rows] = jnp.broadcast_to(
                    jnp.sum(
                        turned[group * head_dim : (group + 1) * head_dim], axis=0, keepdims=True
                    ),
                    (8, rows),
                )


def back_slots(info, first_slot, held, spread, spread_do, lse_ref, delta, dq_t, dkv, out_ref):
    rows = info.half_rows

    def one_key_block(step, carry):
        slot, key_half = step // 2, lax.rem(step, 2)
        source = info.slot_source(first_slot + slot)
        key_block = info.block(source, key_half)
        key_rows = pl.ds(pl.multiple_of(key_half * rows, rows), rows)
        dkv[...] = jnp.zeros_like(dkv)
        for half in range(2):
            query_block = info.block(info.ctx, half)
            visible, whole = info.relation(query_block, key_block)

            def take(masked, half=half, query_block=query_block):
                keys = held[slot, key_rows, 0:LANES]
                values = held[slot, key_rows, LANES : 2 * LANES]
                if masked:
                    allowed = info.mask(query_block, key_block, 1)
                    allowed = jnp.concatenate([allowed] * (BACK_ROWS // rows), axis=1)
                for part in range(4 * rows // BACK_ROWS):
                    at = slice(part * BACK_ROWS, (part + 1) * BACK_ROWS)
                    queries, grads = spread[half, at, :], spread_do[half, at, :]
                    scores = contract(keys, queries, 1, 1) - lse_ref[half, 0:1, at]
                    if masked:
                        scores = jnp.where(allowed, scores, NEG)
                    probs = jnp.exp(scores)
                    grad_probs = contract(values, grads, 1, 1)
                    grad_scores = (probs * (grad_probs - delta[half, 0:1, at])).astype(BF16)
                    dkv[:, LANES : 2 * LANES] += matmul(probs.astype(BF16), grads)
                    dkv[:, 0:LANES] += matmul(grad_scores, queries)
                    dq_t[half, :, at] += contract(keys, grad_scores, 0, 0)

            pl.when(visible & whole)(functools.partial(take, False))
            pl.when(visible & jnp.logical_not(whole))(functools.partial(take, True))
        out_ref[source // 2, key_rows, :] = dkv[...].astype(BF16)
        return carry

    lax.fori_loop(0, 2 * held.shape[0], one_key_block, 0)


def back_first_kernel(devices, head_dim, wt_count, block_ref, start_ref, q_ref, o32_ref, lse_ref,
                      mid_ref, mine_ref, other_ref, c_ref, gain_ref, wo_ref, *refs):
    pairs = devices // 2
    slots = refs[:pairs]
    dkv_out, dq_t, dy_ref, dyb_ref, do_ref, ffn_gain = refs[pairs : pairs + 6]
    held, spread, spread_do, delta, dkv, sems = refs[pairs + 6 :]
    rows = q_ref.shape[0] // 2
    info = Info(block_ref, start_ref, devices, rows)
    copies = fetch([(slots[at], held.at[at]) for at in range(pairs)], sems)
    gain_sum = jnp.zeros((1, gain_ref.shape[1]), F32)
    for half in range(2):
        here = half_slice(half, rows)
        back, terms = norm_back(
            mid_ref[here, :], gain_ref[...], (mine_ref, other_ref)[half][...].astype(F32)
        )
        gain_sum += jnp.sum(terms, axis=0, keepdims=True)
        grad_middle = c_ref[here, :].astype(F32) + back
        dy_ref[here, :] = grad_middle
        dyb_ref[here, :] = grad_middle.astype(BF16)
        do_ref[here, :] = contract(dyb_ref[here, :], wo_ref[...], 1, 1).astype(BF16)
    ffn_gain[...] = gain_sum * (1.0 / wt_count)
    prepare_back(info, head_dim, q_ref, do_ref, o32_ref, spread, spread_do, delta)
    dq_t[...] = jnp.zeros_like(dq_t)
    for copy in copies:
        copy.wait()
    back_slots(info, pairs, held, spread, spread_do, lse_ref, delta, dq_t, dkv, dkv_out)


def back_second_kernel(devices, head_dim, block_ref, start_ref, q_ref, do_ref, o32_ref, lse_ref,
                       raw_ref, qg_ref, bc_ref, bs_ref, sc_ref, ss_ref, dq_in, *refs):
    pairs = devices // 2
    slots = refs[:pairs]
    dkv_out, dq_ref, gain_ref, held, spread, spread_do, delta, dq_t, dkv, sems = refs[pairs:]
    rows = q_ref.shape[0] // 2
    info = Info(block_ref, start_ref, devices, rows)
    copies = fetch([(slots[at], held.at[at]) for at in range(pairs)] + [(dq_in, dq_t)], sems)
    prepare_back(info, head_dim, q_ref, do_ref, o32_ref, spread, spread_do, delta)
    for copy in copies:
        copy.wait()
    back_slots(info, 0, held, spread, spread_do, lse_ref, delta, dq_t, dkv, dkv_out)
    query_gain = twice(qg_ref)
    gain_sum = jnp.zeros((1, LANES), F32)
    for half in range(2):
        here = half_slice(half, rows)
        cos, sin = rope_rows(info, (bc_ref, bs_ref, sc_ref, ss_ref), half, head_dim)
        chunks = join_heads(jnp.transpose(dq_t[half]), rows, head_dim)
        for chunk in range(2):
            cols = slice(chunk * LANES, (chunk + 1) * LANES)
            grad = chunks[chunk] * SCALE
            grad = grad * cos - swap_halves(grad, head_dim) * sin
            back, term = head_norm_back(raw_ref[here, cols], query_gain, grad, head_dim)
            dq_ref[here, cols] = back.astype(BF16)
            gain_sum += term
    gain_ref[...] = gain_sum


def key_back_kernel(devices, head_dim, count, block_ref, start_ref, raw_ref, kg_ref, bc_ref, bs_ref,
                    sc_ref, ss_ref, dq_ref, x_ref, wq_ref, wk_ref, wv_ref, ffn_gain, query_gain,
                    *refs):
    parts = refs[:count]
    dkv_ref, mine_ref, other_ref, gains_ref = refs[count:]
    rows = raw_ref.shape[0] // 2
    width = x_ref.shape[1]
    info = Info(block_ref, start_ref, devices, rows)
    key_gain = twice(kg_ref)
    key_sum = jnp.zeros((1, LANES), F32)
    attn_sum = jnp.zeros((1, width), F32)
    for half in (1, 0):
        here = half_slice(half, rows)
        grad = sum(part[here, :].astype(F32) for part in parts)
        cos, sin = rope_rows(info, (bc_ref, bs_ref, sc_ref, ss_ref), half, head_dim)
        grad_k = grad[:, 0:LANES]
        grad_k = grad_k * cos - swap_halves(grad_k, head_dim) * sin
        back, term = head_norm_back(raw_ref[here, 2 * LANES : 3 * LANES], key_gain, grad_k, head_dim)
        key_sum += term
        key_low, value_low = back.astype(BF16), grad[:, LANES : 2 * LANES].astype(BF16)
        dkv_ref[here, 0:LANES] = key_low
        dkv_ref[here, LANES : 2 * LANES] = value_low
        part = (
            contract(dq_ref[here, :], wq_ref[...], 1, 1)
            + contract(key_low, wk_ref[...], 1, 1)
            + contract(value_low, wv_ref[...], 1, 1)
        )
        (mine_ref, other_ref)[half][...] = part.astype(BF16)
        inputs = x_ref[here, :].astype(F32)
        inverse = lax.rsqrt(jnp.mean(inputs * inputs, axis=-1, keepdims=True) + EPS)
        attn_sum += jnp.sum(part * inputs * inverse, axis=0, keepdims=True)
    gains_ref[:, 0:width] = attn_sum
    gains_ref[:, width : 2 * width] = ffn_gain[...]
    gains_ref[:, 2 * width : 2 * width + LANES] = query_gain[...]
    gains_ref[:, 2 * width + LANES : 2 * width + 2 * LANES] = key_sum


def finish_kernel(x_ref, mine_ref, other_ref, gain_ref, dy_ref, out_ref):
    rows = x_ref.shape[0] // 2
    core = lax.rem(lax.axis_index("wt"), 2)
    for half in range(2):
        here = half_slice(half, rows)
        back, _ = norm_back(
            x_ref[here, :].astype(F32), gain_ref[...], (mine_ref, other_ref)[half][...].astype(F32)
        )
        to_row = pl.multiple_of(jnp.bitwise_xor(half, core) * rows, rows)
        out_ref[pl.ds(to_row, rows), :] = dy_ref[here, :] + back


def put_shard(kept, sent, bit, device, rows, cols, piece):
    index = device // (2 << bit) * (1 << bit) + device % (1 << bit)
    same = lax.rem(lax.axis_index("ctx") // (1 << bit), 2) == device // (1 << bit) % 2

    @pl.when(same)
    def _():
        kept[index, rows, cols] = piece

    @pl.when(jnp.logical_not(same))
    def _():
        sent[index, rows, cols] = piece


def put_rows(kept, sent, bit, shard, row, cols, block):
    for part in range(block.shape[0] // shard):
        piece = block[part * shard : (part + 1) * shard]
        put_shard(kept, sent, bit, row // shard + part, slice(0, shard), cols, piece)


def feed_grad_kernel(per_step, c_ref, n2_ref, hid_ref, dgate_ref, dup_ref, wd_ref, *refs):
    mine_ref, other_ref, y_kept, y_sent, z_kept, z_sent = refs[-6:]
    rows = c_ref.shape[0] // 2
    hidden = hid_ref.shape[1]
    shard, first = y_kept.shape[1:]
    gate_end = z_kept.shape[2]
    gate_at = 2 * hidden - first
    begin = pl.program_id(0) * per_step
    ctx = lax.axis_index("ctx")

    def put(kept, sent, bit, cols, block):
        for part in range(per_step):
            index = part // (2 << bit) * (1 << bit) + part % (1 << bit)
            side = lax.rem((begin + part) // (1 << bit), 2)
            same = lax.rem(ctx // (1 << bit), 2) == side
            piece = block[part * shard : (part + 1) * shard]

            @pl.when(same)
            def _():
                kept[index, :, cols] = piece

            @pl.when(jnp.logical_not(same))
            def _():
                sent[index, :, cols] = piece

    for half, out in ((1, other_ref), (0, mine_ref)):
        out[...] = matmul(hid_ref[half_slice(half, rows), :], wd_ref[...]).astype(BF16)
    turned = jnp.transpose(n2_ref[...])
    block = matmul(turned, dup_ref[...]).astype(BF16)
    put(y_kept, y_sent, 0, slice(0, first), block[:, :first])
    put(z_kept, z_sent, 1, slice(hidden, gate_at), block[:, first:])
    block = matmul(turned, dgate_ref[:, : gate_end - gate_at]).astype(BF16)
    put(z_kept, z_sent, 1, slice(gate_at, gate_end), block)
    block = matmul(jnp.transpose(c_ref[...]), hid_ref[...]).astype(BF16)
    put(z_kept, z_sent, 1, slice(0, hidden), block)


def feed_grads(out_grad, normed, hidden, grad_gate, grad_up, w_down, y_width, z_width, after):
    tok_rows, width = out_grad.shape
    devices = lax.axis_size("ctx")
    shard = width // devices
    step = 2 * LANES
    per_step = step // shard
    pairs = devices // 2
    whole = pl.BlockSpec(hidden.shape, lambda i: (0, 0))
    columns = pl.BlockSpec((tok_rows, step), lambda i: (0, i))
    out = pl.BlockSpec((tok_rows // 2, step), lambda i: (0, i))
    y_spec = pl.BlockSpec((per_step // 2, shard, y_width), lambda i: (i, 0, 0))
    if per_step == 2:
        z_spec = pl.BlockSpec((2, shard, z_width), lambda i: (i // 2, 0, 0))
    else:
        z_spec = pl.BlockSpec((per_step // 2, shard, z_width), lambda i: (i, 0, 0))
    half_low = jax.ShapeDtypeStruct((tok_rows // 2, width), BF16)
    y_shape = jax.ShapeDtypeStruct((pairs, shard, y_width), BF16)
    z_shape = jax.ShapeDtypeStruct((pairs, shard, z_width), BF16)
    return pl.pallas_call(
        functools.partial(feed_grad_kernel, per_step),
        grid=(width // step,),
        out_shape=[half_low, half_low, y_shape, y_shape, z_shape, z_shape],
        in_specs=[columns, columns, whole, whole, whole]
        + [pl.BlockSpec((w_down.shape[0], step), lambda i: (0, i))]
        + [pl.BlockSpec(memory_space=pl.ANY)] * len(after),
        out_specs=[out, out, y_spec, y_spec, z_spec, z_spec],
        compiler_params=pltpu.CompilerParams(vmem_limit_bytes=VMEM_LIMIT),
        cost_estimate=pl.CostEstimate(flops=14 * 10**9, bytes_accessed=0, transcendentals=0),
    )(out_grad, normed, hidden, grad_gate, grad_up, w_down, *after)


def narrow_grad_kernel(devices, skips, *refs):
    kept, sent = refs[-2:]
    count = len(skips)
    width = refs[0].shape[1]
    shard = width // devices
    begin = 0
    if len(refs) > 2 * count + 2:
        gains = refs[2 * count][...]
        for device in range(devices):
            at = device * shard
            blank = [jnp.zeros((1, LANES - shard), F32)] if shard < LANES else []
            first = [gains[:, at : at + shard]] + blank
            second = [gains[:, width + at : width + at + shard]] + blank
            block = jnp.concatenate(
                [
                    jnp.concatenate(first + second, axis=1),
                    gains[:, 2 * width : 2 * width + 2 * LANES],
                    jnp.zeros((GAIN_ROWS - 2, 2 * LANES), F32),
                ],
                axis=0,
            ).astype(BF16)
            put_shard(
                kept, sent, 0, device, slice(shard, shard + GAIN_ROWS), slice(0, 2 * LANES), block
            )
    step = 2 * LANES
    for at in range(count):
        left, right = refs[2 * at], refs[2 * at + 1]
        cols = slice(begin, begin + right.shape[1] - skips[at])
        begin = cols.stop
        for row in range(0, width, step):
            block = matmul(jnp.transpose(left[:, row : row + step]), right[:, skips[at] :])
            block = block.astype(BF16)
            put_rows(kept, sent, 0, shard, row, cols, block)


def call_kernel(body, outs, operands, memory, scratch=(), flops=1000, after=()):
    kinds = {
        "s": pl.BlockSpec(memory_space=pltpu.SMEM),
        "v": pl.BlockSpec(memory_space=pltpu.VMEM),
        "a": pl.BlockSpec(memory_space=pl.ANY),
    }
    count = len(operands)

    def whole(*refs):
        body(*refs[:count], *refs[count + len(after) :])

    return pl.pallas_call(
        whole,
        out_shape=[jax.ShapeDtypeStruct(shape, kind) for shape, kind, *_ in outs],
        in_specs=[kinds[m] for m in memory] + [kinds["a"]] * len(after),
        out_specs=[kinds[out[2] if len(out) > 2 else "v"] for out in outs],
        scratch_shapes=list(scratch),
        compiler_params=pltpu.CompilerParams(vmem_limit_bytes=VMEM_LIMIT),
        cost_estimate=pl.CostEstimate(flops=flops, bytes_accessed=0, transcendentals=0),
    )(*operands, *after)


def hold(values, after):
    return pl.pallas_call(
        lambda *refs: None,
        out_shape=jax.ShapeDtypeStruct(values.shape, values.dtype),
        in_specs=[pl.BlockSpec(memory_space=pl.ANY)] * (1 + len(after)),
        out_specs=pl.BlockSpec(memory_space=pl.ANY),
        input_output_aliases={0: 0},
        cost_estimate=pl.CostEstimate(flops=0, bytes_accessed=0, transcendentals=0),
    )(values, *after)


def flip(values, axis, bit):
    size = lax.axis_size(axis)
    return lax.ppermute(values, axis, [(i, i ^ bit) for i in range(size)])


def shift(values, step):
    size = lax.axis_size("ctx")
    return lax.ppermute(values, "ctx", [(i, (i + step) % size) for i in range(size)])


def gather_slots(values):
    pairs = lax.axis_size("ctx") // 2
    same = [values] + [shift(values, 2 * k) for k in range(1, pairs)]
    return same, [flip(part, "ctx", 1) for part in same]


def chip_sum(mine, other):
    return (mine.astype(F32) + flip(other, "wt", 1).astype(F32)).astype(BF16)


def slice_sum(chip):
    whole = (chip.astype(F32) + flip(chip, "wt", 2).astype(F32)).astype(BF16)
    return whole, flip(whole, "wt", 1)


def halve(kept, received, bits, bit):
    after = len([b for b in bits if b < bit])
    view = (-1, 2, 1 << after) + kept.shape[1:]
    kept, received = kept.reshape(view), received.reshape(view)
    side = (lax.axis_index("ctx") // (1 << bit)) % 2

    def pick(at):
        picked = lax.dynamic_index_in_dim(kept, at, 1, keepdims=False).astype(
            F32
        ) + lax.dynamic_index_in_dim(received, at, 1, keepdims=False).astype(F32)
        return picked.astype(BF16).reshape((-1,) + view[3:])

    return pick(side), pick(1 - side)


def last_sum(kept, received):
    return kept[0].astype(F32) + received[0].astype(F32)


def ctx_bits():
    return range(lax.axis_size("ctx").bit_length() - 1)


def scatter_tail(kept, received, bits):
    bits = list(bits)
    sends = []
    for bit in list(bits):
        kept, sent = halve(kept, received, bits, bit)
        bits.remove(bit)
        sends.append(sent)
        received = flip(sent, "ctx", 1 << bit)
    return last_sum(kept, received), sends


def scatter_tail_from(kept, received, bits):
    if len(bits) == 1:
        return last_sum(kept, received), []
    return scatter_tail(kept, received, bits[1:])


def scatter_rest(kept, received, first, waits=()):
    bits = [bit for bit in ctx_bits() if bit != first]
    sends = []
    for step, bit in enumerate(list(bits)):
        if step < len(waits):
            kept = hold(kept, waits[step])
        kept, sent = halve(kept, received, bits, bit)
        bits.remove(bit)
        sends.append(sent)
        received = flip(sent, "ctx", 1 << bit)
    return last_sum(kept, received), sends


def on_device(
    block_in,
    doc_ids,
    block_of,
    w_query,
    w_key,
    w_value,
    w_out,
    w_gate,
    w_up,
    w_down,
    attn_gain,
    ffn_gain,
    query_gain,
    key_gain,
    cotangent,
):
    tok_rows, width = block_in.shape
    half_rows = tok_rows // 2
    head_dim = query_gain.shape[0]
    q_width, kv_width = w_query.shape[1], w_key.shape[1]
    hidden_width = w_gate.shape[1]
    devices = lax.axis_size("ctx")
    pairs = devices // 2
    blocks = block_of.shape[0]
    wt_count = lax.axis_size("wt")
    ctx = lax.axis_index("ctx")
    core = lax.axis_index("wt") % 2
    mine, other = slice(0, half_rows), slice(half_rows, tok_rows)

    half_dim = head_dim // 2
    freqs = THETA ** (-2.0 * (np.arange(LANES) % half_dim).astype(np.float64) / head_dim)
    base_angle = (np.arange(blocks) * half_rows)[:, None] * freqs[None, :]
    step_angle = np.arange(half_rows)[:, None] * freqs[None, :]
    tables = [
        jnp.asarray(table.astype(np.float32))
        for table in (np.cos(base_angle), np.sin(base_angle), np.cos(step_angle), np.sin(step_angle))
    ]
    attn_gain_row, ffn_gain_row = attn_gain[None, :], ffn_gain[None, :]
    query_gain_row, key_gain_row = query_gain[None, :], key_gain[None, :]
    stacked = 4 * half_rows
    half_low = ((half_rows, width), BF16)
    held = pltpu.VMEM((pairs, tok_rows, 2 * kv_width), BF16)
    spread = pltpu.VMEM((2, stacked, LANES), BF16)

    key_value, query, raw, normed_one, x_local, starts = call_kernel(
        functools.partial(project_kernel, devices, head_dim),
        [
            ((tok_rows, 2 * kv_width), BF16),
            ((tok_rows, q_width), BF16),
            ((tok_rows, q_width + kv_width), F32),
            ((tok_rows, width), BF16),
            ((tok_rows, width), BF16),
            ((DOCS,), jnp.int32, "s"),
        ],
        [
            block_of,
            block_in,
            doc_ids.reshape(-1, LANES),
            attn_gain_row,
            w_query,
            w_key,
            w_value,
            query_gain_row,
            key_gain_row,
        ]
        + tables,
        "s" + "v" * 12,
    )
    place = [block_of, starts]
    same_slots, other_slots = gather_slots(key_value)

    out_grad = jnp.where(core == 0, cotangent, jnp.roll(cotangent, half_rows, 0))
    grad_hidden = contract(out_grad, w_down, 1, 1)

    total, spread_query = call_kernel(
        functools.partial(attend_first_kernel, devices, head_dim),
        [((2, stacked, 2 * LANES), F32), ((2, stacked, LANES), BF16)],
        place + [query] + same_slots + other_slots[:1],
        "ssv" + "a" * (pairs + 1),
        [
            pltpu.VMEM((pairs + 1, tok_rows, 2 * kv_width), BF16),
            pltpu.SemaphoreType.DMA((pairs + 1,)),
        ],
        after=[grad_hidden],
    )
    out_low, out_wide, log_total, attn_mine, attn_other = call_kernel(
        functools.partial(attend_second_kernel, devices, head_dim),
        [
            ((tok_rows, q_width), BF16),
            ((tok_rows, q_width), F32),
            ((2, 8, stacked), F32),
            half_low,
            half_low,
        ],
        place + [spread_query, total, w_out] + other_slots[1:],
        "ssvav" + "a" * (pairs - 1),
        [
            pltpu.VMEM((pairs - 1, tok_rows, 2 * kv_width), BF16),
            pltpu.VMEM((2, stacked, 2 * LANES), F32),
            pltpu.SemaphoreType.DMA((pairs,)),
        ],
    )
    attn_mine, attn_other = slice_sum(chip_sum(attn_mine, attn_other))

    middle, normed_two, hidden, grad_gate, grad_upper, part_mine, part_other = call_kernel(
        feed_kernel,
        [
            ((tok_rows, width), F32),
            ((tok_rows, width), BF16),
            ((tok_rows, hidden_width), BF16),
            ((tok_rows, hidden_width), BF16),
            ((tok_rows, hidden_width), BF16),
            half_low,
            half_low,
        ],
        [x_local, attn_mine, attn_other, ffn_gain_row, w_gate, w_up, grad_hidden],
        "v" * 7,
    )
    chip = chip_sum(part_mine, part_other)
    n2_mine, n2_other = slice_sum(chip)

    shard = width // devices
    y_width = hidden_width * 7 // 9 // LANES * LANES
    gate_cut = hidden_width // 3 // LANES * LANES
    gate_at = 2 * hidden_width - y_width
    z_width = gate_at + gate_cut
    ffn_mine, ffn_other, y_kept, y_sent, z_kept, z_sent = feed_grads(
        out_grad, normed_two, hidden, grad_gate, grad_upper, w_down, y_width, z_width, [chip]
    )
    ffn_chip = hold(chip_sum(ffn_mine, ffn_other), [n2_mine])
    y_received = flip(y_sent, "ctx", 1)
    z_received = flip(z_sent, "ctx", 2)

    grad_other, grad_query_t, grad_middle, grad_middle_low, grad_attended, ffn_gain_part = (
        call_kernel(
            functools.partial(back_first_kernel, devices, head_dim, wt_count),
            [
                ((pairs, tok_rows, 2 * kv_width), BF16),
                ((2, LANES, stacked), F32),
                ((tok_rows, width), F32),
                ((tok_rows, width), BF16),
                ((tok_rows, q_width), BF16),
                ((1, width), F32),
            ],
            place
            + [query, out_wide, log_total, middle, n2_mine, n2_other, out_grad, ffn_gain_row, w_out]
            + other_slots,
            "ss" + "v" * 9 + "a" * pairs,
            [
                held,
                spread,
                spread,
                pltpu.VMEM((2, 8, stacked), F32),
                pltpu.VMEM((half_rows, 2 * LANES), F32),
                pltpu.SemaphoreType.DMA((pairs,)),
            ],
            after=[ffn_chip],
            )
    )
    ffn_mine, ffn_other = slice_sum(ffn_chip)
    grad_same, query_raw_low, query_gain_sum = call_kernel(
        functools.partial(back_second_kernel, devices, head_dim),
        [
            ((pairs, tok_rows, 2 * kv_width), BF16),
            ((tok_rows, q_width), BF16),
            ((1, LANES), F32),
        ],
        place
        + [query, grad_attended, out_wide, log_total, raw, query_gain_row]
        + tables
        + [grad_query_t]
        + same_slots,
        "ss" + "v" * 10 + "a" * (1 + pairs),
        [
            held,
            spread,
            spread,
            pltpu.VMEM((2, 8, stacked), F32),
            pltpu.VMEM((2, LANES, stacked), F32),
            pltpu.VMEM((half_rows, 2 * LANES), F32),
            pltpu.SemaphoreType.DMA((pairs + 1,)),
        ],
        after=[ffn_mine],
    )
    bits = list(ctx_bits())
    key_value_received = flip(grad_other, "ctx", 1)
    y_kept, y_sent = halve(hold(y_kept, [grad_same]), y_received, bits[1:], 1)
    y_received = flip(y_sent, "ctx", 2)
    first_kept, first_sent = call_kernel(
        functools.partial(narrow_grad_kernel, devices, (gate_cut, 0, 0)),
        [((pairs, shard, hidden_width - gate_cut + 2 * q_width), BF16)] * 2,
        [normed_two, grad_gate, normed_one, query_raw_low, grad_middle_low, out_low],
        "v" * 6,
        after=[y_sent],
    )
    z_kept, z_sent = halve(hold(z_kept, [first_sent]), z_received, bits[:1] + bits[2:], 0)
    z_received = flip(z_sent, "ctx", 1)
    key_value_kept = hold(grad_same, [z_sent])
    key_value_sends = []
    rest = bits[1:]
    for bit in bits[1:]:
        key_value_kept, sent = halve(key_value_kept, key_value_received, rest, bit)
        rest.remove(bit)
        key_value_received = flip(sent, "ctx", 1 << bit)
        key_value_sends.append(sent)
    first_received = flip(hold(first_sent, key_value_sends[:1]), "ctx", 1)
    z_kept, z_sent = halve(hold(z_kept, key_value_sends[1:2]), z_received, bits[2:], bits[2])
    z_received = flip(z_sent, "ctx", 1 << bits[2])
    y_total, _ = scatter_tail(hold(y_kept, key_value_sends[:1]), y_received, bits[2:])

    grad_key_value_low, part_mine, part_other, gains = call_kernel(
        functools.partial(key_back_kernel, devices, head_dim, 2),
        [
            ((tok_rows, 2 * kv_width), BF16),
            half_low,
            half_low,
            ((1, 2 * width + 2 * LANES), F32),
        ],
        place
        + [raw, key_gain_row]
        + tables
        + [query_raw_low, x_local, w_query, w_key, w_value, ffn_gain_part, query_gain_sum]
        + [key_value_kept[0], key_value_received[0]],
        "ss" + "v" * 15,
        after=[y_total, z_sent],
    )
    n1_chip = chip_sum(part_mine, part_other)
    n1_received = flip(n1_chip, "wt", 2)

    second_kept, second_sent = call_kernel(
        functools.partial(narrow_grad_kernel, devices, (0,)),
        [((pairs, shard + GAIN_ROWS, 2 * kv_width), BF16)] * 2,
        [normed_one, grad_key_value_low, gains],
        "v" * 3,
        after=[n1_chip],
    )
    first_kept, first_sent = halve(hold(first_kept, [second_sent]), first_received, bits[1:], 1)
    first_received = flip(first_sent, "ctx", 2)
    n1_mine = (hold(n1_chip, [first_sent]).astype(F32) + n1_received.astype(F32)).astype(BF16)
    n1_other = flip(n1_mine, "wt", 1)
    second_kept, second_sent = halve(
        hold(second_kept, [n1_mine]), flip(second_sent, "ctx", 1), bits[1:], 1
    )
    second_received = flip(second_sent, "ctx", 2)
    (grad_input,) = call_kernel(
        finish_kernel,
        [((tok_rows, width), F32)],
        [x_local, n1_mine, n1_other, attn_gain_row, grad_middle],
        "v" * 5,
        after=[second_sent],
    )
    first, first_sends = scatter_tail(hold(first_kept, [grad_input]), first_received, bits[2:])
    second, second_sends = scatter_tail(
        hold(second_kept, first_sends[-1:]), second_received, bits[2:]
    )
    z_total, _ = scatter_tail_from(hold(z_kept, second_sends[-1:]), z_received, bits[2:])
    gain_rows = second[shard : shard + 2]
    gain_rows = sum([flip(gain_rows, "wt", other_wt) for other_wt in range(1, wt_count)], gain_rows)

    def head_gain(at):
        row = jnp.sum(gain_rows[1, at * LANES : (at + 1) * LANES].reshape(-1, head_dim), axis=0)
        return lax.dynamic_slice_in_dim(row, ctx * (head_dim // devices), head_dim // devices)

    gate_rest = hidden_width - gate_cut
    ffn_mine = hold(ffn_mine, [n1_mine])
    out_mine = (middle[mine] + ffn_mine.astype(F32)).astype(BF16)
    out_other = (middle[other] + ffn_other.astype(F32)).astype(BF16)
    return (
        jnp.concatenate(
            [jnp.where(core == 0, out_mine, out_other), jnp.where(core == 0, out_other, out_mine)],
            axis=0,
        ),
        grad_input,
        first[:, gate_rest : gate_rest + q_width],
        second[:shard, :kv_width],
        second[:shard, kv_width:],
        first[:, gate_rest + q_width :].T,
        jnp.concatenate([z_total[:, gate_at:], first[:, :gate_rest]], axis=1),
        jnp.concatenate([y_total, z_total[:, hidden_width:gate_at]], axis=1),
        z_total[:, :hidden_width].T,
        gain_rows[0, :shard],
        gain_rows[0, LANES : LANES + shard],
        head_gain(0),
        head_gain(1),
    )


def solution(mesh):
    in_specs = (
        P("ctx", None),
        P(),
        P(),
        P(None, "wt"),
        P(None, "wt"),
        P(None, "wt"),
        P("wt", None),
        P(None, "wt"),
        P(None, "wt"),
        P("wt", None),
        P(),
        P(),
        P(),
        P(),
        P("ctx", None),
    )
    out_specs = (
        P("ctx", None),
        P("ctx", None),
        P("ctx", "wt"),
        P("ctx", "wt"),
        P("ctx", "wt"),
        P("wt", "ctx"),
        P("ctx", "wt"),
        P("ctx", "wt"),
        P("wt", "ctx"),
        P("ctx"),
        P("ctx"),
        P("ctx"),
        P("ctx"),
    )
    return jax.shard_map(
        on_device, mesh=mesh, in_specs=in_specs, out_specs=out_specs, check_vma=False
    )
```

```python
import functools

import jax
import jax.numpy as jnp
import numpy as np
from jax import lax
from jax.experimental import pallas as pl
from jax.experimental.pallas import tpu as pltpu
from jax.sharding import PartitionSpec as P

EPS = 1e-05
THETA = 1000000.0
NEG = -1e30
SCALE = 0.125
LANES = 128
DOCS = 4
FORWARD_ROWS = 512
BACK_ROWS = 512
GAIN_ROWS = 16
VMEM_LIMIT = 60 * 1024 * 1024
F32 = jnp.float32
BF16 = jnp.bfloat16


def matmul(left, right):
    return jnp.dot(left, right, preferred_element_type=F32)


def contract(left, right, left_dim, right_dim):
    return lax.dot_general(
        left, right, (((left_dim,), (right_dim,)), ((), ())), preferred_element_type=F32
    )


def rms_norm(vector, gain):
    return vector * lax.rsqrt(jnp.mean(vector * vector, axis=-1, keepdims=True) + EPS) * gain


def norm_back(vector, gain, gradient):
    inverse = lax.rsqrt(jnp.mean(vector * vector, axis=-1, keepdims=True) + EPS)
    scaled = gradient * gain
    back = inverse * scaled - vector * inverse**3 * jnp.mean(
        scaled * vector, axis=-1, keepdims=True
    )
    return (back, gradient * vector * inverse)


def lane_index(shape):
    return lax.broadcasted_iota(jnp.int32, shape, len(shape) - 1)


def head_mean(values, head_dim):
    row_id = lax.broadcasted_iota(jnp.int32, (LANES, LANES), 0) // head_dim
    col_id = lax.broadcasted_iota(jnp.int32, (LANES, LANES), 1) // head_dim
    ones = (row_id == col_id).astype(BF16)
    high = values.astype(BF16)
    low = (values - high.astype(F32)).astype(BF16)
    return (matmul(high, ones) + matmul(low, ones)) * (1.0 / head_dim)


def swap_halves(values, head_dim):
    half = head_dim // 2
    lane = lane_index(values.shape)
    return jnp.where(
        lane % head_dim < half,
        pltpu.roll(values, LANES - half, 1),
        pltpu.roll(values, half, 1),
    )


def mix_heads(first, second, head_dim):
    lane = lane_index(first.shape)
    return (
        jnp.where(lane < head_dim, first, pltpu.roll(second, head_dim, 1)),
        jnp.where(lane < head_dim, pltpu.roll(first, head_dim, 1), second),
    )


def mix_low(first, second, head_dim):
    one, two = mix_heads(first.astype(F32), second.astype(F32), head_dim)
    return one.astype(BF16), two.astype(BF16)


def block_tables(base_cos, base_sin, step_cos, step_sin, head_dim):
    cos = base_cos * step_cos - base_sin * step_sin
    sin = base_sin * step_cos + base_cos * step_sin
    lane = lane_index(cos.shape)
    return cos, jnp.where(lane % head_dim < head_dim // 2, -sin, sin)


def head_norm_back(raw, gain, gradient, head_dim):
    inverse = lax.rsqrt(head_mean(raw * raw, head_dim) + EPS)
    scaled = gradient * gain
    back = inverse * scaled - raw * inverse**3 * head_mean(scaled * raw, head_dim)
    return back, jnp.sum(gradient * raw * inverse, axis=0, keepdims=True)


class Info:
    def __init__(self, block_ref, start_ref, devices, half_rows):
        self.block_ref, self.start_ref = block_ref, start_ref
        self.devices, self.half_rows = devices, half_rows
        self.ctx, self.core = lax.axis_index("ctx"), lax.rem(lax.axis_index("wt"), 2)

    def block(self, source, half):
        return self.block_ref[2 * source + jnp.bitwise_xor(half, self.core)]

    def slot_source(self, slot):
        pairs = self.devices // 2
        same = slot < pairs
        column = jnp.where(same, self.ctx, jnp.bitwise_xor(self.ctx, 1))
        step = jnp.where(same, slot, slot - pairs)
        return lax.rem(column - 2 * step + self.devices, self.devices)

    def doc_start(self, position):
        start = jnp.zeros_like(position)
        for doc in range(1, DOCS):
            first = self.start_ref[doc]
            start = jnp.where(position >= first, first, start)
        return start

    def relation(self, query_block, key_block):
        rows = self.half_rows
        low = self.doc_start(query_block * rows)
        high = self.doc_start(query_block * rows + rows - 1)
        visible = (key_block <= query_block) & (key_block * rows + rows - 1 >= low)
        whole = (key_block < query_block) & (key_block * rows >= high)
        return visible, whole

    def mask(self, query_block, key_block, query_dim):
        rows = self.half_rows
        query_pos = query_block * rows + lax.broadcasted_iota(jnp.int32, (rows, rows), query_dim)
        key_pos = key_block * rows + lax.broadcasted_iota(jnp.int32, (rows, rows), 1 - query_dim)
        return (key_pos <= query_pos) & (key_pos >= self.doc_start(query_pos))


def rope_rows(info, tables, half, head_dim):
    base_cos, base_sin, step_cos, step_sin = tables
    block = info.block(info.ctx, half)
    return block_tables(
        base_cos[pl.ds(block, 1), :],
        base_sin[pl.ds(block, 1), :],
        step_cos[...],
        step_sin[...],
        head_dim,
    )


def half_slice(half, rows):
    return slice(half * rows, half * rows + rows)


def twice(ref):
    row = ref[...]
    return jnp.concatenate([row] * (LANES // row.shape[1]), axis=1)


def project_kernel(devices, head_dim, block_ref, x_ref, doc_ref, gain_ref, wq_ref, wk_ref, wv_ref,
                   qg_ref, kg_ref, bc_ref, bs_ref, sc_ref, ss_ref,
                   kv_ref, q_ref, raw_ref, n1_ref, x_out, start_ref):
    rows = x_ref.shape[0] // 2
    start_ref[0] = 0
    for doc in range(1, DOCS):
        start_ref[doc] = jnp.sum((doc_ref[...] < doc).astype(jnp.int32))
    info = Info(block_ref, start_ref, devices, rows)
    tables = (bc_ref, bs_ref, sc_ref, ss_ref)
    query_gain, key_gain = twice(qg_ref), twice(kg_ref)
    chunks = wq_ref.shape[1] // LANES
    for half in range(2):
        here = half_slice(half, rows)
        from_row = pl.multiple_of(jnp.bitwise_xor(half, info.core) * rows, rows)
        x_low = x_ref[pl.ds(from_row, rows), :]
        x_out[here, :] = x_low
        normed = rms_norm(x_low.astype(F32), gain_ref[...]).astype(BF16)
        n1_ref[here, :] = normed
        cos, sin = rope_rows(info, tables, half, head_dim)

        def turned(raw, gain):
            unit = raw * lax.rsqrt(head_mean(raw * raw, head_dim) + EPS) * gain
            return unit * cos + swap_halves(unit, head_dim) * sin

        key_raw = matmul(normed, wk_ref[...])
        kv_ref[here, 0:LANES] = turned(key_raw, key_gain).astype(BF16)
        kv_ref[here, LANES : 2 * LANES] = matmul(normed, wv_ref[...]).astype(BF16)
        raw_ref[here, chunks * LANES : (chunks + 1) * LANES] = key_raw
        query_raw = matmul(normed, wq_ref[...])
        raw_ref[here, 0 : chunks * LANES] = query_raw
        for chunk in range(chunks):
            cols = slice(chunk * LANES, (chunk + 1) * LANES)
            q_ref[here, cols] = (turned(query_raw[:, cols], query_gain) * SCALE).astype(BF16)


def spread_heads(low, rows, half, head_dim, out_ref):
    here = half_slice(half, rows)
    groups = mix_low(low[here, 0:LANES], low[here, LANES : 2 * LANES], head_dim)
    lane = lane_index((rows, LANES))
    for kv in range(2):
        for group in range(2):
            at = (2 * kv + group) * rows
            out_ref[half, at : at + rows, :] = jnp.where(
                lane // head_dim == kv, groups[group].astype(F32), 0.0
            ).astype(BF16)


def join_heads(stacked, rows, head_dim):
    lane = lane_index((rows, LANES))
    groups = [
        jnp.where(
            lane < head_dim,
            stacked[group * rows : (group + 1) * rows],
            stacked[(2 + group) * rows : (3 + group) * rows],
        )
        for group in range(2)
    ]
    return mix_heads(groups[0], groups[1], head_dim)


def fetch(pairs_of_refs, sems):
    copies = [
        pltpu.make_async_copy(source, target, sems.at[at])
        for at, (source, target) in enumerate(pairs_of_refs)
    ]
    for copy in copies:
        copy.start()
    return copies


def attend_slots(info, first_slot, held, spread, total):
    rows = info.half_rows

    def one_key_block(step, carry):
        slot, key_half = step // 2, lax.rem(step, 2)
        key_block = info.block(info.slot_source(first_slot + slot), key_half)
        key_rows = pl.ds(pl.multiple_of(key_half * rows, rows), rows)
        for half in range(2):
            query_block = info.block(info.ctx, half)
            visible, whole = info.relation(query_block, key_block)

            def take(masked, half=half, query_block=query_block):
                keys = held[slot, key_rows, 0:LANES]
                values = jnp.concatenate(
                    [held[slot, key_rows, LANES : 2 * LANES], jnp.ones((rows, LANES), BF16)], axis=1
                )
                if masked:
                    allowed = info.mask(query_block, key_block, 0)
                    allowed = jnp.concatenate([allowed] * (FORWARD_ROWS // rows), axis=0)
                for part in range(4 * rows // FORWARD_ROWS):
                    at = slice(part * FORWARD_ROWS, (part + 1) * FORWARD_ROWS)
                    scores = contract(spread[half, at, :], keys, 1, 1)
                    if masked:
                        scores = jnp.where(allowed, scores, NEG)
                    weights = jnp.exp(scores).astype(BF16)
                    total[half, at, :] += matmul(weights, values)

            pl.when(visible & whole)(functools.partial(take, False))
            pl.when(visible & jnp.logical_not(whole))(functools.partial(take, True))
        return carry

    lax.fori_loop(0, 2 * held.shape[0], one_key_block, 0)


def attend_first_kernel(devices, head_dim, block_ref, start_ref, q_ref, *refs):
    count = devices // 2 + 1
    slots = refs[:count]
    total, spread, held, sems = refs[count:]
    rows = q_ref.shape[0] // 2
    info = Info(block_ref, start_ref, devices, rows)
    copies = fetch([(slots[at], held.at[at]) for at in range(count)], sems)
    q_low = q_ref[...]
    for half in range(2):
        spread_heads(q_low, rows, half, head_dim, spread)
    total[...] = jnp.zeros_like(total)
    for copy in copies:
        copy.wait()
    attend_slots(info, 0, held, spread, total)


def attend_second_kernel(devices, head_dim, block_ref, start_ref, spread, total_ref, wo_ref, *refs):
    count = devices // 2 - 1
    slots = refs[:count]
    o_ref, o32_ref, lse_ref, mine_ref, other_ref, held, total, sems = refs[count:]
    rows = o_ref.shape[0] // 2
    info = Info(block_ref, start_ref, devices, rows)
    copies = fetch(
        [(slots[at], held.at[at]) for at in range(count)] + [(total_ref, total)], sems
    )
    for copy in copies:
        copy.wait()
    attend_slots(info, devices - count, held, spread, total)
    for half in (1, 0):
        here = half_slice(half, rows)
        sums = total[half, :, LANES : 2 * LANES]
        chunks = join_heads(total[half, :, 0:LANES] / sums, rows, head_dim)
        for chunk in range(2):
            cols = slice(chunk * LANES, (chunk + 1) * LANES)
            o32_ref[here, cols] = chunks[chunk]
            o_ref[here, cols] = chunks[chunk].astype(BF16)
        lse_ref[half] = jnp.transpose(jnp.log(sums))[0:8, :]
        part = matmul(o_ref[here, :], wo_ref[...]).astype(BF16)
        (mine_ref, other_ref)[half][...] = part


def feed_kernel(x_ref, mine_ref, other_ref, gain_ref, wg_ref, wu_ref, dh_ref,
                mid_out, n2_out, hid_out, dgate_out, dup_out, part_mine, part_other,
                mid_ref, n2_ref, hid_ref, dgate_ref, dup_ref, sems):
    rows = x_ref.shape[0] // 2
    hidden = wg_ref.shape[1]
    for half in range(2):
        here = half_slice(half, rows)
        middle = x_ref[here, :].astype(F32) + (mine_ref, other_ref)[half][...].astype(F32)
        mid_ref[here, :] = middle
        n2_ref[here, :] = rms_norm(middle, gain_ref[...]).astype(BF16)
    early = fetch([(mid_ref, mid_out), (n2_ref, n2_out)], sems)
    step = 2 * LANES
    for at in range(0, hidden, step):
        cols = slice(at, min(at + step, hidden))
        normed = n2_ref[...]
        gate = matmul(normed, wg_ref[:, cols])
        up = matmul(normed, wu_ref[:, cols])
        grad_hidden = dh_ref[:, cols]
        sigmoid = jax.nn.sigmoid(gate)
        silu = gate * sigmoid
        hid_ref[:, cols] = (silu * up).astype(BF16)
        dgate_ref[:, cols] = (
            grad_hidden * up * sigmoid * (1.0 + gate * (1.0 - sigmoid))
        ).astype(BF16)
        dup_ref[:, cols] = (grad_hidden * silu).astype(BF16)
    late = fetch([(hid_ref, hid_out), (dgate_ref, dgate_out), (dup_ref, dup_out)], sems.at[2:5])
    for half, part in ((1, part_other), (0, part_mine)):
        here = half_slice(half, rows)
        for at in range(0, wg_ref.shape[0], step):
            wide = slice(at, at + step)
            part[:, wide] = (
                contract(dgate_ref[here, :], wg_ref[wide, :], 1, 1)
                + contract(dup_ref[here, :], wu_ref[wide, :], 1, 1)
            ).astype(BF16)
    for copy in early + late:
        copy.wait()


def prepare_back(info, head_dim, q_ref, do_ref, o32_ref, spread, spread_do, delta):
    rows = info.half_rows
    q_low, do_low = q_ref[...], do_ref[...]
    for half in range(2):
        here = half_slice(half, rows)
        spread_heads(q_low, rows, half, head_dim, spread)
        spread_heads(do_low, rows, half, head_dim, spread_do)
        product = do_low[here, :].astype(F32) * o32_ref[here, :]
        for chunk in range(2):
            turned = jnp.transpose(product[:, chunk * LANES : (chunk + 1) * LANES])
            for group in range(2):
                at = (2 * chunk + group) * rows
                delta[half, :, at : at + rows] = jnp.broadcast_to(
                    jnp.sum(
                        turned[group * head_dim : (group + 1) * head_dim], axis=0, keepdims=True
                    ),
                    (8, rows),
                )


def back_slots(info, first_slot, held, spread, spread_do, lse_ref, delta, dq_t, dkv, out_ref):
    rows = info.half_rows

    def one_key_block(step, carry):
        slot, key_half = step // 2, lax.rem(step, 2)
        source = info.slot_source(first_slot + slot)
        key_block = info.block(source, key_half)
        key_rows = pl.ds(pl.multiple_of(key_half * rows, rows), rows)
        dkv[...] = jnp.zeros_like(dkv)
        for half in range(2):
            query_block = info.block(info.ctx, half)
            visible, whole = info.relation(query_block, key_block)

            def take(masked, half=half, query_block=query_block):
                keys = held[slot, key_rows, 0:LANES]
                values = held[slot, key_rows, LANES : 2 * LANES]
                if masked:
                    allowed = info.mask(query_block, key_block, 1)
                    allowed = jnp.concatenate([allowed] * (BACK_ROWS // rows), axis=1)
                for part in range(4 * rows // BACK_ROWS):
                    at = slice(part * BACK_ROWS, (part + 1) * BACK_ROWS)
                    queries, grads = spread[half, at, :], spread_do[half, at, :]
                    scores = contract(keys, queries, 1, 1) - lse_ref[half, 0:1, at]
                    if masked:
                        scores = jnp.where(allowed, scores, NEG)
                    probs = jnp.exp(scores)
                    grad_probs = contract(values, grads, 1, 1)
                    grad_scores = (probs * (grad_probs - delta[half, 0:1, at])).astype(BF16)
                    dkv[:, LANES : 2 * LANES] += matmul(probs.astype(BF16), grads)
                    dkv[:, 0:LANES] += matmul(grad_scores, queries)
                    dq_t[half, :, at] += contract(keys, grad_scores, 0, 0)

            pl.when(visible & whole)(functools.partial(take, False))
            pl.when(visible & jnp.logical_not(whole))(functools.partial(take, True))
        out_ref[source // 2, key_rows, :] = dkv[...].astype(BF16)
        return carry

    lax.fori_loop(0, 2 * held.shape[0], one_key_block, 0)


def back_first_kernel(devices, head_dim, wt_count, block_ref, start_ref, q_ref, o32_ref, lse_ref,
                      mid_ref, mine_ref, other_ref, c_ref, gain_ref, wo_ref, *refs):
    pairs = devices // 2
    slots = refs[:pairs]
    dkv_out, dq_t, dy_ref, dyb_ref, do_ref, ffn_gain = refs[pairs : pairs + 6]
    held, spread, spread_do, delta, dkv, sems = refs[pairs + 6 :]
    rows = q_ref.shape[0] // 2
    info = Info(block_ref, start_ref, devices, rows)
    copies = fetch([(slots[at], held.at[at]) for at in range(pairs)], sems)
    gain_sum = jnp.zeros((1, gain_ref.shape[1]), F32)
    for half in range(2):
        here = half_slice(half, rows)
        back, terms = norm_back(
            mid_ref[here, :], gain_ref[...], (mine_ref, other_ref)[half][...].astype(F32)
        )
        gain_sum += jnp.sum(terms, axis=0, keepdims=True)
        grad_middle = c_ref[here, :].astype(F32) + back
        dy_ref[here, :] = grad_middle
        dyb_ref[here, :] = grad_middle.astype(BF16)
        do_ref[here, :] = contract(dyb_ref[here, :], wo_ref[...], 1, 1).astype(BF16)
    ffn_gain[...] = gain_sum * (1.0 / wt_count)
    prepare_back(info, head_dim, q_ref, do_ref, o32_ref, spread, spread_do, delta)
    dq_t[...] = jnp.zeros_like(dq_t)
    for copy in copies:
        copy.wait()
    back_slots(info, pairs, held, spread, spread_do, lse_ref, delta, dq_t, dkv, dkv_out)


def back_second_kernel(devices, head_dim, block_ref, start_ref, q_ref, do_ref, o32_ref, lse_ref,
                       raw_ref, qg_ref, bc_ref, bs_ref, sc_ref, ss_ref, dq_in, *refs):
    pairs = devices // 2
    slots = refs[:pairs]
    dkv_out, dq_ref, gain_ref, held, spread, spread_do, delta, dq_t, dkv, sems = refs[pairs:]
    rows = q_ref.shape[0] // 2
    info = Info(block_ref, start_ref, devices, rows)
    copies = fetch([(slots[at], held.at[at]) for at in range(pairs)] + [(dq_in, dq_t)], sems)
    prepare_back(info, head_dim, q_ref, do_ref, o32_ref, spread, spread_do, delta)
    for copy in copies:
        copy.wait()
    back_slots(info, 0, held, spread, spread_do, lse_ref, delta, dq_t, dkv, dkv_out)
    query_gain = twice(qg_ref)
    gain_sum = jnp.zeros((1, LANES), F32)
    for half in range(2):
        here = half_slice(half, rows)
        cos, sin = rope_rows(info, (bc_ref, bs_ref, sc_ref, ss_ref), half, head_dim)
        chunks = join_heads(jnp.transpose(dq_t[half]), rows, head_dim)
        for chunk in range(2):
            cols = slice(chunk * LANES, (chunk + 1) * LANES)
            grad = chunks[chunk] * SCALE
            grad = grad * cos - swap_halves(grad, head_dim) * sin
            back, term = head_norm_back(raw_ref[here, cols], query_gain, grad, head_dim)
            dq_ref[here, cols] = back.astype(BF16)
            gain_sum += term
    gain_ref[...] = gain_sum


def key_back_kernel(devices, head_dim, count, block_ref, start_ref, raw_ref, kg_ref, bc_ref, bs_ref,
                    sc_ref, ss_ref, dq_ref, x_ref, wq_ref, wk_ref, wv_ref, ffn_gain, query_gain,
                    *refs):
    parts = refs[:count]
    dkv_ref, mine_ref, other_ref, gains_ref = refs[count:]
    rows = raw_ref.shape[0] // 2
    width = x_ref.shape[1]
    info = Info(block_ref, start_ref, devices, rows)
    key_gain = twice(kg_ref)
    key_sum = jnp.zeros((1, LANES), F32)
    attn_sum = jnp.zeros((1, width), F32)
    for half in (1, 0):
        here = half_slice(half, rows)
        grad = sum(part[here, :].astype(F32) for part in parts)
        cos, sin = rope_rows(info, (bc_ref, bs_ref, sc_ref, ss_ref), half, head_dim)
        grad_k = grad[:, 0:LANES]
        grad_k = grad_k * cos - swap_halves(grad_k, head_dim) * sin
        back, term = head_norm_back(raw_ref[here, 2 * LANES : 3 * LANES], key_gain, grad_k, head_dim)
        key_sum += term
        key_low, value_low = back.astype(BF16), grad[:, LANES : 2 * LANES].astype(BF16)
        dkv_ref[here, 0:LANES] = key_low
        dkv_ref[here, LANES : 2 * LANES] = value_low
        part = (
            contract(dq_ref[here, :], wq_ref[...], 1, 1)
            + contract(key_low, wk_ref[...], 1, 1)
            + contract(value_low, wv_ref[...], 1, 1)
        )
        (mine_ref, other_ref)[half][...] = part.astype(BF16)
        inputs = x_ref[here, :].astype(F32)
        inverse = lax.rsqrt(jnp.mean(inputs * inputs, axis=-1, keepdims=True) + EPS)
        attn_sum += jnp.sum(part * inputs * inverse, axis=0, keepdims=True)
    gains_ref[:, 0:width] = attn_sum
    gains_ref[:, width : 2 * width] = ffn_gain[...]
    gains_ref[:, 2 * width : 2 * width + LANES] = query_gain[...]
    gains_ref[:, 2 * width + LANES : 2 * width + 2 * LANES] = key_sum


def finish_kernel(x_ref, mine_ref, other_ref, gain_ref, dy_ref, out_ref):
    rows = x_ref.shape[0] // 2
    core = lax.rem(lax.axis_index("wt"), 2)
    for half in range(2):
        here = half_slice(half, rows)
        back, _ = norm_back(
            x_ref[here, :].astype(F32), gain_ref[...], (mine_ref, other_ref)[half][...].astype(F32)
        )
        to_row = pl.multiple_of(jnp.bitwise_xor(half, core) * rows, rows)
        out_ref[pl.ds(to_row, rows), :] = dy_ref[here, :] + back


def put_shard(kept, sent, bit, device, rows, cols, piece):
    index = device // (2 << bit) * (1 << bit) + device % (1 << bit)
    same = lax.rem(lax.axis_index("ctx") // (1 << bit), 2) == device // (1 << bit) % 2

    @pl.when(same)
    def _():
        kept[index, rows, cols] = piece

    @pl.when(jnp.logical_not(same))
    def _():
        sent[index, rows, cols] = piece


def put_rows(kept, sent, bit, shard, row, cols, block):
    for part in range(block.shape[0] // shard):
        piece = block[part * shard : (part + 1) * shard]
        put_shard(kept, sent, bit, row // shard + part, slice(0, shard), cols, piece)


def feed_grad_kernel(per_step, c_ref, n2_ref, hid_ref, dgate_ref, dup_ref, wd_ref, *refs):
    mine_ref, other_ref, y_kept, y_sent, z_kept, z_sent = refs[-6:]
    rows = c_ref.shape[0] // 2
    hidden = hid_ref.shape[1]
    shard, first = y_kept.shape[1:]
    gate_end = z_kept.shape[2]
    gate_at = 2 * hidden - first
    begin = pl.program_id(0) * per_step
    ctx = lax.axis_index("ctx")

    def put(kept, sent, bit, cols, block):
        for part in range(per_step):
            index = part // (2 << bit) * (1 << bit) + part % (1 << bit)
            side = lax.rem((begin + part) // (1 << bit), 2)
            same = lax.rem(ctx // (1 << bit), 2) == side
            piece = block[part * shard : (part + 1) * shard]

            @pl.when(same)
            def _():
                kept[index, :, cols] = piece

            @pl.when(jnp.logical_not(same))
            def _():
                sent[index, :, cols] = piece

    for half, out in ((1, other_ref), (0, mine_ref)):
        out[...] = matmul(hid_ref[half_slice(half, rows), :], wd_ref[...]).astype(BF16)
    turned = jnp.transpose(n2_ref[...])
    block = matmul(turned, dup_ref[...]).astype(BF16)
    put(y_kept, y_sent, 0, slice(0, first), block[:, :first])
    put(z_kept, z_sent, 1, slice(hidden, gate_at), block[:, first:])
    block = matmul(turned, dgate_ref[:, : gate_end - gate_at]).astype(BF16)
    put(z_kept, z_sent, 1, slice(gate_at, gate_end), block)
    block = matmul(jnp.transpose(c_ref[...]), hid_ref[...]).astype(BF16)
    put(z_kept, z_sent, 1, slice(0, hidden), block)


def feed_grads(out_grad, normed, hidden, grad_gate, grad_up, w_down, y_width, z_width, after):
    tok_rows, width = out_grad.shape
    devices = lax.axis_size("ctx")
    shard = width // devices
    step = 2 * LANES
    per_step = step // shard
    pairs = devices // 2
    whole = pl.BlockSpec(hidden.shape, lambda i: (0, 0))
    columns = pl.BlockSpec((tok_rows, step), lambda i: (0, i))
    out = pl.BlockSpec((tok_rows // 2, step), lambda i: (0, i))
    y_spec = pl.BlockSpec((per_step // 2, shard, y_width), lambda i: (i, 0, 0))
    if per_step == 2:
        z_spec = pl.BlockSpec((2, shard, z_width), lambda i: (i // 2, 0, 0))
    else:
        z_spec = pl.BlockSpec((per_step // 2, shard, z_width), lambda i: (i, 0, 0))
    half_low = jax.ShapeDtypeStruct((tok_rows // 2, width), BF16)
    y_shape = jax.ShapeDtypeStruct((pairs, shard, y_width), BF16)
    z_shape = jax.ShapeDtypeStruct((pairs, shard, z_width), BF16)
    return pl.pallas_call(
        functools.partial(feed_grad_kernel, per_step),
        grid=(width // step,),
        out_shape=[half_low, half_low, y_shape, y_shape, z_shape, z_shape],
        in_specs=[columns, columns, whole, whole, whole]
        + [pl.BlockSpec((w_down.shape[0], step), lambda i: (0, i))]
        + [pl.BlockSpec(memory_space=pl.ANY)] * len(after),
        out_specs=[out, out, y_spec, y_spec, z_spec, z_spec],
        compiler_params=pltpu.CompilerParams(vmem_limit_bytes=VMEM_LIMIT),
        cost_estimate=pl.CostEstimate(flops=14 * 10**9, bytes_accessed=0, transcendentals=0),
    )(out_grad, normed, hidden, grad_gate, grad_up, w_down, *after)


def narrow_grad_kernel(devices, skips, *refs):
    kept, sent = refs[-2:]
    count = len(skips)
    width = refs[0].shape[1]
    shard = width // devices
    begin = 0
    if len(refs) > 2 * count + 2:
        gains = refs[2 * count][...]
        for device in range(devices):
            at = device * shard
            blank = [jnp.zeros((1, LANES - shard), F32)] if shard < LANES else []
            first = [gains[:, at : at + shard]] + blank
            second = [gains[:, width + at : width + at + shard]] + blank
            block = jnp.concatenate(
                [
                    jnp.concatenate(first + second, axis=1),
                    gains[:, 2 * width : 2 * width + 2 * LANES],
                    jnp.zeros((GAIN_ROWS - 2, 2 * LANES), F32),
                ],
                axis=0,
            ).astype(BF16)
            put_shard(
                kept, sent, 0, device, slice(shard, shard + GAIN_ROWS), slice(0, 2 * LANES), block
            )
    step = 2 * LANES
    for at in range(count):
        left, right = refs[2 * at], refs[2 * at + 1]
        cols = slice(begin, begin + right.shape[1] - skips[at])
        begin = cols.stop
        for row in range(0, width, step):
            block = matmul(jnp.transpose(left[:, row : row + step]), right[:, skips[at] :])
            block = block.astype(BF16)
            put_rows(kept, sent, 0, shard, row, cols, block)


def call_kernel(body, outs, operands, memory, scratch=(), flops=1000, after=()):
    kinds = {
        "s": pl.BlockSpec(memory_space=pltpu.SMEM),
        "v": pl.BlockSpec(memory_space=pltpu.VMEM),
        "a": pl.BlockSpec(memory_space=pl.ANY),
    }
    count = len(operands)

    def whole(*refs):
        body(*refs[:count], *refs[count + len(after) :])

    return pl.pallas_call(
        whole,
        out_shape=[jax.ShapeDtypeStruct(shape, kind) for shape, kind, *_ in outs],
        in_specs=[kinds[m] for m in memory] + [kinds["a"]] * len(after),
        out_specs=[kinds[out[2] if len(out) > 2 else "v"] for out in outs],
        scratch_shapes=list(scratch),
        compiler_params=pltpu.CompilerParams(vmem_limit_bytes=VMEM_LIMIT),
        cost_estimate=pl.CostEstimate(flops=flops, bytes_accessed=0, transcendentals=0),
    )(*operands, *after)


def hold(values, after):
    return pl.pallas_call(
        lambda *refs: None,
        out_shape=jax.ShapeDtypeStruct(values.shape, values.dtype),
        in_specs=[pl.BlockSpec(memory_space=pl.ANY)] * (1 + len(after)),
        out_specs=pl.BlockSpec(memory_space=pl.ANY),
        input_output_aliases={0: 0},
        cost_estimate=pl.CostEstimate(flops=0, bytes_accessed=0, transcendentals=0),
    )(values, *after)


def flip(values, axis, bit):
    size = lax.axis_size(axis)
    return lax.ppermute(values, axis, [(i, i ^ bit) for i in range(size)])


def shift(values, step):
    size = lax.axis_size("ctx")
    return lax.ppermute(values, "ctx", [(i, (i + step) % size) for i in range(size)])


def gather_slots(values):
    pairs = lax.axis_size("ctx") // 2
    same = [values] + [shift(values, 2 * k) for k in range(1, pairs)]
    return same, [flip(part, "ctx", 1) for part in same]


def chip_sum(mine, other):
    return (mine.astype(F32) + flip(other, "wt", 1).astype(F32)).astype(BF16)


def slice_sum(chip):
    whole = (chip.astype(F32) + flip(chip, "wt", 2).astype(F32)).astype(BF16)
    return whole, flip(whole, "wt", 1)


def halve(kept, received, bits, bit):
    after = len([b for b in bits if b < bit])
    view = (-1, 2, 1 << after) + kept.shape[1:]
    kept, received = kept.reshape(view), received.reshape(view)
    side = (lax.axis_index("ctx") // (1 << bit)) % 2

    def pick(at):
        picked = lax.dynamic_index_in_dim(kept, at, 1, keepdims=False).astype(
            F32
        ) + lax.dynamic_index_in_dim(received, at, 1, keepdims=False).astype(F32)
        return picked.astype(BF16).reshape((-1,) + view[3:])

    return pick(side), pick(1 - side)


def last_sum(kept, received):
    return kept[0].astype(F32) + received[0].astype(F32)


def ctx_bits():
    return range(lax.axis_size("ctx").bit_length() - 1)


def scatter_tail(kept, received, bits):
    bits = list(bits)
    sends = []
    for bit in list(bits):
        kept, sent = halve(kept, received, bits, bit)
        bits.remove(bit)
        sends.append(sent)
        received = flip(sent, "ctx", 1 << bit)
    return last_sum(kept, received), sends


def scatter_tail_from(kept, received, bits):
    if len(bits) == 1:
        return last_sum(kept, received), []
    return scatter_tail(kept, received, bits[1:])


def scatter_rest(kept, received, first, waits=()):
    bits = [bit for bit in ctx_bits() if bit != first]
    sends = []
    for step, bit in enumerate(list(bits)):
        if step < len(waits):
            kept = hold(kept, waits[step])
        kept, sent = halve(kept, received, bits, bit)
        bits.remove(bit)
        sends.append(sent)
        received = flip(sent, "ctx", 1 << bit)
    return last_sum(kept, received), sends


def on_device(
    block_in,
    doc_ids,
    block_of,
    w_query,
    w_key,
    w_value,
    w_out,
    w_gate,
    w_up,
    w_down,
    attn_gain,
    ffn_gain,
    query_gain,
    key_gain,
    cotangent,
):
    tok_rows, width = block_in.shape
    half_rows = tok_rows // 2
    head_dim = query_gain.shape[0]
    q_width, kv_width = w_query.shape[1], w_key.shape[1]
    hidden_width = w_gate.shape[1]
    devices = lax.axis_size("ctx")
    pairs = devices // 2
    blocks = block_of.shape[0]
    wt_count = lax.axis_size("wt")
    ctx = lax.axis_index("ctx")
    core = lax.axis_index("wt") % 2
    mine, other = slice(0, half_rows), slice(half_rows, tok_rows)

    half_dim = head_dim // 2
    freqs = THETA ** (-2.0 * (np.arange(LANES) % half_dim).astype(np.float64) / head_dim)
    base_angle = (np.arange(blocks) * half_rows)[:, None] * freqs[None, :]
    step_angle = np.arange(half_rows)[:, None] * freqs[None, :]
    tables = [
        jnp.asarray(table.astype(np.float32))
        for table in (np.cos(base_angle), np.sin(base_angle), np.cos(step_angle), np.sin(step_angle))
    ]
    attn_gain_row, ffn_gain_row = attn_gain[None, :], ffn_gain[None, :]
    query_gain_row, key_gain_row = query_gain[None, :], key_gain[None, :]
    stacked = 4 * half_rows
    half_low = ((half_rows, width), BF16)
    held = pltpu.VMEM((pairs, tok_rows, 2 * kv_width), BF16)
    spread = pltpu.VMEM((2, stacked, LANES), BF16)

    key_value, query, raw, normed_one, x_local, starts = call_kernel(
        functools.partial(project_kernel, devices, head_dim),
        [
            ((tok_rows, 2 * kv_width), BF16),
            ((tok_rows, q_width), BF16),
            ((tok_rows, q_width + kv_width), F32),
            ((tok_rows, width), BF16),
            ((tok_rows, width), BF16),
            ((DOCS,), jnp.int32, "s"),
        ],
        [
            block_of,
            block_in,
            doc_ids.reshape(-1, LANES),
            attn_gain_row,
            w_query,
            w_key,
            w_value,
            query_gain_row,
            key_gain_row,
        ]
        + tables,
        "s" + "v" * 12,
    )
    place = [block_of, starts]
    same_slots, other_slots = gather_slots(key_value)

    out_grad = jnp.where(core == 0, cotangent, jnp.roll(cotangent, half_rows, 0))
    grad_hidden = contract(out_grad, w_down, 1, 1)

    total, spread_query = call_kernel(
        functools.partial(attend_first_kernel, devices, head_dim),
        [((2, stacked, 2 * LANES), F32), ((2, stacked, LANES), BF16)],
        place + [query] + same_slots + other_slots[:1],
        "ssv" + "a" * (pairs + 1),
        [
            pltpu.VMEM((pairs + 1, tok_rows, 2 * kv_width), BF16),
            pltpu.SemaphoreType.DMA((pairs + 1,)),
        ],
        after=[grad_hidden],
    )
    out_low, out_wide, log_total, attn_mine, attn_other = call_kernel(
        functools.partial(attend_second_kernel, devices, head_dim),
        [
            ((tok_rows, q_width), BF16),
            ((tok_rows, q_width), F32),
            ((2, 8, stacked), F32),
            half_low,
            half_low,
        ],
        place + [spread_query, total, w_out] + other_slots[1:],
        "ssvav" + "a" * (pairs - 1),
        [
            pltpu.VMEM((pairs - 1, tok_rows, 2 * kv_width), BF16),
            pltpu.VMEM((2, stacked, 2 * LANES), F32),
            pltpu.SemaphoreType.DMA((pairs,)),
        ],
    )
    attn_mine, attn_other = slice_sum(chip_sum(attn_mine, attn_other))

    feed_shapes = [((tok_rows, width), F32), ((tok_rows, width), BF16)]
    feed_shapes += [((tok_rows, hidden_width), BF16)] * 3
    middle, normed_two, hidden, grad_gate, grad_upper, part_mine, part_other = call_kernel(
        feed_kernel,
        [(*shape, "a") for shape in feed_shapes] + [half_low, half_low],
        [x_local, attn_mine, attn_other, ffn_gain_row, w_gate, w_up, grad_hidden],
        "v" * 7,
        [pltpu.VMEM(*shape) for shape in feed_shapes] + [pltpu.SemaphoreType.DMA((5,))],
    )
    chip = chip_sum(part_mine, part_other)
    n2_mine, n2_other = slice_sum(chip)

    shard = width // devices
    y_width = hidden_width * 7 // 9 // LANES * LANES
    gate_cut = hidden_width // 3 // LANES * LANES
    gate_at = 2 * hidden_width - y_width
    z_width = gate_at + gate_cut
    ffn_mine, ffn_other, y_kept, y_sent, z_kept, z_sent = feed_grads(
        out_grad, normed_two, hidden, grad_gate, grad_upper, w_down, y_width, z_width, [chip]
    )
    ffn_chip = hold(chip_sum(ffn_mine, ffn_other), [n2_mine])
    y_received = flip(y_sent, "ctx", 1)
    z_received = flip(z_sent, "ctx", 2)

    grad_other, grad_query_t, grad_middle, grad_middle_low, grad_attended, ffn_gain_part = (
        call_kernel(
            functools.partial(back_first_kernel, devices, head_dim, wt_count),
            [
                ((pairs, tok_rows, 2 * kv_width), BF16),
                ((2, LANES, stacked), F32),
                ((tok_rows, width), F32),
                ((tok_rows, width), BF16),
                ((tok_rows, q_width), BF16),
                ((1, width), F32),
            ],
            place
            + [query, out_wide, log_total, middle, n2_mine, n2_other, out_grad, ffn_gain_row, w_out]
            + other_slots,
            "ss" + "v" * 9 + "a" * pairs,
            [
                held,
                spread,
                spread,
                pltpu.VMEM((2, 8, stacked), F32),
                pltpu.VMEM((half_rows, 2 * LANES), F32),
                pltpu.SemaphoreType.DMA((pairs,)),
            ],
            after=[ffn_chip],
            )
    )
    ffn_mine, ffn_other = slice_sum(ffn_chip)
    grad_same, query_raw_low, query_gain_sum = call_kernel(
        functools.partial(back_second_kernel, devices, head_dim),
        [
            ((pairs, tok_rows, 2 * kv_width), BF16),
            ((tok_rows, q_width), BF16),
            ((1, LANES), F32),
        ],
        place
        + [query, grad_attended, out_wide, log_total, raw, query_gain_row]
        + tables
        + [grad_query_t]
        + same_slots,
        "ss" + "v" * 10 + "a" * (1 + pairs),
        [
            held,
            spread,
            spread,
            pltpu.VMEM((2, 8, stacked), F32),
            pltpu.VMEM((2, LANES, stacked), F32),
            pltpu.VMEM((half_rows, 2 * LANES), F32),
            pltpu.SemaphoreType.DMA((pairs + 1,)),
        ],
        after=[ffn_mine],
    )
    bits = list(ctx_bits())
    key_value_received = flip(grad_other, "ctx", 1)
    y_kept, y_sent = halve(hold(y_kept, [grad_same]), y_received, bits[1:], 1)
    y_received = flip(y_sent, "ctx", 2)
    first_kept, first_sent = call_kernel(
        functools.partial(narrow_grad_kernel, devices, (gate_cut, 0, 0)),
        [((pairs, shard, hidden_width - gate_cut + 2 * q_width), BF16)] * 2,
        [normed_two, grad_gate, normed_one, query_raw_low, grad_middle_low, out_low],
        "v" * 6,
        after=[y_sent],
    )
    z_kept, z_sent = halve(hold(z_kept, [first_sent]), z_received, bits[:1] + bits[2:], 0)
    z_received = flip(z_sent, "ctx", 1)
    key_value_kept = hold(grad_same, [z_sent])
    key_value_sends = []
    rest = bits[1:]
    for bit in bits[1:]:
        key_value_kept, sent = halve(key_value_kept, key_value_received, rest, bit)
        rest.remove(bit)
        key_value_received = flip(sent, "ctx", 1 << bit)
        key_value_sends.append(sent)
    first_received = flip(hold(first_sent, key_value_sends[:1]), "ctx", 1)
    z_kept, z_sent = halve(hold(z_kept, key_value_sends[1:2]), z_received, bits[2:], bits[2])
    z_received = flip(z_sent, "ctx", 1 << bits[2])
    y_total, _ = scatter_tail(hold(y_kept, key_value_sends[:1]), y_received, bits[2:])

    grad_key_value_low, part_mine, part_other, gains = call_kernel(
        functools.partial(key_back_kernel, devices, head_dim, 2),
        [
            ((tok_rows, 2 * kv_width), BF16),
            half_low,
            half_low,
            ((1, 2 * width + 2 * LANES), F32),
        ],
        place
        + [raw, key_gain_row]
        + tables
        + [query_raw_low, x_local, w_query, w_key, w_value, ffn_gain_part, query_gain_sum]
        + [key_value_kept[0], key_value_received[0]],
        "ss" + "v" * 15,
        after=[y_total, z_sent],
    )
    n1_chip = chip_sum(part_mine, part_other)
    n1_received = flip(n1_chip, "wt", 2)

    second_kept, second_sent = call_kernel(
        functools.partial(narrow_grad_kernel, devices, (0,)),
        [((pairs, shard + GAIN_ROWS, 2 * kv_width), BF16)] * 2,
        [normed_one, grad_key_value_low, gains],
        "v" * 3,
        after=[n1_chip],
    )
    first_kept, first_sent = halve(hold(first_kept, [second_sent]), first_received, bits[1:], 1)
    first_received = flip(first_sent, "ctx", 2)
    n1_mine = (hold(n1_chip, [first_sent]).astype(F32) + n1_received.astype(F32)).astype(BF16)
    n1_other = flip(n1_mine, "wt", 1)
    second_kept, second_sent = halve(
        hold(second_kept, [n1_mine]), flip(second_sent, "ctx", 1), bits[1:], 1
    )
    second_received = flip(second_sent, "ctx", 2)
    (grad_input,) = call_kernel(
        finish_kernel,
        [((tok_rows, width), F32)],
        [x_local, n1_mine, n1_other, attn_gain_row, grad_middle],
        "v" * 5,
        after=[second_sent],
    )
    first, first_sends = scatter_tail(hold(first_kept, [grad_input]), first_received, bits[2:])
    second, second_sends = scatter_tail(
        hold(second_kept, first_sends[-1:]), second_received, bits[2:]
    )
    z_total, _ = scatter_tail_from(hold(z_kept, second_sends[-1:]), z_received, bits[2:])
    gain_rows = second[shard : shard + 2]
    gain_rows = sum([flip(gain_rows, "wt", other_wt) for other_wt in range(1, wt_count)], gain_rows)

    def head_gain(at):
        row = jnp.sum(gain_rows[1, at * LANES : (at + 1) * LANES].reshape(-1, head_dim), axis=0)
        return lax.dynamic_slice_in_dim(row, ctx * (head_dim // devices), head_dim // devices)

    gate_rest = hidden_width - gate_cut
    ffn_mine = hold(ffn_mine, [n1_mine])
    out_mine = (middle[mine] + ffn_mine.astype(F32)).astype(BF16)
    out_other = (middle[other] + ffn_other.astype(F32)).astype(BF16)
    return (
        jnp.concatenate(
            [jnp.where(core == 0, out_mine, out_other), jnp.where(core == 0, out_other, out_mine)],
            axis=0,
        ),
        grad_input,
        first[:, gate_rest : gate_rest + q_width],
        second[:shard, :kv_width],
        second[:shard, kv_width:],
        first[:, gate_rest + q_width :].T,
        jnp.concatenate([z_total[:, gate_at:], first[:, :gate_rest]], axis=1),
        jnp.concatenate([y_total, z_total[:, hidden_width:gate_at]], axis=1),
        z_total[:, :hidden_width].T,
        gain_rows[0, :shard],
        gain_rows[0, LANES : LANES + shard],
        head_gain(0),
        head_gain(1),
    )


def solution(mesh):
    in_specs = (
        P("ctx", None),
        P(),
        P(),
        P(None, "wt"),
        P(None, "wt"),
        P(None, "wt"),
        P("wt", None),
        P(None, "wt"),
        P(None, "wt"),
        P("wt", None),
        P(),
        P(),
        P(),
        P(),
        P("ctx", None),
    )
    out_specs = (
        P("ctx", None),
        P("ctx", None),
        P("ctx", "wt"),
        P("ctx", "wt"),
        P("ctx", "wt"),
        P("wt", "ctx"),
        P("ctx", "wt"),
        P("ctx", "wt"),
        P("wt", "ctx"),
        P("ctx"),
        P("ctx"),
        P("ctx"),
        P("ctx"),
    )
    return jax.shard_map(
        on_device, mesh=mesh, in_specs=in_specs, out_specs=out_specs, check_vma=False
    )
```
